512 devices in a mesh: sub: 64 (over z, x), crs: 8 (over y, core).
Axes of the slice: x: 4, y: 4, z: 16, core: 2. Of those that a mesh axis runs over, the one named last changes fastest.
Arguments:
- right_side: float32 [4, 64, 8, 384], P(None, 'sub', 'crs'), may hold values from -40 to 40
- own_block: bfloat16 [64, 8, 384, 384], P('sub', 'crs'), may hold values from -1 to 3
- coupling: bfloat16 [64, 8, 384, 768], P('sub', 'crs'), may hold values from -0.1875 to 0.1875
- local_inverse: bfloat16 [64, 8, 384, 1152], P('sub', 'crs'), may hold values from -1 to 3
- coarse_basis: float32 [64, 8, 40, 384], P('sub', 'crs'), may hold values from -0.3125 to 0.3125
- coarse_inverse: bfloat16 [64, 320, 8, 2560], P('sub', None, 'crs'), may hold values from -1 to 4
- neighbours: int32 [64, 8, 6], P('sub', 'crs'), may hold values from 0 to 63, as said below
- margin_rows: int32 [64, 8, 6, 128], P('sub', 'crs'), may hold values from 0 to 383, as said below
- block_counts: int32 [64, 8], P('sub', 'crs'), may hold values from 4 to 6, as said below
Outputs:
- solution: float32 [4, 64, 8, 384], P(None, 'sub', 'crs')
- basis_next: float32 [4, 64, 8, 384], P(None, 'sub', 'crs')
The draws below stay inside these ranges and needn't reach their ends.
Inputs may be any that keep to these rules, and one draw needn't show every extreme that they name: A subdomain's listed neighbours are distinct sub indices other than its own; slot j of (s, c) names subdomain (neighbours[s, c, j], c). `margin_rows`: the rows of one block are distinct. `block_counts`: some subdomain uses all 6 slots.
All inputs are finite; a program needn't handle non-finite values.
Results may differ from the reference program's by a relative error of at most 0.0095.
Values may be sent and summed in bfloat16 or wider, within the bound.
No kernel may reach another device: no remote copies, remote signals or barrier semaphores. Data moves between devices by JAX's collectives and lax.ppermute only.
A program may use at most 64 MiB of HBM per device.

```python
import math
import jax
import jax.numpy as jnp
from jax import lax

OWN_ROWS = 384
BLK = 128
NBMAX = 6
KC = 40
COLS = 4
ITERS = 2
SUBS = 64
OWNERS = 8
ROWS_ALL = 196608


def draw_right_side(key, part):
    key = jax.random.fold_in(key, 101)
    key_base, key_scale = jax.random.split(key)
    full_shape = (COLS, SUBS, OWNERS, OWN_ROWS)
    position = (lax.broadcasted_iota(jnp.float32, full_shape, 1) * OWNERS + lax.broadcasted_iota(jnp.float32, full_shape, 2)) / (SUBS * OWNERS - 1)
    row_scale = jnp.exp(jax.random.uniform(key_scale, (1, SUBS, OWNERS, OWN_ROWS), jnp.float32, math.log(0.5), math.log(5.0)))
    trend_scale = 1.0 + 0.8 * position
    values = jnp.clip(jax.random.normal(key_base, full_shape, jnp.float32), -4.0, 4.0)
    return values * row_scale * trend_scale


def draw_own_block(key, part):
    key = jax.random.fold_in(key, 102)
    key_one, key_two = jax.random.split(key)
    full_shape = (SUBS, OWNERS, OWN_ROWS, OWN_ROWS)
    noise_part = jnp.clip(jax.random.normal(key_one, full_shape, jnp.float32), -4.0, 4.0) * (OWN_ROWS + NBMAX * BLK) ** (-0.5)
    diagonal = jax.random.uniform(key_two, (SUBS, OWNERS, OWN_ROWS, 1), jnp.float32, 1.0, 2.0)
    on_diagonal = lax.broadcasted_iota(jnp.int32, full_shape, 2) == lax.broadcasted_iota(jnp.int32, full_shape, 3)
    return (noise_part + jnp.where(on_diagonal, diagonal, 0.0)).astype(jnp.bfloat16)


def draw_local_inverse(key, part):
    key = jax.random.fold_in(key, 103)
    key_one, key_two = jax.random.split(key)
    full_shape = (SUBS, OWNERS, OWN_ROWS, OWN_ROWS + NBMAX * BLK)
    noise_part = jnp.clip(jax.random.normal(key_one, full_shape, jnp.float32), -4.0, 4.0) * (OWN_ROWS + NBMAX * BLK) ** (-0.5)
    diagonal = jax.random.uniform(key_two, (SUBS, OWNERS, OWN_ROWS, 1), jnp.float32, 0.8, 1.6)
    on_diagonal = lax.broadcasted_iota(jnp.int32, full_shape, 2) == lax.broadcasted_iota(jnp.int32, full_shape, 3)
    return (noise_part + jnp.where(on_diagonal, diagonal, 0.0)).astype(jnp.bfloat16)


def draw_coarse_inverse(key, part):
    key = jax.random.fold_in(key, 104)
    full_shape = (SUBS, OWNERS * KC, OWNERS, SUBS * KC)
    noise_part = jnp.clip(jax.random.normal(key, full_shape, jnp.float32), -4.0, 4.0) * (SUBS * OWNERS * KC) ** (-0.5)
    sub_rows = lax.broadcasted_iota(jnp.int32, (SUBS, 1, 1, 1), 0)
    sub_cols = lax.broadcasted_iota(jnp.int32, (1, 1, 1, SUBS * KC), 3)
    owner_rows = lax.broadcasted_iota(jnp.int32, (1, OWNERS * KC, 1, 1), 1)
    owner_cols = lax.broadcasted_iota(jnp.int32, (1, 1, OWNERS, 1), 2)
    matches = (sub_rows == sub_cols // KC) & (owner_rows // KC == owner_cols) & (owner_rows % KC == sub_cols % KC)
    return (noise_part + jnp.where(matches, 3.0, 0.0)).astype(jnp.bfloat16)


def draw_neighbours(key, part):
    key = jax.random.fold_in(key, 105)
    full_shape = (SUBS, OWNERS, SUBS - 1)
    scores = jax.random.randint(key, full_shape, 0, 1 << 20) * (SUBS - 1) + lax.broadcasted_iota(jnp.int32, full_shape, 2)
    ranking = jnp.argsort(scores, axis=2)[:, :, :NBMAX].astype(jnp.int32)
    own_index = lax.broadcasted_iota(jnp.int32, (SUBS, OWNERS, NBMAX), 0)
    return ((own_index + 1 + ranking) % SUBS).astype(jnp.int32)


def draw_margin_rows(key, part):
    key = jax.random.fold_in(key, 106)
    full_shape = (SUBS, OWNERS, NBMAX, OWN_ROWS)
    scores = jax.random.randint(key, full_shape, 0, 1 << 20) * OWN_ROWS + lax.broadcasted_iota(jnp.int32, full_shape, 3)
    return jnp.argsort(scores, axis=3)[:, :, :, :BLK].astype(jnp.int32)


def draw_block_counts(key, part):
    key = jax.random.fold_in(key, 107)
    key_one, key_two = jax.random.split(key)
    counts = NBMAX - 2 + jax.random.randint(key_one, (SUBS, OWNERS), 0, 3)
    forced_index = jax.random.randint(key_two, (), 0, SUBS * OWNERS)
    flat_index = lax.broadcasted_iota(jnp.int32, (SUBS, OWNERS), 0) * OWNERS + lax.broadcasted_iota(jnp.int32, (SUBS, OWNERS), 1)
    return jnp.where(flat_index == forced_index, NBMAX, counts).astype(jnp.int32)


def level_of(key, extent, cuts, least, top_value):
    gain = 1.0
    for axis_at, shards_of in cuts:
        draws = jax.random.uniform(jax.random.fold_in(jax.random.fold_in(key, 6), axis_at), (shards_of,), jnp.float32, least / len(cuts), top_value / len(cuts))
        gain = gain * jnp.repeat(jnp.exp(draws), extent[axis_at] // shards_of).reshape((-1,) + (1,) * (len(extent) - 1 - axis_at))
    return gain


def gaussian(rng, dims, scale, limit, cuts=(), held_as=jnp.bfloat16):
    level = level_of(rng, dims, cuts, -0.22, 0.18) if cuts else 1.0
    drawn = jax.random.normal(rng, dims, jnp.float32) * scale * level
    return jnp.minimum(jnp.maximum(drawn, -limit), limit).astype(held_as)


def setup_inputs(seed: int = 0) -> dict:
    key_of = jax.random.split(jax.random.key(seed), 10)
    return {
        "right_side": draw_right_side(jax.random.fold_in(key_of[9], 71), 0),
        "own_block": draw_own_block(jax.random.fold_in(key_of[9], 71), 0),
        "coupling": gaussian(key_of[2], (SUBS, OWNERS, OWN_ROWS, NBMAX * BLK), (OWN_ROWS + NBMAX * BLK) ** -0.5, 0.1875, ((0, 64), (1, 8))),
        "local_inverse": draw_local_inverse(jax.random.fold_in(key_of[9], 71), 0),
        "coarse_basis": gaussian(key_of[4], (SUBS, OWNERS, KC, OWN_ROWS), OWN_ROWS ** -0.5, 0.3125, ((0, 64), (1, 8)), jnp.float32),
        "coarse_inverse": draw_coarse_inverse(jax.random.fold_in(key_of[9], 71), 0),
        "neighbours": draw_neighbours(jax.random.fold_in(key_of[9], 71), 0),
        "margin_rows": draw_margin_rows(jax.random.fold_in(key_of[9], 71), 0),
        "block_counts": draw_block_counts(jax.random.fold_in(key_of[9], 71), 0),
    }


epsilon = 1e-06

def margin_of(vector_low, neighbours, margin_rows, block_counts):
    subs_here, owners_here, slot_count, block_rows = margin_rows.shape
    owner_index = lax.broadcasted_iota(jnp.int32, margin_rows.shape, 1)
    sub_index = jnp.broadcast_to(neighbours[:, :, :, None], margin_rows.shape).astype(jnp.int32)
    fetched = vector_low[sub_index, owner_index, :, margin_rows.astype(jnp.int32)]
    fetched = jnp.moveaxis(fetched, 4, 2)
    live_slots = jnp.arange(slot_count)[None, None, :] < block_counts[:, :, None]
    fetched = jnp.where(live_slots[:, :, None, :, None], fetched, jnp.zeros_like(fetched))
    return fetched.reshape(subs_here, owners_here, fetched.shape[2], slot_count * block_rows)

def apply_local(matrices, vectors):

    def per_group(members):
        matrix_one, vector_one = members
        return jnp.einsum('crk,cqk->cqr', matrix_one.astype(jnp.float32), vector_one.astype(jnp.float32))
    return lax.map(per_group, (matrices, vectors))

def spread(values):
    return values[None, None, :, None]

def least_squares(start_norm, columns):
    cosines = []
    sine_terms = []
    triangle = []
    target = [start_norm] + [jnp.zeros_like(start_norm) for j in range(len(columns))]
    for j, column in enumerate(columns):
        column = list(column)
        for i in range(j):
            upper_value = cosines[i] * column[i] + sine_terms[i] * column[i + 1]
            column[i + 1] = -sine_terms[i] * column[i] + cosines[i] * column[i + 1]
            column[i] = upper_value
        radius = jnp.sqrt(column[j] * column[j] + column[j + 1] * column[j + 1])
        cosine = column[j] / radius
        sine_part = column[j + 1] / radius
        column[j] = radius
        target[j + 1] = -sine_part * target[j]
        target[j] = cosine * target[j]
        cosines.append(cosine)
        sine_terms.append(sine_part)
        triangle.append(column[:j + 1])
    weights = [None] * len(columns)
    for j in reversed(range(len(columns))):
        running = target[j]
        for k in range(j + 1, len(columns)):
            running = running - triangle[k][j] * weights[k]
        weights[j] = running / triangle[j][j]
    return weights

def reference(right_side, own_block, coupling, local_inverse, coarse_basis, coarse_inverse, neighbours, margin_rows, block_counts):
    right_cols = jnp.transpose(right_side, (1, 2, 0, 3))
    coarse_view = coarse_inverse.reshape(SUBS, OWNERS, KC, OWNERS, SUBS, KC)

    def operate(vector):
        vector_low = vector.astype(jnp.bfloat16)
        margin = margin_of(vector_low, neighbours, margin_rows, block_counts)
        return apply_local(own_block, vector_low) + apply_local(coupling, margin)

    def precondition(vector):
        vector_low = vector.astype(jnp.bfloat16)
        margin = margin_of(vector_low, neighbours, margin_rows, block_counts)
        fine_part = apply_local(local_inverse, jnp.concatenate([vector_low, margin], axis=3))
        restricted = jnp.einsum('sckr,scqr->scqk', coarse_basis, vector, precision=lax.Precision.HIGHEST).astype(jnp.bfloat16)
        restricted_wide = restricted.astype(jnp.float32)

        def solve_rows(matrix):
            return jnp.einsum('akbjl,jbql->aqk', matrix.astype(jnp.float32), restricted_wide)
        solved = lax.map(solve_rows, coarse_view)
        coarse_part = jnp.einsum('scqk,sckr->scqr', solved, coarse_basis, precision=lax.Precision.HIGHEST)
        return fine_part + coarse_part

    def mean_product(first, second):
        return lax.optimization_barrier(jnp.sum(first * second, axis=(0, 1, 3))) / ROWS_ALL
    start_norm = jnp.sqrt(mean_product(right_cols, right_cols) + epsilon)
    krylov = [right_cols / spread(start_norm)]
    directions = []
    columns = []
    for j in range(ITERS):
        direction = precondition(krylov[j])
        mapped = operate(direction)
        heights = [mean_product(mapped, krylov[i]) for i in range(j + 1)]
        for i in range(j + 1):
            mapped = mapped - spread(heights[i]) * krylov[i]
        length = jnp.sqrt(mean_product(mapped, mapped) + epsilon)
        columns.append(heights + [length])
        krylov.append(mapped / spread(length))
        directions.append(direction)
    weights = least_squares(start_norm, columns)
    solution = spread(weights[0]) * directions[0]
    for j in range(1, ITERS):
        solution = solution + spread(weights[j]) * directions[j]
    return (jnp.transpose(solution, (2, 0, 1, 3)), jnp.transpose(krylov[-1], (2, 0, 1, 3)))
```

```python
import jax
import jax.numpy as jnp
from jax import lax
from jax.sharding import PartitionSpec as P

EPS = 1e-06
HIGH = lax.Precision.HIGHEST
LAST = (((1,), (1,)), ((), ()))


def least_squares(start_norm, columns):
    cosines = []
    sine_terms = []
    triangle = []
    target = [start_norm] + [jnp.zeros_like(start_norm) for j in range(len(columns))]
    for j, column in enumerate(columns):
        column = list(column)
        for i in range(j):
            upper_value = cosines[i] * column[i] + sine_terms[i] * column[i + 1]
            column[i + 1] = -sine_terms[i] * column[i] + cosines[i] * column[i + 1]
            column[i] = upper_value
        radius = jnp.sqrt(column[j] * column[j] + column[j + 1] * column[j + 1])
        cosine = column[j] / radius
        sine_part = column[j + 1] / radius
        column[j] = radius
        target[j + 1] = -sine_part * target[j]
        target[j] = cosine * target[j]
        cosines.append(cosine)
        sine_terms.append(sine_part)
        triangle.append(column[: j + 1])
    weights = [None] * len(columns)
    for j in reversed(range(len(columns))):
        running = target[j]
        for k in range(j + 1, len(columns)):
            running = running - triangle[k][j] * weights[k]
        weights[j] = running / triangle[j][j]
    return weights


def split3(x):
    hi = x.astype(jnp.bfloat16)
    rest = x - hi.astype(jnp.float32)
    mid = rest.astype(jnp.bfloat16)
    low = (rest - mid.astype(jnp.float32)).astype(jnp.bfloat16)
    return [hi, mid, low]


def body(
    right_side,
    own_block,
    coupling,
    local_inverse,
    coarse_basis,
    coarse_inverse,
    neighbours,
    margin_rows,
    block_counts,
):
    cols, own_rows = right_side.shape[0], right_side.shape[3]
    r = right_side.reshape(cols, own_rows)
    own_matrix = own_block[0, 0]
    couple_matrix = coupling[0, 0]
    inverse = local_inverse[0, 0]
    basis = coarse_basis[0, 0]
    kc = basis.shape[0]
    coarse_rows = coarse_inverse[0, :, 0, :]
    listed = neighbours[0, 0]
    picked = margin_rows[0, 0]
    live = block_counts[0, 0]
    slots, blk = picked.shape
    subs, owners = lax.axis_size("sub"), lax.axis_size("crs")
    all_rows = own_rows * subs * owners
    chosen = (listed[:, None] == jnp.arange(subs)[None, :]) & (
        jnp.arange(slots)[:, None] < live
    )
    chosen = chosen.astype(jnp.bfloat16)
    picks = (picked[:, :, None] == jnp.arange(own_rows)[None, None, :]).astype(jnp.bfloat16)

    def spread(block):
        copies = jnp.broadcast_to(block[None], (subs,) + block.shape)
        return lax.all_to_all(copies, "sub", 0, 0)

    def margin_of(gathered):
        near = jnp.einsum(
            "js,sqr->jqr", chosen, gathered, preferred_element_type=jnp.float32
        ).astype(jnp.bfloat16)
        rows = jnp.einsum(
            "jqr,jbr->qjb", near, picks, preferred_element_type=jnp.float32
        ).astype(jnp.bfloat16)
        return rows.reshape(cols, slots * blk)

    def restrict(v):
        return lax.dot_general(
            v, basis, LAST, precision=HIGH, preferred_element_type=jnp.float32
        ).astype(jnp.bfloat16)

    def precondition(v_low, gathered):
        margin = margin_of(gathered[:, :, :own_rows])
        fine = lax.dot_general(
            jnp.concatenate([v_low, margin], axis=1),
            inverse,
            LAST,
            preferred_element_type=jnp.float32,
        )
        coarse = gathered[:, :, own_rows : own_rows + kc]
        coarse = jnp.transpose(coarse, (1, 0, 2)).reshape(cols, subs * kc)
        share = lax.dot_general(coarse, coarse_rows, LAST, preferred_element_type=jnp.float32)
        return fine, share.reshape(cols, owners, kc).transpose(1, 0, 2)

    def operate(z_low, gathered):
        return lax.dot_general(
            z_low, own_matrix, LAST, preferred_element_type=jnp.float32
        ) + lax.dot_general(
            margin_of(gathered), couple_matrix, LAST, preferred_element_type=jnp.float32
        )

    def prolong(solved):
        return jnp.dot(solved, basis, precision=HIGH, preferred_element_type=jnp.float32)

    r_low = r.astype(jnp.bfloat16)
    fine, share = precondition(r_low, spread(jnp.concatenate([r_low, restrict(r)], axis=1)))
    solved = jnp.sum(lax.all_to_all(share, "crs", 0, 0), axis=0)
    p1 = fine + prolong(solved)
    p1_low = p1.astype(jnp.bfloat16)
    q1 = operate(p1_low, spread(p1_low))

    inner = jnp.stack(
        [jnp.sum(r * r, axis=1), jnp.sum(q1 * r, axis=1), jnp.sum(q1 * q1, axis=1)], axis=1
    )
    q1_low = q1.astype(jnp.bfloat16)
    gathered = spread(jnp.concatenate([q1_low, restrict(q1)] + split3(inner), axis=1))
    fine, share = precondition(q1_low, gathered)
    terms = gathered[:, :, own_rows + kc :].astype(jnp.float32)
    terms = jnp.sum(terms, axis=0).reshape(cols, 3, 3).sum(axis=1)
    share = jnp.concatenate([share, jnp.broadcast_to(terms[None], (owners, cols, 3))], axis=2)
    summed = jnp.sum(lax.all_to_all(share, "crs", 0, 0), axis=0)
    p2 = fine + prolong(summed[:, :kc])
    rr, qr, qq = [summed[:, kc + i] / all_rows for i in range(3)]

    start = jnp.sqrt(rr + EPS)
    h11 = qr / start / start
    w = q1 / start[:, None]
    v1 = r / start[:, None]
    part = h11 / start
    left = qq / start / start - 2.0 * part * (qr / start) + part * part * rr
    h21 = jnp.sqrt(jnp.maximum(left, 0.0) + EPS)
    v2 = (w - h11[:, None] * v1) / h21[:, None]
    z1 = p1 / start[:, None]
    z2 = (p2 / start[:, None] - h11[:, None] * z1) / h21[:, None]
    z2_low = z2.astype(jnp.bfloat16)
    w = operate(z2_low, spread(z2_low))
    pairs = [(w, v1), (w, v2), (w, w), (v1, v1), (v1, v2), (v2, v2)]
    inner = jnp.stack([jnp.sum(a * b, axis=1) for a, b in pairs])
    inner = lax.all_to_all(
        jnp.broadcast_to(inner[None], (owners,) + inner.shape), "crs", 0, 0
    ).sum(axis=0)
    inner = lax.all_to_all(
        jnp.broadcast_to(inner[None], (subs,) + inner.shape), "sub", 0, 0
    ).sum(axis=0)
    h12, h22, ww, g11, g12, g22 = inner / all_rows
    left = (
        ww
        - 2.0 * (h12 * h12 + h22 * h22)
        + h12 * h12 * g11
        + 2.0 * h12 * h22 * g12
        + h22 * h22 * g22
    )
    h32 = jnp.sqrt(jnp.maximum(left, 0.0) + EPS)
    v3 = (w - h12[:, None] * v1 - h22[:, None] * v2) / h32[:, None]
    weights = least_squares(start, [[h11, h21], [h12, h22, h32]])
    answer = weights[0][:, None] * z1 + weights[1][:, None] * z2
    shape = (cols, 1, 1, own_rows)
    return answer.reshape(shape), v3.reshape(shape)


def solution(mesh):
    in_specs = (
        P(None, "sub", "crs", None),
        P("sub", "crs", None, None),
        P("sub", "crs", None, None),
        P("sub", "crs", None, None),
        P("sub", "crs", None, None),
        P("sub", None, "crs", None),
        P("sub", "crs", None),
        P("sub", "crs", None, None),
        P("sub", "crs"),
    )
    out_specs = (P(None, "sub", "crs", None), P(None, "sub", "crs", None))
    return jax.shard_map(body, mesh=mesh, in_specs=in_specs, out_specs=out_specs, check_vma=False)
```

```python
import jax
import jax.numpy as jnp
from jax import lax
from jax.experimental import pallas as pl
from jax.experimental.pallas import tpu as pltpu
from jax.sharding import PartitionSpec as P

EPS = 1e-06
HIGH = lax.Precision.HIGHEST
LAST = (((1,), (1,)), ((), ()))
FIRST = (((1,), (0,)), ((), ()))
LANES = 128
VMEM_BYTES = 16 << 20


def least_squares(start_norm, columns):
    cosines = []
    sine_terms = []
    triangle = []
    target = [start_norm] + [jnp.zeros_like(start_norm) for j in range(len(columns))]
    for j, column in enumerate(columns):
        column = list(column)
        for i in range(j):
            upper_value = cosines[i] * column[i] + sine_terms[i] * column[i + 1]
            column[i + 1] = -sine_terms[i] * column[i] + cosines[i] * column[i + 1]
            column[i] = upper_value
        radius = jnp.sqrt(column[j] * column[j] + column[j + 1] * column[j + 1])
        cosine = column[j] / radius
        sine_part = column[j + 1] / radius
        column[j] = radius
        target[j + 1] = -sine_part * target[j]
        target[j] = cosine * target[j]
        cosines.append(cosine)
        sine_terms.append(sine_part)
        triangle.append(column[: j + 1])
    weights = [None] * len(columns)
    for j in reversed(range(len(columns))):
        running = target[j]
        for k in range(j + 1, len(columns)):
            running = running - triangle[k][j] * weights[k]
        weights[j] = running / triangle[j][j]
    return weights


def split3(x):
    hi = x.astype(jnp.bfloat16).astype(jnp.float32)
    rest = x - hi
    mid = rest.astype(jnp.bfloat16).astype(jnp.float32)
    return hi, mid, rest - mid


def place(column, lane, at):
    return jnp.where(lane == at, column, 0.0)


def pick_lanes(tiles, index):
    low = index & (LANES - 1)
    high = index >> 7
    out = jnp.take_along_axis(tiles[0], low, axis=1, mode="promise_in_bounds")
    for t in range(1, len(tiles)):
        other = jnp.take_along_axis(tiles[t], low, axis=1, mode="promise_in_bounds")
        out = jnp.where(high == t, other, out)
    return out


def lanes_of(shape):
    return lax.broadcasted_iota(jnp.int32, shape, 1)


def twice(x):
    return jnp.concatenate([x, x], axis=0)


def send_rows(vector, asked_ref, out_ref):
    tiles = [twice(vector[:, t * LANES : (t + 1) * LANES]) for t in range(vector.shape[1] // LANES)]
    cols = vector.shape[0]
    for i in range(asked_ref.shape[0]):
        chosen = pick_lanes(tiles, asked_ref[i])
        out_ref[2 * i, :, 0:LANES] = chosen[:cols].astype(jnp.bfloat16)
        out_ref[2 * i + 1, :, 0:LANES] = chosen[cols:].astype(jnp.bfloat16)


def margin_from(got_ref, near_ref, live_ref, slots):
    parts = []
    for j in range(slots):
        part = got_ref[near_ref[j], :, 0:LANES]
        parts.append(jnp.where(j < live_ref[0], part, jnp.zeros_like(part)))
    return jnp.concatenate(parts, axis=1)


def first_send_kernel(near_ref, live_ref, r_ref, basis_ref, picked_ref, out_ref):
    subs, cols, _ = out_ref.shape
    rows = r_ref.shape[1]
    kc = basis_ref.shape[0]
    r = r_ref[...]
    low = r.astype(jnp.bfloat16)
    residual = lax.dot_general(
        r, basis_ref[...], LAST, precision=HIGH, preferred_element_type=jnp.float32
    )
    tail = jnp.concatenate([residual, jnp.zeros((cols, LANES - kc), jnp.float32)], axis=1)
    whole = jnp.concatenate([low, tail.astype(jnp.bfloat16)], axis=1)
    out_ref[...] = jnp.broadcast_to(whole[None], out_ref.shape)
    lane = lanes_of((cols, LANES))
    sub = lax.broadcasted_iota(jnp.int32, (cols, LANES), 0)
    wide = LANES // cols
    slots = picked_ref.shape[0]
    for j in range(slots):
        wanted = (picked_ref[pl.ds(j, 1), :] - rows // 2).astype(jnp.float32)
        wanted = jnp.broadcast_to(wanted, (cols, LANES))
        packed = jnp.zeros((cols, LANES), jnp.float32)
        for i in range(cols):
            moved = pltpu.roll(wanted, (kc - i * wide) % LANES, 1)
            packed = jnp.where(sub == i, moved, packed)
        packed = jnp.where((lane >= kc) & (lane < kc + wide), packed, tail)

        @pl.when(j < live_ref[0])
        def _():
            out_ref[near_ref[j], :, rows : rows + LANES] = packed.astype(jnp.bfloat16)


def share_kernel(at, with_terms, got_ref, coarse_ref, out_ref):
    subs, cols, _ = got_ref.shape
    owners = out_ref.shape[0]
    kc = coarse_ref.shape[0] // owners
    lane = lanes_of((cols, LANES))
    tiles = [jnp.zeros((cols, LANES), jnp.float32) for _ in range(subs * kc // LANES)]
    terms = jnp.zeros((cols, LANES), jnp.float32)
    for s in range(subs):
        got = got_ref[s, :, at : at + LANES].astype(jnp.float32)
        if with_terms:
            terms = terms + got
        t, off = divmod(s * kc, LANES)
        moved = pltpu.roll(got, off, 1) if off else got
        if off + kc <= LANES:
            tiles[t] = jnp.where((lane >= off) & (lane < off + kc), moved, tiles[t])
        else:
            tiles[t] = jnp.where(lane >= off, moved, tiles[t])
            tiles[t + 1] = jnp.where(lane < off + kc - LANES, moved, tiles[t + 1])
    residuals = jnp.concatenate(tiles, axis=1).astype(jnp.bfloat16)
    share = lax.dot_general(
        residuals, coarse_ref[...], LAST, preferred_element_type=jnp.float32
    )
    extra = jnp.zeros((cols, LANES), jnp.float32)
    if with_terms:
        summed = terms + pltpu.roll(terms, LANES - 3, 1) + pltpu.roll(terms, LANES - 6, 1)
        extra = jnp.where((lane >= kc) & (lane < kc + 3), summed, 0.0)
    wide = jnp.concatenate(
        [share, jnp.zeros((cols, -share.shape[1] % LANES), jnp.float32)], axis=1
    )
    for c in range(owners):
        t, off = divmod(c * kc, LANES)
        part = wide[:, t * LANES : (t + 1) * LANES]
        if off:
            part = pltpu.roll(part, LANES - off, 1)
        if off + kc > LANES:
            after = pltpu.roll(wide[:, (t + 1) * LANES : (t + 2) * LANES], LANES - off, 1)
            part = jnp.where(lane < LANES - off, part, after)
        out_ref[c] = jnp.where(lane < kc, part, extra)


def first_fine_kernel(
    kc, near_ref, live_ref, r_ref, picked_ref, got_ref, inverse_ref, fine_ref, asked_ref
):
    subs, cols, _ = got_ref.shape
    rows = r_ref.shape[1]
    slots = picked_ref.shape[0]
    parts = [r_ref[...].astype(jnp.bfloat16)]
    for j in range(slots):
        near = got_ref[near_ref[j], :, 0:rows].astype(jnp.float32)
        tiles = [twice(near[:, t * LANES : (t + 1) * LANES]) for t in range(rows // LANES)]
        index = jnp.broadcast_to(picked_ref[pl.ds(j, 1), :], (2 * cols, LANES))
        part = pick_lanes(tiles, index)[:cols]
        parts.append(jnp.where(j < live_ref[0], part, 0.0).astype(jnp.bfloat16))
    extended = jnp.concatenate(parts, axis=1)
    fine_ref[...] = lax.dot_general(
        extended, inverse_ref[...], LAST, preferred_element_type=jnp.float32
    )
    lane = lanes_of((cols, LANES))
    wide = LANES // cols
    for i in range(subs // 2):
        pair = []
        for s in (2 * i, 2 * i + 1):
            got = got_ref[s, :, rows : rows + LANES].astype(jnp.float32)
            index = jnp.zeros((cols, LANES), jnp.float32)
            for k in range(cols):
                moved = pltpu.roll(
                    jnp.broadcast_to(got[k : k + 1], (cols, LANES)), (k * wide - kc) % LANES, 1
                )
                index = jnp.where((lane >= k * wide) & (lane < (k + 1) * wide), moved, index)
            pair.append(index)
        index = jnp.concatenate(pair, axis=0).astype(jnp.int32) + rows // 2
        asked_ref[i] = jnp.clip(index, 0, rows - 1)


def fine_kernel(near_ref, live_ref, vector_ref, got_ref, inverse_ref, fine_ref):
    rows = vector_ref.shape[1]
    slots = (inverse_ref.shape[1] - rows) // LANES
    margin = margin_from(got_ref, near_ref, live_ref, slots)
    extended = jnp.concatenate([vector_ref[...].astype(jnp.bfloat16), margin], axis=1)
    fine_ref[...] = lax.dot_general(
        extended, inverse_ref[...], LAST, preferred_element_type=jnp.float32
    )


def prolong(summed, fine_ref, basis_ref):
    kc = basis_ref.shape[0]
    return fine_ref[...] + lax.dot_general(
        summed[:, :kc], basis_ref[...], FIRST, precision=HIGH, preferred_element_type=jnp.float32
    )


def first_direction_kernel(shares_ref, fine_ref, basis_ref, asked_ref, p_ref, out_ref):
    p = prolong(jnp.sum(shares_ref[...], axis=0), fine_ref, basis_ref)
    p_ref[...] = p
    send_rows(p, asked_ref, out_ref)


def own_kernel(vector_ref, own_ref, out_ref):
    out_ref[...] = lax.dot_general(
        vector_ref[...].astype(jnp.bfloat16), own_ref[...], LAST, preferred_element_type=jnp.float32
    )


def operate(near_ref, live_ref, own_part_ref, got_ref, coupling_ref):
    margin = margin_from(got_ref, near_ref, live_ref, coupling_ref.shape[1] // LANES)
    return own_part_ref[...] + lax.dot_general(
        margin, coupling_ref[...], LAST, preferred_element_type=jnp.float32
    )


def row_sum(x):
    return jnp.sum(x, axis=1, keepdims=True)


def first_operate_kernel(
    near_ref, live_ref, own_part_ref, got_ref, coupling_ref, r_ref, basis_ref, asked_ref, q_ref, out_ref
):
    cols = r_ref.shape[0]
    kc = basis_ref.shape[0]
    q = operate(near_ref, live_ref, own_part_ref, got_ref, coupling_ref)
    q_ref[...] = q
    r = r_ref[...]
    residual = lax.dot_general(
        q, basis_ref[...], LAST, precision=HIGH, preferred_element_type=jnp.float32
    )
    tail = jnp.concatenate([residual, jnp.zeros((cols, LANES - kc), jnp.float32)], axis=1)
    lane = lanes_of((cols, LANES))
    for i, inner in enumerate([row_sum(r * r), row_sum(q * r), row_sum(q * q)]):
        for k, term in enumerate(split3(inner)):
            tail = jnp.where(lane == kc + 3 * k + i, term, tail)
    send_rows(q, asked_ref, out_ref)
    out_ref[:, :, LANES : 2 * LANES] = jnp.broadcast_to(
        tail.astype(jnp.bfloat16)[None], (out_ref.shape[0], cols, LANES)
    )


def second_direction_kernel(
    all_rows, shares_ref, fine_ref, basis_ref, asked_ref, r_ref, q_ref, p_ref,
    v1_ref, v2_ref, z1_ref, z2_ref, scalars_ref, out_ref,
):
    kc = basis_ref.shape[0]
    summed = jnp.sum(shares_ref[...], axis=0)
    p2 = prolong(summed, fine_ref, basis_ref)
    rr, qr, qq = [summed[:, kc + i : kc + i + 1] / all_rows for i in range(3)]
    start = jnp.sqrt(rr + EPS)
    h11 = qr / start / start
    part = h11 / start
    left = qq / start / start - 2.0 * part * (qr / start) + part * part * rr
    h21 = jnp.sqrt(jnp.maximum(left, 0.0) + EPS)
    v1 = r_ref[...] / start
    z1 = p_ref[...] / start
    v2 = (q_ref[...] / start - h11 * v1) / h21
    z2 = (p2 / start - h11 * z1) / h21
    v1_ref[...] = v1
    v2_ref[...] = v2
    z1_ref[...] = z1
    z2_ref[...] = z2
    lane = lanes_of(scalars_ref.shape)
    scalars_ref[...] = place(start, lane, 0) + place(h11, lane, 1) + place(h21, lane, 2)
    send_rows(z2, asked_ref, out_ref)


def second_operate_kernel(
    near_ref, live_ref, own_part_ref, got_ref, coupling_ref, v1_ref, v2_ref, w_ref, out_ref
):
    w = operate(near_ref, live_ref, own_part_ref, got_ref, coupling_ref)
    w_ref[...] = w
    v1 = v1_ref[...]
    v2 = v2_ref[...]
    lane = lanes_of((w.shape[0], LANES))
    pairs = [(w, v1), (w, v2), (w, w), (v1, v1), (v1, v2), (v2, v2)]
    inner = jnp.zeros((w.shape[0], LANES), jnp.float32)
    for i, (a, b) in enumerate(pairs):
        inner = inner + place(row_sum(a * b), lane, i)
    out_ref[...] = jnp.broadcast_to(inner[None], out_ref.shape)


def between_kernel(got_ref, out_ref):
    out_ref[...] = jnp.broadcast_to(jnp.sum(got_ref[...], axis=0)[None], out_ref.shape)


def last_kernel(
    all_rows, got_ref, w_ref, v1_ref, v2_ref, z1_ref, z2_ref, scalars_ref, answer_ref, next_ref
):
    inner = jnp.sum(got_ref[...], axis=0) / all_rows
    h12, h22, ww, g11, g12, g22 = [inner[:, i : i + 1] for i in range(6)]
    start, h11, h21 = [scalars_ref[:, i : i + 1] for i in range(3)]
    left = (
        ww
        - 2.0 * (h12 * h12 + h22 * h22)
        + h12 * h12 * g11
        + 2.0 * h12 * h22 * g12
        + h22 * h22 * g22
    )
    h32 = jnp.sqrt(jnp.maximum(left, 0.0) + EPS)
    next_ref[...] = (w_ref[...] - h12 * v1_ref[...] - h22 * v2_ref[...]) / h32
    weights = least_squares(start, [[h11, h21], [h12, h22, h32]])
    answer_ref[...] = weights[0] * z1_ref[...] + weights[1] * z2_ref[...]


def call(kernel, outs, *args, scalars=0, name):
    smem = pl.BlockSpec(memory_space=pltpu.SMEM)
    vmem = pl.BlockSpec(memory_space=pltpu.VMEM)
    return pl.pallas_call(
        kernel,
        out_shape=outs,
        in_specs=[smem] * scalars + [vmem] * (len(args) - scalars),
        out_specs=jax.tree.map(lambda _: vmem, outs),
        compiler_params=pltpu.CompilerParams(vmem_limit_bytes=VMEM_BYTES),
        name=name,
    )(*args)


def body(
    right_side,
    own_block,
    coupling,
    local_inverse,
    coarse_basis,
    coarse_inverse,
    neighbours,
    margin_rows,
    block_counts,
):
    cols, rows = right_side.shape[0], right_side.shape[3]
    r = right_side.reshape(cols, rows)
    own = own_block[0, 0]
    couple = coupling[0, 0]
    inverse = local_inverse[0, 0]
    basis = coarse_basis[0, 0]
    coarse = coarse_inverse[0, :, 0, :]
    near = neighbours[0, 0]
    picked = margin_rows[0, 0]
    live = block_counts[0]
    subs, owners = lax.axis_size("sub"), lax.axis_size("crs")
    all_rows = rows * subs * owners
    f32, bf16 = jnp.float32, jnp.bfloat16

    def shape(*dims, dtype=f32):
        return jax.ShapeDtypeStruct(dims, dtype)

    vector = shape(cols, rows)
    tile = shape(cols, LANES)

    def over_sub(blocks):
        return lax.all_to_all(blocks, "sub", 0, 0)

    def over_crs(blocks):
        return lax.all_to_all(blocks, "crs", 0, 0)

    def share_of(at, with_terms, got, name):
        def kernel(*refs):
            share_kernel(at, with_terms, *refs)

        return call(kernel, shape(owners, cols, LANES), got, coarse, name=name)

    sent = call(
        first_send_kernel, shape(subs, cols, rows + LANES, dtype=bf16),
        near, live, r, basis, picked, scalars=2, name="first_send",
    )
    got = over_sub(sent)
    shares = over_crs(share_of(rows, False, got, "first_share"))

    def first_fine(*refs):
        first_fine_kernel(basis.shape[0], *refs)

    fine, asked = call(
        first_fine, (vector, shape(subs // 2, 2 * cols, LANES, dtype=jnp.int32)),
        near, live, r, picked, got, inverse, scalars=2, name="first_fine",
    )
    p1, sent = call(
        first_direction_kernel, (vector, shape(subs, cols, LANES, dtype=bf16)),
        shares, fine, basis, asked, name="first_direction",
    )
    got = over_sub(sent)
    own_part = call(own_kernel, vector, p1, own, name="first_own")
    q1, sent = call(
        first_operate_kernel, (vector, shape(subs, cols, 2 * LANES, dtype=bf16)),
        near, live, own_part, got, couple, r, basis, asked, scalars=2, name="first_operate",
    )
    got = over_sub(sent)
    shares = over_crs(share_of(LANES, True, got, "second_share"))
    fine = call(
        fine_kernel, vector, near, live, q1, got, inverse, scalars=2, name="second_fine"
    )

    def second_direction(*refs):
        second_direction_kernel(float(all_rows), *refs)

    v1, v2, z1, z2, scalars, sent = call(
        second_direction,
        (vector, vector, vector, vector, tile, shape(subs, cols, LANES, dtype=bf16)),
        shares, fine, basis, asked, r, q1, p1, name="second_direction",
    )
    got = over_sub(sent)
    own_part = call(own_kernel, vector, z2, own, name="second_own")
    w, sent = call(
        second_operate_kernel, (vector, shape(owners, cols, LANES)),
        near, live, own_part, got, couple, v1, v2, scalars=2, name="second_operate",
    )
    got = over_crs(sent)
    sent = call(between_kernel, shape(subs, cols, LANES), got, name="between")
    got = over_sub(sent)

    def last(*refs):
        last_kernel(float(all_rows), *refs)

    answer, following = call(
        last, (vector, vector), got, w, v1, v2, z1, z2, scalars, name="last"
    )
    out = (cols, 1, 1, rows)
    return answer.reshape(out), following.reshape(out)


def solution(mesh):
    in_specs = (
        P(None, "sub", "crs", None),
        P("sub", "crs", None, None),
        P("sub", "crs", None, None),
        P("sub", "crs", None, None),
        P("sub", "crs", None, None),
        P("sub", None, "crs", None),
        P("sub", "crs", None),
        P("sub", "crs", None, None),
        P("sub", "crs"),
    )
    out_specs = (P(None, "sub", "crs", None), P(None, "sub", "crs", None))
    return jax.shard_map(body, mesh=mesh, in_specs=in_specs, out_specs=out_specs, check_vma=False)
```

```python
import jax
import jax.numpy as jnp
from jax import lax
from jax.experimental import pallas as pl
from jax.experimental.pallas import tpu as pltpu
from jax.sharding import PartitionSpec as P

EPS = 1e-06
HIGH = lax.Precision.HIGHEST
LAST = (((1,), (1,)), ((), ()))
FIRST = (((1,), (0,)), ((), ()))
LANES = 128
VMEM_BYTES = 16 << 20


def least_squares(start_norm, columns):
    cosines = []
    sine_terms = []
    triangle = []
    target = [start_norm] + [jnp.zeros_like(start_norm) for j in range(len(columns))]
    for j, column in enumerate(columns):
        column = list(column)
        for i in range(j):
            upper_value = cosines[i] * column[i] + sine_terms[i] * column[i + 1]
            column[i + 1] = -sine_terms[i] * column[i] + cosines[i] * column[i + 1]
            column[i] = upper_value
        radius = jnp.sqrt(column[j] * column[j] + column[j + 1] * column[j + 1])
        cosine = column[j] / radius
        sine_part = column[j + 1] / radius
        column[j] = radius
        target[j + 1] = -sine_part * target[j]
        target[j] = cosine * target[j]
        cosines.append(cosine)
        sine_terms.append(sine_part)
        triangle.append(column[: j + 1])
    weights = [None] * len(columns)
    for j in reversed(range(len(columns))):
        running = target[j]
        for k in range(j + 1, len(columns)):
            running = running - triangle[k][j] * weights[k]
        weights[j] = running / triangle[j][j]
    return weights


def split3(x):
    hi = x.astype(jnp.bfloat16).astype(jnp.float32)
    rest = x - hi
    mid = rest.astype(jnp.bfloat16).astype(jnp.float32)
    return hi, mid, rest - mid


def place(column, lane, at):
    return jnp.where(lane == at, column, 0.0)


def pick_lanes(tiles, index):
    low = index & (LANES - 1)
    high = index >> 7
    out = jnp.take_along_axis(tiles[0], low, axis=1, mode="promise_in_bounds")
    for t in range(1, len(tiles)):
        other = jnp.take_along_axis(tiles[t], low, axis=1, mode="promise_in_bounds")
        out = jnp.where(high == t, other, out)
    return out


def lanes_of(shape):
    return lax.broadcasted_iota(jnp.int32, shape, 1)


def twice(x):
    return jnp.concatenate([x, x], axis=0)


def send_rows(vector, asked_ref, out_ref):
    tiles = [twice(vector[:, t * LANES : (t + 1) * LANES]) for t in range(vector.shape[1] // LANES)]
    cols = vector.shape[0]
    for i in range(asked_ref.shape[0]):
        chosen = pick_lanes(tiles, asked_ref[i])
        out_ref[2 * i, :, 0:LANES] = chosen[:cols].astype(jnp.bfloat16)
        out_ref[2 * i + 1, :, 0:LANES] = chosen[cols:].astype(jnp.bfloat16)


def margin_from(got_ref, near_ref, live_ref, slots):
    parts = []
    for j in range(slots):
        part = got_ref[near_ref[j], :, 0:LANES]
        parts.append(jnp.where(j < live_ref[0], part, jnp.zeros_like(part)))
    return jnp.concatenate(parts, axis=1)


def first_send_kernel(
    near, live, r_hbm, basis_hbm, picked_hbm, coarse_hbm, inverse_hbm, own_hbm, couple_hbm,
    out_ref, r_ref, basis_ref, picked, coarse_ref, inverse_ref, own_ref, couple_ref, sems,
):
    pairs = [
        (r_hbm, r_ref),
        (basis_hbm, basis_ref),
        (picked_hbm, picked),
        (coarse_hbm, coarse_ref),
        (inverse_hbm, inverse_ref),
        (own_hbm, own_ref),
        (couple_hbm, couple_ref),
    ]
    moves = [
        pltpu.make_async_copy(source, target, sems.at[i])
        for i, (source, target) in enumerate(pairs)
    ]
    for move in moves:
        move.start()
    for move in moves[:3]:
        move.wait()
    subs, cols, _ = out_ref.shape
    rows = r_ref.shape[2]
    kc = basis_ref.shape[0]
    r = r_ref[:, 0, :]
    low = r.astype(jnp.bfloat16)
    residual = lax.dot_general(
        r, basis_ref[...], LAST, precision=HIGH, preferred_element_type=jnp.float32
    )
    tail = jnp.concatenate([residual, jnp.zeros((cols, LANES - kc), jnp.float32)], axis=1)
    whole = jnp.concatenate([low, tail.astype(jnp.bfloat16)], axis=1)
    out_ref[...] = jnp.broadcast_to(whole[None], out_ref.shape)
    lane = lanes_of((cols, LANES))
    sub = lax.broadcasted_iota(jnp.int32, (cols, LANES), 0)
    wide = LANES // cols
    slots = picked.shape[0]
    for j in range(slots):
        wanted = (picked[j] - rows // 2).astype(jnp.float32)
        wanted = jnp.broadcast_to(wanted, (cols, LANES))
        packed = jnp.zeros((cols, LANES), jnp.float32)
        for i in range(cols):
            moved = pltpu.roll(wanted, (kc - i * wide) % LANES, 1)
            packed = jnp.where(sub == i, moved, packed)
        packed = jnp.where((lane >= kc) & (lane < kc + wide), packed, tail)

        @pl.when(j < live[0])
        def _():
            out_ref[near[j], :, rows : rows + LANES] = packed.astype(jnp.bfloat16)

    for move in moves[3:]:
        move.wait()


def write_share(at, with_terms, got_ref, coarse_ref, out_ref):
    subs, cols, _ = got_ref.shape
    owners = out_ref.shape[0]
    kc = coarse_ref.shape[0] // owners
    lane = lanes_of((cols, LANES))
    tiles = [jnp.zeros((cols, LANES), jnp.float32) for _ in range(subs * kc // LANES)]
    terms = jnp.zeros((cols, LANES), jnp.float32)
    for s in range(subs):
        got = got_ref[s, :, at : at + LANES].astype(jnp.float32)
        if with_terms:
            terms = terms + got
        t, off = divmod(s * kc, LANES)
        moved = pltpu.roll(got, off, 1) if off else got
        if off + kc <= LANES:
            tiles[t] = jnp.where((lane >= off) & (lane < off + kc), moved, tiles[t])
        else:
            tiles[t] = jnp.where(lane >= off, moved, tiles[t])
            tiles[t + 1] = jnp.where(lane < off + kc - LANES, moved, tiles[t + 1])
    residuals = jnp.concatenate(tiles, axis=1).astype(jnp.bfloat16)
    share = lax.dot_general(
        residuals, coarse_ref[...], LAST, preferred_element_type=jnp.float32
    )
    extra = jnp.zeros((cols, LANES), jnp.float32)
    if with_terms:
        summed = terms + pltpu.roll(terms, LANES - 3, 1) + pltpu.roll(terms, LANES - 6, 1)
        extra = jnp.where((lane >= kc) & (lane < kc + 3), summed, 0.0)
    wide = jnp.concatenate(
        [share, jnp.zeros((cols, -share.shape[1] % LANES), jnp.float32)], axis=1
    )
    for c in range(owners):
        t, off = divmod(c * kc, LANES)
        part = wide[:, t * LANES : (t + 1) * LANES]
        if off:
            part = pltpu.roll(part, LANES - off, 1)
        if off + kc > LANES:
            after = pltpu.roll(wide[:, (t + 1) * LANES : (t + 2) * LANES], LANES - off, 1)
            part = jnp.where(lane < LANES - off, part, after)
        out_ref[c] = jnp.where(lane < kc, part, extra)


def first_gather_kernel(
    near_ref, live_ref, r_ref, picked_ref, got_ref, inverse_ref, coarse_ref, fine_ref, asked_ref, out_ref
):
    subs, cols, _ = got_ref.shape
    rows = r_ref.shape[2]
    slots = picked_ref.shape[0]
    write_share(rows, False, got_ref, coarse_ref, out_ref)
    parts = [r_ref[:, 0, :].astype(jnp.bfloat16)]
    for j in range(slots):
        near = got_ref[near_ref[j], :, 0:rows].astype(jnp.float32)
        tiles = [twice(near[:, t * LANES : (t + 1) * LANES]) for t in range(rows // LANES)]
        index = jnp.broadcast_to(picked_ref[j], (2 * cols, LANES))
        part = pick_lanes(tiles, index)[:cols]
        parts.append(jnp.where(j < live_ref[0], part, 0.0).astype(jnp.bfloat16))
    extended = jnp.concatenate(parts, axis=1)
    fine_ref[...] = lax.dot_general(
        extended, inverse_ref[...], LAST, preferred_element_type=jnp.float32
    )
    lane = lanes_of((cols, LANES))
    kc = coarse_ref.shape[0] // out_ref.shape[0]
    wide = LANES // cols
    for i in range(subs // 2):
        pair = []
        for s in (2 * i, 2 * i + 1):
            got = got_ref[s, :, rows : rows + LANES].astype(jnp.float32)
            index = jnp.zeros((cols, LANES), jnp.float32)
            for k in range(cols):
                moved = pltpu.roll(
                    jnp.broadcast_to(got[k : k + 1], (cols, LANES)), (k * wide - kc) % LANES, 1
                )
                index = jnp.where((lane >= k * wide) & (lane < (k + 1) * wide), moved, index)
            pair.append(index)
        index = jnp.concatenate(pair, axis=0).astype(jnp.int32) + rows // 2
        asked_ref[i] = jnp.clip(index, 0, rows - 1)


def second_gather_kernel(
    near_ref, live_ref, vector_ref, got_ref, inverse_ref, coarse_ref, fine_ref, out_ref
):
    rows = vector_ref.shape[1]
    slots = (inverse_ref.shape[1] - rows) // LANES
    write_share(LANES, True, got_ref, coarse_ref, out_ref)
    margin = margin_from(got_ref, near_ref, live_ref, slots)
    extended = jnp.concatenate([vector_ref[...].astype(jnp.bfloat16), margin], axis=1)
    fine_ref[...] = lax.dot_general(
        extended, inverse_ref[...], LAST, preferred_element_type=jnp.float32
    )


def prolong(summed, fine_ref, basis_ref):
    kc = basis_ref.shape[0]
    return fine_ref[...] + lax.dot_general(
        summed[:, :kc], basis_ref[...], FIRST, precision=HIGH, preferred_element_type=jnp.float32
    )


def first_direction_kernel(shares_ref, fine_ref, basis_ref, asked_ref, p_ref, out_ref):
    p = prolong(jnp.sum(shares_ref[...], axis=0), fine_ref, basis_ref)
    p_ref[...] = p
    send_rows(p, asked_ref, out_ref)


def operate(near_ref, live_ref, vector_ref, got_ref, own_ref, coupling_ref):
    margin = margin_from(got_ref, near_ref, live_ref, coupling_ref.shape[1] // LANES)
    low = vector_ref[...].astype(jnp.bfloat16)
    return lax.dot_general(
        low, own_ref[...], LAST, preferred_element_type=jnp.float32
    ) + lax.dot_general(margin, coupling_ref[...], LAST, preferred_element_type=jnp.float32)


def row_sum(x):
    return jnp.sum(x, axis=1, keepdims=True)


def first_operate_kernel(
    near_ref, live_ref, p_ref, got_ref, own_ref, coupling_ref, r_ref, basis_ref, asked_ref, q_ref, out_ref
):
    cols = r_ref.shape[0]
    kc = basis_ref.shape[0]
    q = operate(near_ref, live_ref, p_ref, got_ref, own_ref, coupling_ref)
    q_ref[...] = q
    r = r_ref[:, 0, :]
    residual = lax.dot_general(
        q, basis_ref[...], LAST, precision=HIGH, preferred_element_type=jnp.float32
    )
    tail = jnp.concatenate([residual, jnp.zeros((cols, LANES - kc), jnp.float32)], axis=1)
    lane = lanes_of((cols, LANES))
    for i, inner in enumerate([row_sum(r * r), row_sum(q * r), row_sum(q * q)]):
        for k, term in enumerate(split3(inner)):
            tail = jnp.where(lane == kc + 3 * k + i, term, tail)
    send_rows(q, asked_ref, out_ref)
    out_ref[:, :, LANES : 2 * LANES] = jnp.broadcast_to(
        tail.astype(jnp.bfloat16)[None], (out_ref.shape[0], cols, LANES)
    )


def second_direction_kernel(
    all_rows, shares_ref, fine_ref, basis_ref, asked_ref, r_ref, q_ref, p_ref,
    v1_ref, v2_ref, z1_ref, z2_ref, scalars_ref, out_ref,
):
    kc = basis_ref.shape[0]
    summed = jnp.sum(shares_ref[...], axis=0)
    p2 = prolong(summed, fine_ref, basis_ref)
    rr, qr, qq = [summed[:, kc + i : kc + i + 1] / all_rows for i in range(3)]
    start = jnp.sqrt(rr + EPS)
    h11 = qr / start / start
    part = h11 / start
    left = qq / start / start - 2.0 * part * (qr / start) + part * part * rr
    h21 = jnp.sqrt(jnp.maximum(left, 0.0) + EPS)
    v1 = r_ref[:, 0, :] / start
    z1 = p_ref[...] / start
    v2 = (q_ref[...] / start - h11 * v1) / h21
    z2 = (p2 / start - h11 * z1) / h21
    v1_ref[...] = v1
    v2_ref[...] = v2
    z1_ref[...] = z1
    z2_ref[...] = z2
    lane = lanes_of(scalars_ref.shape)
    scalars_ref[...] = place(start, lane, 0) + place(h11, lane, 1) + place(h21, lane, 2)
    send_rows(z2, asked_ref, out_ref)


def second_operate_kernel(
    near_ref, live_ref, z_ref, got_ref, own_ref, coupling_ref, v1_ref, v2_ref, w_ref, out_ref
):
    w = operate(near_ref, live_ref, z_ref, got_ref, own_ref, coupling_ref)
    w_ref[...] = w
    v1 = v1_ref[...]
    v2 = v2_ref[...]
    cols = w.shape[0]
    lane = lanes_of((cols, LANES))
    col = lax.broadcasted_iota(jnp.int32, (cols, LANES), 0)
    pairs = [(w, v1), (w, v2), (w, w), (v1, v1), (v1, v2), (v2, v2)]
    inner = jnp.zeros((cols, LANES), jnp.float32)
    for i, (a, b) in enumerate(pairs):
        inner = jnp.where(lane == i * cols + col, row_sum(a * b), inner)
    out_ref[...] = jnp.broadcast_to(jnp.sum(inner, axis=0, keepdims=True)[None], out_ref.shape)


def between_kernel(got_ref, out_ref):
    out_ref[...] = jnp.broadcast_to(jnp.sum(got_ref[...], axis=0)[None], out_ref.shape)


def last_kernel(
    all_rows, got_ref, w_ref, v1_ref, v2_ref, z1_ref, z2_ref, scalars_ref, answer_ref, next_ref
):
    cols = w_ref.shape[0]
    lane = lanes_of((cols, LANES))
    col = lax.broadcasted_iota(jnp.int32, (cols, LANES), 0)
    inner = jnp.broadcast_to(jnp.sum(got_ref[...], axis=0) / all_rows, (cols, LANES))
    h12, h22, ww, g11, g12, g22 = [
        row_sum(jnp.where(lane == i * cols + col, inner, 0.0)) for i in range(6)
    ]
    start, h11, h21 = [scalars_ref[:, i : i + 1] for i in range(3)]
    left = (
        ww
        - 2.0 * (h12 * h12 + h22 * h22)
        + h12 * h12 * g11
        + 2.0 * h12 * h22 * g12
        + h22 * h22 * g22
    )
    h32 = jnp.sqrt(jnp.maximum(left, 0.0) + EPS)
    next_ref[:, 0, :] = (w_ref[...] - h12 * v1_ref[...] - h22 * v2_ref[...]) / h32
    weights = least_squares(start, [[h11, h21], [h12, h22, h32]])
    answer_ref[:, 0, :] = weights[0] * z1_ref[...] + weights[1] * z2_ref[...]


def call(kernel, outs, *args, scalars=0, name):
    smem = pl.BlockSpec(memory_space=pltpu.SMEM)
    vmem = pl.BlockSpec(memory_space=pltpu.VMEM)
    return pl.pallas_call(
        kernel,
        out_shape=outs,
        in_specs=[smem] * scalars + [vmem] * (len(args) - scalars),
        out_specs=jax.tree.map(lambda _: vmem, outs),
        compiler_params=pltpu.CompilerParams(vmem_limit_bytes=VMEM_BYTES),
        name=name,
    )(*args)


def body(
    right_side,
    own_block,
    coupling,
    local_inverse,
    coarse_basis,
    coarse_inverse,
    neighbours,
    margin_rows,
    block_counts,
):
    cols, rows = right_side.shape[0], right_side.shape[3]
    r = right_side.reshape(cols, 1, rows)
    own = own_block[0, 0]
    couple = coupling[0, 0]
    inverse = local_inverse[0, 0]
    basis = coarse_basis[0, 0]
    coarse = coarse_inverse[0, :, 0, :]
    near = neighbours[0, 0]
    picked = margin_rows.reshape(margin_rows.shape[2], 1, margin_rows.shape[3])
    live = block_counts[0]
    subs, owners = lax.axis_size("sub"), lax.axis_size("crs")
    all_rows = rows * subs * owners
    f32, bf16 = jnp.float32, jnp.bfloat16

    def shape(*dims, dtype=f32):
        return jax.ShapeDtypeStruct(dims, dtype)

    vector = shape(cols, rows)
    tile = shape(cols, LANES)

    def over_sub(blocks):
        return lax.all_to_all(blocks, "sub", 0, 0)

    def over_crs(blocks):
        return lax.all_to_all(blocks, "crs", 0, 0)

    near_live = (near, live)
    held = [r, basis, picked, coarse, inverse, own, couple]
    vmem = pl.BlockSpec(memory_space=pltpu.VMEM)
    sent, r, basis, picked, coarse, inverse, own, couple = pl.pallas_call(
        first_send_kernel,
        out_shape=[shape(subs, cols, rows + LANES, dtype=bf16)]
        + [shape(*x.shape, dtype=x.dtype) for x in held],
        in_specs=[pl.BlockSpec(memory_space=pltpu.SMEM)] * 2
        + [pl.BlockSpec(memory_space=pltpu.HBM)] * 7,
        out_specs=[vmem] * 8,
        scratch_shapes=[
            pltpu.SemaphoreType.DMA((7,)),
        ],
        compiler_params=pltpu.CompilerParams(vmem_limit_bytes=VMEM_BYTES),
        name="first_send",
    )(near, live, *[pltpu.with_memory_space_constraint(x, pltpu.HBM) for x in held])
    got = over_sub(sent)
    fine, asked, shares = call(
        first_gather_kernel,
        (vector, shape(subs // 2, 2 * cols, LANES, dtype=jnp.int32), shape(owners, cols, LANES)),
        *near_live, r, picked, got, inverse, coarse, scalars=2, name="first_gather",
    )
    shares = over_crs(shares)
    p1, sent = call(
        first_direction_kernel, (vector, shape(subs, cols, LANES, dtype=bf16)),
        shares, fine, basis, asked, name="first_direction",
    )
    got = over_sub(sent)
    q1, sent = call(
        first_operate_kernel, (vector, shape(subs, cols, 2 * LANES, dtype=bf16)),
        *near_live, p1, got, own, couple, r, basis, asked, scalars=2, name="first_operate",
    )
    got = over_sub(sent)
    fine, shares = call(
        second_gather_kernel, (vector, shape(owners, cols, LANES)),
        *near_live, q1, got, inverse, coarse, scalars=2, name="second_gather",
    )
    shares = over_crs(shares)

    def second_direction(*refs):
        second_direction_kernel(float(all_rows), *refs)

    v1, v2, z1, z2, scalars, sent = call(
        second_direction,
        (vector, vector, vector, vector, tile, shape(subs, cols, LANES, dtype=bf16)),
        shares, fine, basis, asked, r, q1, p1, name="second_direction",
    )
    got = over_sub(sent)
    w, sent = call(
        second_operate_kernel, (vector, shape(owners, 1, LANES)),
        *near_live, z2, got, own, couple, v1, v2, scalars=2, name="second_operate",
    )
    got = over_crs(sent)
    sent = call(between_kernel, shape(subs, 1, LANES), got, name="between")
    got = over_sub(sent)

    def last(*refs):
        last_kernel(float(all_rows), *refs)

    answer, following = call(
        last, (shape(cols, 1, rows), shape(cols, 1, rows)),
        got, w, v1, v2, z1, z2, scalars, name="last",
    )
    out = (cols, 1, 1, rows)
    return answer.reshape(out), following.reshape(out)


def solution(mesh):
    in_specs = (
        P(None, "sub", "crs", None),
        P("sub", "crs", None, None),
        P("sub", "crs", None, None),
        P("sub", "crs", None, None),
        P("sub", "crs", None, None),
        P("sub", None, "crs", None),
        P("sub", "crs", None),
        P("sub", "crs", None, None),
        P("sub", "crs"),
    )
    out_specs = (P(None, "sub", "crs", None), P(None, "sub", "crs", None))
    return jax.shard_map(body, mesh=mesh, in_specs=in_specs, out_specs=out_specs, check_vma=False)
```

```python
import jax
import jax.numpy as jnp
from jax import lax
from jax.experimental import pallas as pl
from jax.experimental.pallas import tpu as pltpu
from jax.sharding import PartitionSpec as P

EPS = 1e-06
HIGH = lax.Precision.HIGHEST
LAST = (((1,), (1,)), ((), ()))
FIRST = (((1,), (0,)), ((), ()))
LANES = 128
VMEM_BYTES = 16 << 20


def least_squares(start_norm, columns):
    cosines = []
    sine_terms = []
    triangle = []
    target = [start_norm] + [jnp.zeros_like(start_norm) for j in range(len(columns))]
    for j, column in enumerate(columns):
        column = list(column)
        for i in range(j):
            upper_value = cosines[i] * column[i] + sine_terms[i] * column[i + 1]
            column[i + 1] = -sine_terms[i] * column[i] + cosines[i] * column[i + 1]
            column[i] = upper_value
        radius = jnp.sqrt(column[j] * column[j] + column[j + 1] * column[j + 1])
        cosine = column[j] / radius
        sine_part = column[j + 1] / radius
        column[j] = radius
        target[j + 1] = -sine_part * target[j]
        target[j] = cosine * target[j]
        cosines.append(cosine)
        sine_terms.append(sine_part)
        triangle.append(column[: j + 1])
    weights = [None] * len(columns)
    for j in reversed(range(len(columns))):
        running = target[j]
        for k in range(j + 1, len(columns)):
            running = running - triangle[k][j] * weights[k]
        weights[j] = running / triangle[j][j]
    return weights


def split3(x):
    hi = x.astype(jnp.bfloat16).astype(jnp.float32)
    rest = x - hi
    mid = rest.astype(jnp.bfloat16).astype(jnp.float32)
    return hi, mid, rest - mid


def place(column, lane, at):
    return jnp.where(lane == at, column, 0.0)


def pick_lanes(tiles, index):
    low = index & (LANES - 1)
    high = index >> 7
    out = jnp.take_along_axis(tiles[0], low, axis=1, mode="promise_in_bounds")
    for t in range(1, len(tiles)):
        other = jnp.take_along_axis(tiles[t], low, axis=1, mode="promise_in_bounds")
        out = jnp.where(high == t, other, out)
    return out


def lanes_of(shape):
    return lax.broadcasted_iota(jnp.int32, shape, 1)


def twice(x):
    return jnp.concatenate([x, x], axis=0)


def send_rows(vector, asked_ref, out_ref):
    tiles = [twice(vector[:, t * LANES : (t + 1) * LANES]) for t in range(vector.shape[1] // LANES)]
    cols = vector.shape[0]
    for i in range(asked_ref.shape[0]):
        chosen = pick_lanes(tiles, asked_ref[i])
        out_ref[2 * i, :, 0:LANES] = chosen[:cols].astype(jnp.bfloat16)
        out_ref[2 * i + 1, :, 0:LANES] = chosen[cols:].astype(jnp.bfloat16)


def margin_from(got_ref, near_ref, slots):
    near = near_ref[...]
    parts = []
    for j in range(slots):
        source = near[0, j]
        part = got_ref[jnp.maximum(source, 0), :, 0:LANES]
        parts.append(jnp.where(source >= 0, part, jnp.zeros_like(part)))
    return jnp.concatenate(parts, axis=1)


def first_send_kernel(
    live, near_hbm, r_hbm, basis_hbm, picked_hbm, coarse_hbm, inverse_hbm,
    out_ref, table_ref, r_ref, basis_ref, picked, coarse_ref, inverse_ref, near_ref, sems,
):
    pairs = [
        (r_hbm, r_ref),
        (basis_hbm, basis_ref),
        (picked_hbm, picked),
        (near_hbm, near_ref),
        (coarse_hbm, coarse_ref),
        (inverse_hbm, inverse_ref),
    ]
    moves = [
        pltpu.make_async_copy(source, target, sems.at[i])
        for i, (source, target) in enumerate(pairs)
    ]
    for move in moves:
        move.start()
    for move in moves[:4]:
        move.wait()
    subs, cols, _ = out_ref.shape
    rows = r_ref.shape[2]
    kc = basis_ref.shape[0]
    r = r_ref[:, 0, :]
    low = r.astype(jnp.bfloat16)
    residual = lax.dot_general(
        r, basis_ref[...], LAST, precision=HIGH, preferred_element_type=jnp.float32
    )
    tail = jnp.concatenate([residual, jnp.zeros((cols, LANES - kc), jnp.float32)], axis=1)
    whole = jnp.concatenate([low, tail.astype(jnp.bfloat16)], axis=1)
    out_ref[...] = jnp.broadcast_to(whole[None], out_ref.shape)
    lane = lanes_of((cols, LANES))
    sub = lax.broadcasted_iota(jnp.int32, (cols, LANES), 0)
    wide = LANES // cols
    slots = picked.shape[0]
    near = near_ref[...]
    table = jnp.concatenate([near, jnp.zeros((1, LANES - slots), jnp.int32)], axis=1)
    table_ref[...] = jnp.where(lanes_of((1, LANES)) < live[0, 0], table, -1)
    for j in reversed(range(slots)):
        wanted = (picked[j] - rows // 2).astype(jnp.float32)
        wanted = jnp.broadcast_to(wanted, (cols, LANES))
        packed = jnp.zeros((cols, LANES), jnp.float32)
        for i in range(cols):
            moved = pltpu.roll(wanted, (kc - i * wide) % LANES, 1)
            packed = jnp.where(sub == i, moved, packed)
        packed = jnp.where((lane >= kc) & (lane < kc + wide), packed, tail)
        out_ref[near[0, j], :, rows : rows + LANES] = packed.astype(jnp.bfloat16)
    for move in moves[4:]:
        move.wait()


def write_share(at, with_terms, got_ref, coarse_ref, out_ref):
    subs, cols, _ = got_ref.shape
    owners = out_ref.shape[0]
    kc = coarse_ref.shape[0] // owners
    lane = lanes_of((cols, LANES))
    tiles = [jnp.zeros((cols, LANES), jnp.float32) for _ in range(subs * kc // LANES)]
    terms = jnp.zeros((cols, LANES), jnp.float32)
    for s in range(subs):
        got = got_ref[s, :, at : at + LANES].astype(jnp.float32)
        if with_terms:
            terms = terms + got
        t, off = divmod(s * kc, LANES)
        moved = pltpu.roll(got, off, 1) if off else got
        if off + kc <= LANES:
            tiles[t] = jnp.where((lane >= off) & (lane < off + kc), moved, tiles[t])
        else:
            tiles[t] = jnp.where(lane >= off, moved, tiles[t])
            tiles[t + 1] = jnp.where(lane < off + kc - LANES, moved, tiles[t + 1])
    residuals = jnp.concatenate(tiles, axis=1).astype(jnp.bfloat16)
    share = lax.dot_general(
        residuals, coarse_ref[...], LAST, preferred_element_type=jnp.float32
    )
    extra = jnp.zeros((cols, LANES), jnp.float32)
    if with_terms:
        summed = terms + pltpu.roll(terms, LANES - 3, 1) + pltpu.roll(terms, LANES - 6, 1)
        extra = jnp.where((lane >= kc) & (lane < kc + 3), summed, 0.0)
    wide = jnp.concatenate(
        [share, jnp.zeros((cols, -share.shape[1] % LANES), jnp.float32)], axis=1
    )
    for c in range(owners):
        t, off = divmod(c * kc, LANES)
        part = wide[:, t * LANES : (t + 1) * LANES]
        if off:
            part = pltpu.roll(part, LANES - off, 1)
        if off + kc > LANES:
            after = pltpu.roll(wide[:, (t + 1) * LANES : (t + 2) * LANES], LANES - off, 1)
            part = jnp.where(lane < LANES - off, part, after)
        out_ref[c] = jnp.where(lane < kc, part, extra)


def first_gather_kernel(
    near_ref, r_ref, picked_ref, got_ref, inverse_ref, coarse_ref, fine_ref, asked_ref, out_ref
):
    subs, cols, _ = got_ref.shape
    rows = r_ref.shape[2]
    slots = picked_ref.shape[0]
    write_share(rows, False, got_ref, coarse_ref, out_ref)
    near = near_ref[...]
    parts = [r_ref[:, 0, :].astype(jnp.bfloat16)]
    for j in range(slots):
        source = near[0, j]
        other = got_ref[jnp.maximum(source, 0), :, 0:rows].astype(jnp.float32)
        tiles = [twice(other[:, t * LANES : (t + 1) * LANES]) for t in range(rows // LANES)]
        index = jnp.broadcast_to(picked_ref[j], (2 * cols, LANES))
        part = pick_lanes(tiles, index)[:cols]
        parts.append(jnp.where(source >= 0, part, 0.0).astype(jnp.bfloat16))
    extended = jnp.concatenate(parts, axis=1)
    fine_ref[...] = lax.dot_general(
        extended, inverse_ref[...], LAST, preferred_element_type=jnp.float32
    )
    lane = lanes_of((cols, LANES))
    kc = coarse_ref.shape[0] // out_ref.shape[0]
    wide = LANES // cols
    for i in range(subs // 2):
        pair = []
        for s in (2 * i, 2 * i + 1):
            got = got_ref[s, :, rows : rows + LANES].astype(jnp.float32)
            index = jnp.zeros((cols, LANES), jnp.float32)
            for k in range(cols):
                moved = pltpu.roll(
                    jnp.broadcast_to(got[k : k + 1], (cols, LANES)), (k * wide - kc) % LANES, 1
                )
                index = jnp.where((lane >= k * wide) & (lane < (k + 1) * wide), moved, index)
            pair.append(index)
        index = jnp.concatenate(pair, axis=0).astype(jnp.int32) + rows // 2
        asked_ref[i] = jnp.clip(index, 0, rows - 1)


def second_gather_kernel(
    near_ref, vector_ref, got_ref, inverse_ref, coarse_ref, fine_ref, out_ref
):
    rows = vector_ref.shape[1]
    slots = (inverse_ref.shape[1] - rows) // LANES
    write_share(LANES, True, got_ref, coarse_ref, out_ref)
    margin = margin_from(got_ref, near_ref, slots)
    extended = jnp.concatenate([vector_ref[...].astype(jnp.bfloat16), margin], axis=1)
    fine_ref[...] = lax.dot_general(
        extended, inverse_ref[...], LAST, preferred_element_type=jnp.float32
    )


def prolong(summed, fine_ref, basis_ref):
    kc = basis_ref.shape[0]
    return fine_ref[...] + lax.dot_general(
        summed[:, :kc], basis_ref[...], FIRST, precision=HIGH, preferred_element_type=jnp.float32
    )


def first_direction_kernel(shares_ref, fine_ref, basis_ref, asked_ref, p_ref, out_ref):
    p = prolong(jnp.sum(shares_ref[...], axis=0), fine_ref, basis_ref)
    p_ref[...] = p
    send_rows(p, asked_ref, out_ref)


def operate(near_ref, vector_ref, got_ref, own_ref, coupling_ref):
    margin = margin_from(got_ref, near_ref, coupling_ref.shape[1] // LANES)
    low = vector_ref[...].astype(jnp.bfloat16)
    return lax.dot_general(
        low, own_ref[...], LAST, preferred_element_type=jnp.float32
    ) + lax.dot_general(margin, coupling_ref[...], LAST, preferred_element_type=jnp.float32)


def row_sum(x):
    return jnp.sum(x, axis=1, keepdims=True)


def first_operate_kernel(
    near_ref, p_ref, got_ref, own_ref, coupling_ref, r_ref, basis_ref, asked_ref, q_ref, out_ref
):
    cols = r_ref.shape[0]
    kc = basis_ref.shape[0]
    q = operate(near_ref, p_ref, got_ref, own_ref, coupling_ref)
    q_ref[...] = q
    r = r_ref[:, 0, :]
    residual = lax.dot_general(
        q, basis_ref[...], LAST, precision=HIGH, preferred_element_type=jnp.float32
    )
    tail = jnp.concatenate([residual, jnp.zeros((cols, LANES - kc), jnp.float32)], axis=1)
    lane = lanes_of((cols, LANES))
    for i, inner in enumerate([row_sum(r * r), row_sum(q * r), row_sum(q * q)]):
        for k, term in enumerate(split3(inner)):
            tail = jnp.where(lane == kc + 3 * k + i, term, tail)
    send_rows(q, asked_ref, out_ref)
    out_ref[:, :, LANES : 2 * LANES] = jnp.broadcast_to(
        tail.astype(jnp.bfloat16)[None], (out_ref.shape[0], cols, LANES)
    )


def second_direction_kernel(
    all_rows, shares_ref, fine_ref, basis_ref, asked_ref, r_ref, q_ref, p_ref,
    v1_ref, v2_ref, z1_ref, z2_ref, scalars_ref, out_ref,
):
    kc = basis_ref.shape[0]
    summed = jnp.sum(shares_ref[...], axis=0)
    p2 = prolong(summed, fine_ref, basis_ref)
    rr, qr, qq = [summed[:, kc + i : kc + i + 1] / all_rows for i in range(3)]
    start = jnp.sqrt(rr + EPS)
    h11 = qr / start / start
    part = h11 / start
    left = qq / start / start - 2.0 * part * (qr / start) + part * part * rr
    h21 = jnp.sqrt(jnp.maximum(left, 0.0) + EPS)
    v1 = r_ref[:, 0, :] / start
    z1 = p_ref[...] / start
    v2 = (q_ref[...] / start - h11 * v1) / h21
    z2 = (p2 / start - h11 * z1) / h21
    v1_ref[...] = v1
    v2_ref[...] = v2
    z1_ref[...] = z1
    z2_ref[...] = z2
    lane = lanes_of(scalars_ref.shape)
    scalars_ref[...] = place(start, lane, 0) + place(h11, lane, 1) + place(h21, lane, 2)
    send_rows(z2, asked_ref, out_ref)


def second_operate_kernel(
    near_ref, z_ref, got_ref, own_ref, coupling_ref, v1_ref, v2_ref, w_ref, out_ref
):
    w = operate(near_ref, z_ref, got_ref, own_ref, coupling_ref)
    w_ref[...] = w
    v1 = v1_ref[...]
    v2 = v2_ref[...]
    cols = w.shape[0]
    lane = lanes_of((cols, LANES))
    col = lax.broadcasted_iota(jnp.int32, (cols, LANES), 0)
    pairs = [(w, v1), (w, v2), (w, w), (v1, v1), (v1, v2), (v2, v2)]
    inner = jnp.zeros((cols, LANES), jnp.float32)
    for i, (a, b) in enumerate(pairs):
        inner = jnp.where(lane == i * cols + col, row_sum(a * b), inner)
    out_ref[...] = jnp.broadcast_to(jnp.sum(inner, axis=0, keepdims=True)[None], out_ref.shape)


def between_kernel(got_ref, out_ref):
    out_ref[...] = jnp.broadcast_to(jnp.sum(got_ref[...], axis=0)[None], out_ref.shape)


def last_kernel(
    all_rows, got_ref, w_ref, v1_ref, v2_ref, z1_ref, z2_ref, scalars_ref, answer_ref, next_ref
):
    cols = w_ref.shape[0]
    lane = lanes_of((cols, LANES))
    col = lax.broadcasted_iota(jnp.int32, (cols, LANES), 0)
    inner = jnp.broadcast_to(jnp.sum(got_ref[...], axis=0) / all_rows, (cols, LANES))
    h12, h22, ww, g11, g12, g22 = [
        row_sum(jnp.where(lane == i * cols + col, inner, 0.0)) for i in range(6)
    ]
    start, h11, h21 = [scalars_ref[:, i : i + 1] for i in range(3)]
    left = (
        ww
        - 2.0 * (h12 * h12 + h22 * h22)
        + h12 * h12 * g11
        + 2.0 * h12 * h22 * g12
        + h22 * h22 * g22
    )
    h32 = jnp.sqrt(jnp.maximum(left, 0.0) + EPS)
    next_ref[:, 0, :] = (w_ref[...] - h12 * v1_ref[...] - h22 * v2_ref[...]) / h32
    weights = least_squares(start, [[h11, h21], [h12, h22, h32]])
    answer_ref[:, 0, :] = weights[0] * z1_ref[...] + weights[1] * z2_ref[...]


def call(kernel, outs, *args, name):
    vmem = pl.BlockSpec(memory_space=pltpu.VMEM)
    return pl.pallas_call(
        kernel,
        out_shape=outs,
        in_specs=[vmem] * len(args),
        out_specs=jax.tree.map(lambda _: vmem, outs),
        compiler_params=pltpu.CompilerParams(vmem_limit_bytes=VMEM_BYTES),
        name=name,
    )(*args)


def body(
    right_side,
    own_block,
    coupling,
    local_inverse,
    coarse_basis,
    coarse_inverse,
    neighbours,
    margin_rows,
    block_counts,
):
    cols, rows = right_side.shape[0], right_side.shape[3]
    r = right_side.reshape(cols, 1, rows)
    own = own_block[0, 0]
    couple = coupling[0, 0]
    inverse = local_inverse[0, 0]
    basis = coarse_basis[0, 0]
    coarse = coarse_inverse[0, :, 0, :]
    near = neighbours[0]
    picked = margin_rows.reshape(margin_rows.shape[2], 1, margin_rows.shape[3])
    live = block_counts
    subs, owners = lax.axis_size("sub"), lax.axis_size("crs")
    all_rows = rows * subs * owners
    f32, bf16 = jnp.float32, jnp.bfloat16

    def shape(*dims, dtype=f32):
        return jax.ShapeDtypeStruct(dims, dtype)

    vector = shape(cols, rows)
    tile = shape(cols, LANES)

    def over_sub(blocks):
        return lax.all_to_all(blocks, "sub", 0, 0)

    def over_crs(blocks):
        return lax.all_to_all(blocks, "crs", 0, 0)

    held = [r, basis, picked, coarse, inverse]
    vmem = pl.BlockSpec(memory_space=pltpu.VMEM)
    sent, near, r, basis, picked, coarse, inverse = pl.pallas_call(
        first_send_kernel,
        out_shape=[shape(subs, cols, rows + LANES, dtype=bf16), shape(1, LANES, dtype=jnp.int32)]
        + [shape(*x.shape, dtype=x.dtype) for x in held],
        in_specs=[pl.BlockSpec(memory_space=pltpu.SMEM)]
        + [pl.BlockSpec(memory_space=pl.ANY)] * 6,
        out_specs=[vmem] * 7,
        scratch_shapes=[pltpu.VMEM(near.shape, jnp.int32), pltpu.SemaphoreType.DMA((6,))],
        compiler_params=pltpu.CompilerParams(vmem_limit_bytes=VMEM_BYTES),
        name="first_send",
    )(live, *[pltpu.with_memory_space_constraint(x, pltpu.HBM) for x in (near, *held)])
    got = over_sub(sent)
    fine, asked, shares = call(
        first_gather_kernel,
        (vector, shape(subs // 2, 2 * cols, LANES, dtype=jnp.int32), shape(owners, cols, LANES)),
        near, r, picked, got, inverse, coarse, name="first_gather",
    )
    shares = over_crs(shares)
    p1, sent = call(
        first_direction_kernel, (vector, shape(subs, cols, LANES, dtype=bf16)),
        shares, fine, basis, asked, name="first_direction",
    )
    got = over_sub(sent)
    q1, sent = call(
        first_operate_kernel, (vector, shape(subs, cols, 2 * LANES, dtype=bf16)),
        near, p1, got, own, couple, r, basis, asked, name="first_operate",
    )
    got = over_sub(sent)
    fine, shares = call(
        second_gather_kernel, (vector, shape(owners, cols, LANES)),
        near, q1, got, inverse, coarse, name="second_gather",
    )
    shares = over_crs(shares)

    def second_direction(*refs):
        second_direction_kernel(float(all_rows), *refs)

    v1, v2, z1, z2, scalars, sent = call(
        second_direction,
        (vector, vector, vector, vector, tile, shape(subs, cols, LANES, dtype=bf16)),
        shares, fine, basis, asked, r, q1, p1, name="second_direction",
    )
    got = over_sub(sent)
    w, sent = call(
        second_operate_kernel, (vector, shape(owners, 1, LANES)),
        near, z2, got, own, couple, v1, v2, name="second_operate",
    )
    got = over_crs(sent)
    sent = call(between_kernel, shape(subs, 1, LANES), got, name="between")
    got = over_sub(sent)

    def last(*refs):
        last_kernel(float(all_rows), *refs)

    answer, following = call(
        last, (shape(cols, 1, rows), shape(cols, 1, rows)),
        got, w, v1, v2, z1, z2, scalars, name="last",
    )
    out = (cols, 1, 1, rows)
    return answer.reshape(out), following.reshape(out)


def solution(mesh):
    in_specs = (
        P(None, "sub", "crs", None),
        P("sub", "crs", None, None),
        P("sub", "crs", None, None),
        P("sub", "crs", None, None),
        P("sub", "crs", None, None),
        P("sub", None, "crs", None),
        P("sub", "crs", None),
        P("sub", "crs", None, None),
        P("sub", "crs"),
    )
    out_specs = (P(None, "sub", "crs", None), P(None, "sub", "crs", None))
    return jax.shard_map(body, mesh=mesh, in_specs=in_specs, out_specs=out_specs, check_vma=False)
```

```python
import jax
import jax.numpy as jnp
from jax import lax
from jax.experimental import pallas as pl
from jax.experimental.pallas import tpu as pltpu
from jax.sharding import PartitionSpec as P

EPS = 1e-06
HIGH = lax.Precision.HIGH
LAST = (((1,), (1,)), ((), ()))
FIRST = (((1,), (0,)), ((), ()))
LANES = 128
VMEM_BYTES = 16 << 20


def least_squares(start_norm, columns):
    cosines = []
    sine_terms = []
    triangle = []
    target = [start_norm] + [jnp.zeros_like(start_norm) for j in range(len(columns))]
    for j, column in enumerate(columns):
        column = list(column)
        for i in range(j):
            upper_value = cosines[i] * column[i] + sine_terms[i] * column[i + 1]
            column[i + 1] = -sine_terms[i] * column[i] + cosines[i] * column[i + 1]
            column[i] = upper_value
        radius = jnp.sqrt(column[j] * column[j] + column[j + 1] * column[j + 1])
        cosine = column[j] / radius
        sine_part = column[j + 1] / radius
        column[j] = radius
        target[j + 1] = -sine_part * target[j]
        target[j] = cosine * target[j]
        cosines.append(cosine)
        sine_terms.append(sine_part)
        triangle.append(column[: j + 1])
    weights = [None] * len(columns)
    for j in reversed(range(len(columns))):
        running = target[j]
        for k in range(j + 1, len(columns)):
            running = running - triangle[k][j] * weights[k]
        weights[j] = running / triangle[j][j]
    return weights


def split3(x):
    hi = x.astype(jnp.bfloat16).astype(jnp.float32)
    rest = x - hi
    mid = rest.astype(jnp.bfloat16).astype(jnp.float32)
    return hi, mid, rest - mid


def place(column, lane, at):
    return jnp.where(lane == at, column, 0.0)


def pick_lanes(tiles, index):
    low = index & (LANES - 1)
    high = index >> 7
    out = jnp.take_along_axis(tiles[0], low, axis=1, mode="promise_in_bounds")
    for t in range(1, len(tiles)):
        other = jnp.take_along_axis(tiles[t], low, axis=1, mode="promise_in_bounds")
        out = jnp.where(high == t, other, out)
    return out


def lanes_of(shape):
    return lax.broadcasted_iota(jnp.int32, shape, 1)


def twice(x):
    return jnp.concatenate([x, x], axis=0)


def send_rows(vector, asked_ref, out_ref):
    tiles = [twice(vector[:, t * LANES : (t + 1) * LANES]) for t in range(vector.shape[1] // LANES)]
    cols = vector.shape[0]
    for i in range(asked_ref.shape[0]):
        chosen = pick_lanes(tiles, asked_ref[i])
        out_ref[2 * i, :, 0:LANES] = chosen[:cols].astype(jnp.bfloat16)
        out_ref[2 * i + 1, :, 0:LANES] = chosen[cols:].astype(jnp.bfloat16)


def margin_from(got_ref, near_ref, slots):
    near = near_ref[...]
    parts = []
    for j in range(slots):
        source = near[0, j]
        part = got_ref[jnp.maximum(source, 0), :, 0:LANES]
        parts.append(jnp.where(source >= 0, part, jnp.zeros_like(part)))
    return jnp.concatenate(parts, axis=1)


def first_send_kernel(
    live, near_hbm, r_hbm, basis_hbm, picked_hbm,
    out_ref, table_ref, r_ref, basis_ref, picked, near_ref, sems,
):
    pairs = [
        (r_hbm, r_ref),
        (basis_hbm, basis_ref),
        (picked_hbm, picked),
        (near_hbm, near_ref),
    ]
    moves = [
        pltpu.make_async_copy(source, target, sems.at[i])
        for i, (source, target) in enumerate(pairs)
    ]
    for move in moves:
        move.start()
    for move in moves[:4]:
        move.wait()
    subs, cols, _ = out_ref.shape
    rows = r_ref.shape[2]
    kc = basis_ref.shape[0]
    r = r_ref[:, 0, :]
    low = r.astype(jnp.bfloat16)
    residual = lax.dot_general(
        r, basis_ref[...], LAST, precision=HIGH, preferred_element_type=jnp.float32
    )
    tail = jnp.concatenate([residual, jnp.zeros((cols, LANES - kc), jnp.float32)], axis=1)
    whole = jnp.concatenate([low, tail.astype(jnp.bfloat16)], axis=1)
    out_ref[...] = jnp.broadcast_to(whole[None], out_ref.shape)
    lane = lanes_of((cols, LANES))
    sub = lax.broadcasted_iota(jnp.int32, (cols, LANES), 0)
    wide = LANES // cols
    slots = picked.shape[0]
    near = near_ref[...]
    table = jnp.concatenate([near, jnp.zeros((1, LANES - slots), jnp.int32)], axis=1)
    table_ref[...] = jnp.where(lanes_of((1, LANES)) < live[0, 0], table, -1)
    for j in reversed(range(slots)):
        wanted = (picked[j] - rows // 2).astype(jnp.float32)
        wanted = jnp.broadcast_to(wanted, (cols, LANES))
        packed = jnp.zeros((cols, LANES), jnp.float32)
        for i in range(cols):
            moved = pltpu.roll(wanted, (kc - i * wide) % LANES, 1)
            packed = jnp.where(sub == i, moved, packed)
        packed = jnp.where((lane >= kc) & (lane < kc + wide), packed, tail)
        out_ref[near[0, j], :, rows : rows + LANES] = packed.astype(jnp.bfloat16)
    for move in moves[4:]:
        move.wait()


def write_share(at, with_terms, got_ref, coarse_ref, out_ref):
    subs, cols, _ = got_ref.shape
    owners = out_ref.shape[0]
    kc = coarse_ref.shape[0] // owners
    lane = lanes_of((cols, LANES))
    tiles = [jnp.zeros((cols, LANES), jnp.float32) for _ in range(subs * kc // LANES)]
    terms = jnp.zeros((cols, LANES), jnp.float32)
    for s in range(subs):
        got = got_ref[s, :, at : at + LANES].astype(jnp.float32)
        if with_terms:
            terms = terms + got
        t, off = divmod(s * kc, LANES)
        moved = pltpu.roll(got, off, 1) if off else got
        if off + kc <= LANES:
            tiles[t] = jnp.where((lane >= off) & (lane < off + kc), moved, tiles[t])
        else:
            tiles[t] = jnp.where(lane >= off, moved, tiles[t])
            tiles[t + 1] = jnp.where(lane < off + kc - LANES, moved, tiles[t + 1])
    residuals = jnp.concatenate(tiles, axis=1).astype(jnp.bfloat16)
    share = lax.dot_general(
        residuals, coarse_ref[...], LAST, preferred_element_type=jnp.float32
    )
    extra = jnp.zeros((cols, LANES), jnp.float32)
    if with_terms:
        summed = terms + pltpu.roll(terms, LANES - 3, 1) + pltpu.roll(terms, LANES - 6, 1)
        extra = jnp.where((lane >= kc) & (lane < kc + 3), summed, 0.0)
    wide = jnp.concatenate(
        [share, jnp.zeros((cols, -share.shape[1] % LANES), jnp.float32)], axis=1
    )
    for c in range(owners):
        t, off = divmod(c * kc, LANES)
        part = wide[:, t * LANES : (t + 1) * LANES]
        if off:
            part = pltpu.roll(part, LANES - off, 1)
        if off + kc > LANES:
            after = pltpu.roll(wide[:, (t + 1) * LANES : (t + 2) * LANES], LANES - off, 1)
            part = jnp.where(lane < LANES - off, part, after)
        out_ref[c] = jnp.where(lane < kc, part, extra)


def first_gather_kernel(
    near_ref, r_ref, picked_ref, got_ref, coarse_ref, extended_ref, asked_ref, out_ref
):
    subs, cols, _ = got_ref.shape
    rows = r_ref.shape[2]
    slots = picked_ref.shape[0]
    write_share(rows, False, got_ref, coarse_ref, out_ref)
    near = near_ref[...]
    parts = [r_ref[:, 0, :].astype(jnp.bfloat16)]
    for j in range(slots):
        source = near[0, j]
        other = got_ref[jnp.maximum(source, 0), :, 0:rows].astype(jnp.float32)
        tiles = [twice(other[:, t * LANES : (t + 1) * LANES]) for t in range(rows // LANES)]
        index = jnp.broadcast_to(picked_ref[j], (2 * cols, LANES))
        part = pick_lanes(tiles, index)[:cols]
        parts.append(jnp.where(source >= 0, part, 0.0).astype(jnp.bfloat16))
    extended_ref[...] = jnp.concatenate(parts, axis=1)
    lane = lanes_of((cols, LANES))
    kc = coarse_ref.shape[0] // out_ref.shape[0]
    wide = LANES // cols
    for i in range(subs // 2):
        pair = []
        for s in (2 * i, 2 * i + 1):
            got = got_ref[s, :, rows : rows + LANES].astype(jnp.float32)
            index = jnp.zeros((cols, LANES), jnp.float32)
            for k in range(cols):
                moved = pltpu.roll(
                    jnp.broadcast_to(got[k : k + 1], (cols, LANES)), (k * wide - kc) % LANES, 1
                )
                index = jnp.where((lane >= k * wide) & (lane < (k + 1) * wide), moved, index)
            pair.append(index)
        index = jnp.concatenate(pair, axis=0).astype(jnp.int32) + rows // 2
        asked_ref[i] = jnp.clip(index, 0, rows - 1)


def second_gather_kernel(
    near_ref, vector_ref, got_ref, coarse_ref, extended_ref, out_ref
):
    rows = vector_ref.shape[1]
    slots = (extended_ref.shape[1] - rows) // LANES
    write_share(LANES, True, got_ref, coarse_ref, out_ref)
    margin = margin_from(got_ref, near_ref, slots)
    extended_ref[...] = jnp.concatenate([vector_ref[...].astype(jnp.bfloat16), margin], axis=1)


def prolong(summed, extended_ref, inverse_ref, basis_ref):
    kc = basis_ref.shape[0]
    fine = lax.dot_general(
        extended_ref[...], inverse_ref[...], LAST, preferred_element_type=jnp.float32
    )
    return fine + lax.dot_general(
        summed[:, :kc], basis_ref[...], FIRST, precision=HIGH, preferred_element_type=jnp.float32
    )


def first_direction_kernel(shares_ref, extended_ref, inverse_ref, basis_ref, asked_ref, p_ref, out_ref):
    p = prolong(jnp.sum(shares_ref[...], axis=0), extended_ref, inverse_ref, basis_ref)
    p_ref[...] = p
    send_rows(p, asked_ref, out_ref)


def operate(near_ref, vector_ref, got_ref, own_ref, coupling_ref):
    margin = margin_from(got_ref, near_ref, coupling_ref.shape[1] // LANES)
    low = vector_ref[...].astype(jnp.bfloat16)
    return lax.dot_general(
        low, own_ref[...], LAST, preferred_element_type=jnp.float32
    ) + lax.dot_general(margin, coupling_ref[...], LAST, preferred_element_type=jnp.float32)


def row_sum(x):
    return jnp.sum(x, axis=1, keepdims=True)


def first_operate_kernel(
    near_ref, p_ref, got_ref, own_ref, coupling_ref, r_ref, basis_ref, asked_ref, q_ref, out_ref
):
    cols = r_ref.shape[0]
    kc = basis_ref.shape[0]
    q = operate(near_ref, p_ref, got_ref, own_ref, coupling_ref)
    q_ref[...] = q
    r = r_ref[:, 0, :]
    residual = lax.dot_general(
        q, basis_ref[...], LAST, precision=HIGH, preferred_element_type=jnp.float32
    )
    tail = jnp.concatenate([residual, jnp.zeros((cols, LANES - kc), jnp.float32)], axis=1)
    lane = lanes_of((cols, LANES))
    for i, inner in enumerate([row_sum(r * r), row_sum(q * r), row_sum(q * q)]):
        for k, term in enumerate(split3(inner)):
            tail = jnp.where(lane == kc + 3 * k + i, term, tail)
    send_rows(q, asked_ref, out_ref)
    out_ref[:, :, LANES : 2 * LANES] = jnp.broadcast_to(
        tail.astype(jnp.bfloat16)[None], (out_ref.shape[0], cols, LANES)
    )


def second_direction_kernel(
    all_rows, shares_ref, extended_ref, inverse_ref, basis_ref, asked_ref, r_ref, q_ref, p_ref,
    v1_ref, v2_ref, z1_ref, z2_ref, scalars_ref, out_ref,
):
    kc = basis_ref.shape[0]
    summed = jnp.sum(shares_ref[...], axis=0)
    p2 = prolong(summed, extended_ref, inverse_ref, basis_ref)
    rr, qr, qq = [summed[:, kc + i : kc + i + 1] / all_rows for i in range(3)]
    start = jnp.sqrt(rr + EPS)
    h11 = qr / start / start
    part = h11 / start
    left = qq / start / start - 2.0 * part * (qr / start) + part * part * rr
    h21 = jnp.sqrt(jnp.maximum(left, 0.0) + EPS)
    v1 = r_ref[:, 0, :] / start
    z1 = p_ref[...] / start
    v2 = (q_ref[...] / start - h11 * v1) / h21
    z2 = (p2 / start - h11 * z1) / h21
    v1_ref[...] = v1
    v2_ref[...] = v2
    z1_ref[...] = z1
    z2_ref[...] = z2
    lane = lanes_of(scalars_ref.shape)
    scalars_ref[...] = place(start, lane, 0) + place(h11, lane, 1) + place(h21, lane, 2)
    send_rows(z2, asked_ref, out_ref)


def second_operate_kernel(
    near_ref, z_ref, got_ref, own_ref, coupling_ref, v1_ref, v2_ref, w_ref, out_ref
):
    w = operate(near_ref, z_ref, got_ref, own_ref, coupling_ref)
    w_ref[...] = w
    v1 = v1_ref[...]
    v2 = v2_ref[...]
    cols = w.shape[0]
    lane = lanes_of((cols, LANES))
    col = lax.broadcasted_iota(jnp.int32, (cols, LANES), 0)
    pairs = [(w, v1), (w, v2), (w, w), (v1, v1), (v1, v2), (v2, v2)]
    inner = jnp.zeros((cols, LANES), jnp.float32)
    for i, (a, b) in enumerate(pairs):
        inner = jnp.where(lane == i * cols + col, row_sum(a * b), inner)
    out_ref[...] = jnp.broadcast_to(jnp.sum(inner, axis=0, keepdims=True)[None], out_ref.shape)


def between_kernel(got_ref, out_ref):
    out_ref[...] = jnp.broadcast_to(jnp.sum(got_ref[...], axis=0)[None], out_ref.shape)


def last_kernel(
    all_rows, got_ref, w_ref, v1_ref, v2_ref, z1_ref, z2_ref, scalars_ref, answer_ref, next_ref
):
    cols = w_ref.shape[0]
    lane = lanes_of((cols, LANES))
    col = lax.broadcasted_iota(jnp.int32, (cols, LANES), 0)
    inner = jnp.sum(got_ref[...], axis=0, keepdims=True) / all_rows
    inner = jnp.broadcast_to(inner, (cols, LANES))
    h12, h22, ww, g11, g12, g22 = [
        row_sum(jnp.where(lane == i * cols + col, inner, 0.0)) for i in range(6)
    ]
    start, h11, h21 = [scalars_ref[:, i : i + 1] for i in range(3)]
    left = (
        ww
        - 2.0 * (h12 * h12 + h22 * h22)
        + h12 * h12 * g11
        + 2.0 * h12 * h22 * g12
        + h22 * h22 * g22
    )
    h32 = jnp.sqrt(jnp.maximum(left, 0.0) + EPS)
    next_ref[:, 0, :] = (w_ref[...] - h12 * v1_ref[...] - h22 * v2_ref[...]) / h32
    weights = least_squares(start, [[h11, h21], [h12, h22, h32]])
    answer_ref[:, 0, :] = weights[0] * z1_ref[...] + weights[1] * z2_ref[...]


def call(kernel, outs, *args, name):
    vmem = pl.BlockSpec(memory_space=pltpu.VMEM)
    return pl.pallas_call(
        kernel,
        out_shape=outs,
        in_specs=[vmem] * len(args),
        out_specs=jax.tree.map(lambda _: vmem, outs),
        compiler_params=pltpu.CompilerParams(vmem_limit_bytes=VMEM_BYTES),
        name=name,
    )(*args)


def body(
    right_side,
    own_block,
    coupling,
    local_inverse,
    coarse_basis,
    coarse_inverse,
    neighbours,
    margin_rows,
    block_counts,
):
    cols, rows = right_side.shape[0], right_side.shape[3]
    r = right_side.reshape(cols, 1, rows)
    own = own_block[0, 0]
    couple = coupling[0, 0]
    inverse = local_inverse[0, 0]
    basis = coarse_basis[0, 0]
    coarse = coarse_inverse[0, :, 0, :]
    near = neighbours[0]
    picked = margin_rows.reshape(margin_rows.shape[2], 1, margin_rows.shape[3])
    live = block_counts
    subs, owners = lax.axis_size("sub"), lax.axis_size("crs")
    all_rows = rows * subs * owners
    f32, bf16 = jnp.float32, jnp.bfloat16

    def shape(*dims, dtype=f32):
        return jax.ShapeDtypeStruct(dims, dtype)

    vector = shape(cols, rows)
    tile = shape(cols, LANES)

    def over_sub(blocks):
        return lax.all_to_all(blocks, "sub", 0, 0)

    def over_crs(blocks):
        return lax.all_to_all(blocks, "crs", 0, 0)

    held = [r, basis, picked]
    vmem = pl.BlockSpec(memory_space=pltpu.VMEM)
    sent, near, r, basis, picked = pl.pallas_call(
        first_send_kernel,
        out_shape=[shape(subs, cols, rows + LANES, dtype=bf16), shape(1, LANES, dtype=jnp.int32)]
        + [shape(*x.shape, dtype=x.dtype) for x in held],
        in_specs=[pl.BlockSpec(memory_space=pltpu.SMEM)]
        + [pl.BlockSpec(memory_space=pl.ANY)] * 4,
        out_specs=[vmem] * 5,
        scratch_shapes=[pltpu.VMEM(near.shape, jnp.int32), pltpu.SemaphoreType.DMA((8,))],
        compiler_params=pltpu.CompilerParams(vmem_limit_bytes=VMEM_BYTES),
        cost_estimate=pl.CostEstimate(
            flops=1 << 34, bytes_accessed=1 << 30, transcendentals=0
        ),
        name="first_send",
    )(live, *[pltpu.with_memory_space_constraint(x, pltpu.HBM) for x in (near, *held)])
    got = over_sub(sent)
    extended, asked, shares = call(
        first_gather_kernel,
        (
            shape(cols, inverse.shape[1], dtype=bf16),
            shape(subs // 2, 2 * cols, LANES, dtype=jnp.int32),
            shape(owners, cols, LANES),
        ),
        near, r, picked, got, coarse, name="first_gather",
    )
    shares = over_crs(shares)
    p1, sent = call(
        first_direction_kernel, (vector, shape(subs, cols, LANES, dtype=bf16)),
        shares, extended, inverse, basis, asked, name="first_direction",
    )
    got = over_sub(sent)
    q1, sent = call(
        first_operate_kernel, (vector, shape(subs, cols, 2 * LANES, dtype=bf16)),
        near, p1, got, own, couple, r, basis, asked, name="first_operate",
    )
    got = over_sub(sent)
    extended, shares = call(
        second_gather_kernel,
        (shape(cols, inverse.shape[1], dtype=bf16), shape(owners, cols, LANES)),
        near, q1, got, coarse, name="second_gather",
    )
    shares = over_crs(shares)

    def second_direction(*refs):
        second_direction_kernel(float(all_rows), *refs)

    v1, v2, z1, z2, scalars, sent = call(
        second_direction,
        (vector, vector, vector, vector, tile, shape(subs, cols, LANES, dtype=bf16)),
        shares, extended, inverse, basis, asked, r, q1, p1, name="second_direction",
    )
    got = over_sub(sent)
    w, sent = call(
        second_operate_kernel, (vector, shape(owners, 1, LANES)),
        near, z2, got, own, couple, v1, v2, name="second_operate",
    )
    got = over_crs(sent)
    sent = call(between_kernel, shape(subs, 1, LANES), got, name="between")
    got = over_sub(sent).reshape(subs, LANES)

    def last(*refs):
        last_kernel(float(all_rows), *refs)

    answer, following = call(
        last, (shape(cols, 1, rows), shape(cols, 1, rows)),
        got, w, v1, v2, z1, z2, scalars, name="last",
    )
    out = (cols, 1, 1, rows)
    return answer.reshape(out), following.reshape(out)


def solution(mesh):
    in_specs = (
        P(None, "sub", "crs", None),
        P("sub", "crs", None, None),
        P("sub", "crs", None, None),
        P("sub", "crs", None, None),
        P("sub", "crs", None, None),
        P("sub", None, "crs", None),
        P("sub", "crs", None),
        P("sub", "crs", None, None),
        P("sub", "crs"),
    )
    out_specs = (P(None, "sub", "crs", None), P(None, "sub", "crs", None))
    return jax.shard_map(body, mesh=mesh, in_specs=in_specs, out_specs=out_specs, check_vma=False)
```

```python
import jax
import jax.numpy as jnp
from jax import lax
from jax.experimental import pallas as pl
from jax.experimental.pallas import tpu as pltpu
from jax.sharding import PartitionSpec as P

EPS = 1e-06
HIGH = lax.Precision.HIGH
LAST = (((1,), (1,)), ((), ()))
FIRST = (((1,), (0,)), ((), ()))
LANES = 128
VMEM_BYTES = 16 << 20
PLANES = 16
NEAR = 4
STRIDE = 7
BACK = pow(STRIDE, -1, PLANES)


def order_of(subs):
    return [STRIDE * (i // NEAR) % PLANES * NEAR + i % NEAR for i in range(subs)]


def place_of(sub):
    return (((sub >> 2) * BACK) & (PLANES - 1)) * NEAR + (sub & (NEAR - 1))


def least_squares(start_norm, columns):
    cosines = []
    sine_terms = []
    triangle = []
    target = [start_norm] + [jnp.zeros_like(start_norm) for j in range(len(columns))]
    for j, column in enumerate(columns):
        column = list(column)
        for i in range(j):
            upper_value = cosines[i] * column[i] + sine_terms[i] * column[i + 1]
            column[i + 1] = -sine_terms[i] * column[i] + cosines[i] * column[i + 1]
            column[i] = upper_value
        radius = jnp.sqrt(column[j] * column[j] + column[j + 1] * column[j + 1])
        cosine = column[j] / radius
        sine_part = column[j + 1] / radius
        column[j] = radius
        target[j + 1] = -sine_part * target[j]
        target[j] = cosine * target[j]
        cosines.append(cosine)
        sine_terms.append(sine_part)
        triangle.append(column[: j + 1])
    weights = [None] * len(columns)
    for j in reversed(range(len(columns))):
        running = target[j]
        for k in range(j + 1, len(columns)):
            running = running - triangle[k][j] * weights[k]
        weights[j] = running / triangle[j][j]
    return weights


def split3(x):
    hi = x.astype(jnp.bfloat16).astype(jnp.float32)
    rest = x - hi
    mid = rest.astype(jnp.bfloat16).astype(jnp.float32)
    return hi, mid, rest - mid


def place(column, lane, at):
    return jnp.where(lane == at, column, 0.0)


def pick_lanes(tiles, index):
    low = index & (LANES - 1)
    high = index >> 7
    out = jnp.take_along_axis(tiles[0], low, axis=1, mode="promise_in_bounds")
    for t in range(1, len(tiles)):
        other = jnp.take_along_axis(tiles[t], low, axis=1, mode="promise_in_bounds")
        out = jnp.where(high == t, other, out)
    return out


def lanes_of(shape):
    return lax.broadcasted_iota(jnp.int32, shape, 1)


def twice(x):
    return jnp.concatenate([x, x], axis=0)


def send_rows(vector, asked_ref, out_ref):
    tiles = [twice(vector[:, t * LANES : (t + 1) * LANES]) for t in range(vector.shape[1] // LANES)]
    cols = vector.shape[0]
    for i in range(asked_ref.shape[0]):
        chosen = pick_lanes(tiles, asked_ref[i])
        out_ref[2 * i, :, 0:LANES] = chosen[:cols].astype(jnp.bfloat16)
        out_ref[2 * i + 1, :, 0:LANES] = chosen[cols:].astype(jnp.bfloat16)


def margin_from(got_ref, near_ref, slots):
    near = near_ref[...]
    parts = []
    for j in range(slots):
        source = near[0, j]
        part = got_ref[jnp.maximum(source, 0), :, 0:LANES]
        parts.append(jnp.where(source >= 0, part, jnp.zeros_like(part)))
    return jnp.concatenate(parts, axis=1)


def first_send_kernel(
    live, near_hbm, r_hbm, basis_hbm, picked_hbm,
    out_ref, table_ref, r_ref, basis_ref, picked, near_ref, sems,
):
    pairs = [
        (r_hbm, r_ref),
        (basis_hbm, basis_ref),
        (picked_hbm, picked),
        (near_hbm, near_ref),
    ]
    moves = [
        pltpu.make_async_copy(source, target, sems.at[i])
        for i, (source, target) in enumerate(pairs)
    ]
    for move in moves:
        move.start()
    for move in moves[:4]:
        move.wait()
    subs, cols, _ = out_ref.shape
    rows = r_ref.shape[2]
    kc = basis_ref.shape[0]
    r = r_ref[:, 0, :]
    low = r.astype(jnp.bfloat16)
    residual = lax.dot_general(
        r, basis_ref[...], LAST, precision=HIGH, preferred_element_type=jnp.float32
    )
    tail = jnp.concatenate([residual, jnp.zeros((cols, LANES - kc), jnp.float32)], axis=1)
    whole = jnp.concatenate([low, tail.astype(jnp.bfloat16)], axis=1)
    out_ref[...] = jnp.broadcast_to(whole[None], out_ref.shape)
    lane = lanes_of((cols, LANES))
    sub = lax.broadcasted_iota(jnp.int32, (cols, LANES), 0)
    wide = LANES // cols
    slots = picked.shape[0]
    near = place_of(near_ref[...])
    table = jnp.concatenate([near, jnp.zeros((1, LANES - slots), jnp.int32)], axis=1)
    table_ref[...] = jnp.where(lanes_of((1, LANES)) < live[0, 0], table, -1)
    for j in reversed(range(slots)):
        wanted = (picked[j] - rows // 2).astype(jnp.float32)
        wanted = jnp.broadcast_to(wanted, (cols, LANES))
        packed = jnp.zeros((cols, LANES), jnp.float32)
        for i in range(cols):
            moved = pltpu.roll(wanted, (kc - i * wide) % LANES, 1)
            packed = jnp.where(sub == i, moved, packed)
        packed = jnp.where((lane >= kc) & (lane < kc + wide), packed, tail)
        out_ref[near[0, j], :, rows : rows + LANES] = packed.astype(jnp.bfloat16)
    for move in moves[4:]:
        move.wait()


def write_share(at, with_terms, got_ref, coarse_ref, out_ref):
    subs, cols, _ = got_ref.shape
    owners = out_ref.shape[0]
    kc = coarse_ref.shape[0] // owners
    lane = lanes_of((cols, LANES))
    tiles = [jnp.zeros((cols, LANES), jnp.float32) for _ in range(subs * kc // LANES)]
    terms = jnp.zeros((cols, LANES), jnp.float32)
    for block, s in enumerate(order_of(subs)):
        got = got_ref[block, :, at : at + LANES].astype(jnp.float32)
        if with_terms:
            terms = terms + got
        t, off = divmod(s * kc, LANES)
        moved = pltpu.roll(got, off, 1) if off else got
        if off + kc <= LANES:
            tiles[t] = jnp.where((lane >= off) & (lane < off + kc), moved, tiles[t])
        else:
            tiles[t] = jnp.where(lane >= off, moved, tiles[t])
            tiles[t + 1] = jnp.where(lane < off + kc - LANES, moved, tiles[t + 1])
    residuals = jnp.concatenate(tiles, axis=1).astype(jnp.bfloat16)
    share = lax.dot_general(
        residuals, coarse_ref[...], LAST, preferred_element_type=jnp.float32
    )
    extra = jnp.zeros((cols, LANES), jnp.float32)
    if with_terms:
        summed = terms + pltpu.roll(terms, LANES - 3, 1) + pltpu.roll(terms, LANES - 6, 1)
        extra = jnp.where((lane >= kc) & (lane < kc + 3), summed, 0.0)
    wide = jnp.concatenate(
        [share, jnp.zeros((cols, -share.shape[1] % LANES), jnp.float32)], axis=1
    )
    for c in range(owners):
        t, off = divmod(c * kc, LANES)
        part = wide[:, t * LANES : (t + 1) * LANES]
        if off:
            part = pltpu.roll(part, LANES - off, 1)
        if off + kc > LANES:
            after = pltpu.roll(wide[:, (t + 1) * LANES : (t + 2) * LANES], LANES - off, 1)
            part = jnp.where(lane < LANES - off, part, after)
        out_ref[c] = jnp.where(lane < kc, part, extra)


def first_gather_kernel(
    near_ref, r_ref, picked_ref, got_ref, coarse_ref, extended_ref, asked_ref, out_ref
):
    subs, cols, _ = got_ref.shape
    rows = r_ref.shape[2]
    slots = picked_ref.shape[0]
    write_share(rows, False, got_ref, coarse_ref, out_ref)
    near = near_ref[...]
    parts = [r_ref[:, 0, :].astype(jnp.bfloat16)]
    for j in range(slots):
        source = near[0, j]
        other = got_ref[jnp.maximum(source, 0), :, 0:rows].astype(jnp.float32)
        tiles = [twice(other[:, t * LANES : (t + 1) * LANES]) for t in range(rows // LANES)]
        index = jnp.broadcast_to(picked_ref[j], (2 * cols, LANES))
        part = pick_lanes(tiles, index)[:cols]
        parts.append(jnp.where(source >= 0, part, 0.0).astype(jnp.bfloat16))
    extended_ref[...] = jnp.concatenate(parts, axis=1)
    lane = lanes_of((cols, LANES))
    kc = coarse_ref.shape[0] // out_ref.shape[0]
    wide = LANES // cols
    for i in range(subs // 2):
        pair = []
        for s in (2 * i, 2 * i + 1):
            got = got_ref[s, :, rows : rows + LANES].astype(jnp.float32)
            index = jnp.zeros((cols, LANES), jnp.float32)
            for k in range(cols):
                moved = pltpu.roll(
                    jnp.broadcast_to(got[k : k + 1], (cols, LANES)), (k * wide - kc) % LANES, 1
                )
                index = jnp.where((lane >= k * wide) & (lane < (k + 1) * wide), moved, index)
            pair.append(index)
        index = jnp.concatenate(pair, axis=0).astype(jnp.int32) + rows // 2
        asked_ref[i] = jnp.clip(index, 0, rows - 1)


def second_gather_kernel(
    near_ref, vector_ref, got_ref, coarse_ref, extended_ref, out_ref
):
    rows = vector_ref.shape[1]
    slots = (extended_ref.shape[1] - rows) // LANES
    write_share(LANES, True, got_ref, coarse_ref, out_ref)
    margin = margin_from(got_ref, near_ref, slots)
    extended_ref[...] = jnp.concatenate([vector_ref[...].astype(jnp.bfloat16), margin], axis=1)


def prolong(summed, extended_ref, inverse_ref, basis_ref):
    kc = basis_ref.shape[0]
    fine = lax.dot_general(
        extended_ref[...], inverse_ref[...], LAST, preferred_element_type=jnp.float32
    )
    return fine + lax.dot_general(
        summed[:, :kc], basis_ref[...], FIRST, precision=HIGH, preferred_element_type=jnp.float32
    )


def first_direction_kernel(shares_ref, extended_ref, inverse_ref, basis_ref, asked_ref, p_ref, out_ref):
    p = prolong(jnp.sum(shares_ref[...], axis=0), extended_ref, inverse_ref, basis_ref)
    p_ref[...] = p
    send_rows(p, asked_ref, out_ref)


def operate(near_ref, vector_ref, got_ref, own_ref, coupling_ref):
    margin = margin_from(got_ref, near_ref, coupling_ref.shape[1] // LANES)
    low = vector_ref[...].astype(jnp.bfloat16)
    return lax.dot_general(
        low, own_ref[...], LAST, preferred_element_type=jnp.float32
    ) + lax.dot_general(margin, coupling_ref[...], LAST, preferred_element_type=jnp.float32)


def row_sum(x):
    return jnp.sum(x, axis=1, keepdims=True)


def first_operate_kernel(
    near_ref, p_ref, got_ref, own_ref, coupling_ref, r_ref, basis_ref, asked_ref, q_ref, out_ref
):
    cols = r_ref.shape[0]
    kc = basis_ref.shape[0]
    q = operate(near_ref, p_ref, got_ref, own_ref, coupling_ref)
    q_ref[...] = q
    r = r_ref[:, 0, :]
    residual = lax.dot_general(
        q, basis_ref[...], LAST, precision=HIGH, preferred_element_type=jnp.float32
    )
    tail = jnp.concatenate([residual, jnp.zeros((cols, LANES - kc), jnp.float32)], axis=1)
    lane = lanes_of((cols, LANES))
    for i, inner in enumerate([row_sum(r * r), row_sum(q * r), row_sum(q * q)]):
        for k, term in enumerate(split3(inner)):
            tail = jnp.where(lane == kc + 3 * k + i, term, tail)
    send_rows(q, asked_ref, out_ref)
    out_ref[:, :, LANES : 2 * LANES] = jnp.broadcast_to(
        tail.astype(jnp.bfloat16)[None], (out_ref.shape[0], cols, LANES)
    )


def second_direction_kernel(
    all_rows, shares_ref, extended_ref, inverse_ref, basis_ref, asked_ref, r_ref, q_ref, p_ref,
    v1_ref, v2_ref, z1_ref, z2_ref, scalars_ref, out_ref,
):
    kc = basis_ref.shape[0]
    summed = jnp.sum(shares_ref[...], axis=0)
    p2 = prolong(summed, extended_ref, inverse_ref, basis_ref)
    rr, qr, qq = [summed[:, kc + i : kc + i + 1] / all_rows for i in range(3)]
    start = jnp.sqrt(rr + EPS)
    h11 = qr / start / start
    part = h11 / start
    left = qq / start / start - 2.0 * part * (qr / start) + part * part * rr
    h21 = jnp.sqrt(jnp.maximum(left, 0.0) + EPS)
    v1 = r_ref[:, 0, :] / start
    z1 = p_ref[...] / start
    v2 = (q_ref[...] / start - h11 * v1) / h21
    z2 = (p2 / start - h11 * z1) / h21
    v1_ref[...] = v1
    v2_ref[...] = v2
    z1_ref[...] = z1
    z2_ref[...] = z2
    lane = lanes_of(scalars_ref.shape)
    scalars_ref[...] = place(start, lane, 0) + place(h11, lane, 1) + place(h21, lane, 2)
    send_rows(z2, asked_ref, out_ref)


def second_operate_kernel(
    near_ref, z_ref, got_ref, own_ref, coupling_ref, v1_ref, v2_ref, w_ref, out_ref
):
    w = operate(near_ref, z_ref, got_ref, own_ref, coupling_ref)
    w_ref[...] = w
    v1 = v1_ref[...]
    v2 = v2_ref[...]
    cols = w.shape[0]
    lane = lanes_of((cols, LANES))
    col = lax.broadcasted_iota(jnp.int32, (cols, LANES), 0)
    pairs = [(w, v1), (w, v2), (w, w), (v1, v1), (v1, v2), (v2, v2)]
    inner = jnp.zeros((cols, LANES), jnp.float32)
    for i, (a, b) in enumerate(pairs):
        inner = jnp.where(lane == i * cols + col, row_sum(a * b), inner)
    out_ref[...] = jnp.broadcast_to(jnp.sum(inner, axis=0, keepdims=True)[None], out_ref.shape)


def between_kernel(got_ref, out_ref):
    out_ref[...] = jnp.broadcast_to(jnp.sum(got_ref[...], axis=0)[None], out_ref.shape)


def last_kernel(
    all_rows, got_ref, w_ref, v1_ref, v2_ref, z1_ref, z2_ref, scalars_ref, answer_ref, next_ref
):
    cols = w_ref.shape[0]
    lane = lanes_of((cols, LANES))
    col = lax.broadcasted_iota(jnp.int32, (cols, LANES), 0)
    inner = jnp.sum(got_ref[...], axis=0, keepdims=True) / all_rows
    inner = jnp.broadcast_to(inner, (cols, LANES))
    h12, h22, ww, g11, g12, g22 = [
        row_sum(jnp.where(lane == i * cols + col, inner, 0.0)) for i in range(6)
    ]
    start, h11, h21 = [scalars_ref[:, i : i + 1] for i in range(3)]
    left = (
        ww
        - 2.0 * (h12 * h12 + h22 * h22)
        + h12 * h12 * g11
        + 2.0 * h12 * h22 * g12
        + h22 * h22 * g22
    )
    h32 = jnp.sqrt(jnp.maximum(left, 0.0) + EPS)
    next_ref[:, 0, :] = (w_ref[...] - h12 * v1_ref[...] - h22 * v2_ref[...]) / h32
    weights = least_squares(start, [[h11, h21], [h12, h22, h32]])
    answer_ref[:, 0, :] = weights[0] * z1_ref[...] + weights[1] * z2_ref[...]


def call(kernel, outs, *args, name):
    vmem = pl.BlockSpec(memory_space=pltpu.VMEM)
    return pl.pallas_call(
        kernel,
        out_shape=outs,
        in_specs=[vmem] * len(args),
        out_specs=jax.tree.map(lambda _: vmem, outs),
        compiler_params=pltpu.CompilerParams(vmem_limit_bytes=VMEM_BYTES),
        name=name,
    )(*args)


def body(
    right_side,
    own_block,
    coupling,
    local_inverse,
    coarse_basis,
    coarse_inverse,
    neighbours,
    margin_rows,
    block_counts,
):
    cols, rows = right_side.shape[0], right_side.shape[3]
    r = right_side.reshape(cols, 1, rows)
    own = own_block[0, 0]
    couple = coupling[0, 0]
    inverse = local_inverse[0, 0]
    basis = coarse_basis[0, 0]
    coarse = coarse_inverse[0, :, 0, :]
    near = neighbours[0]
    picked = margin_rows.reshape(margin_rows.shape[2], 1, margin_rows.shape[3])
    live = block_counts
    subs, owners = lax.axis_size("sub"), lax.axis_size("crs")
    all_rows = rows * subs * owners
    f32, bf16 = jnp.float32, jnp.bfloat16

    def shape(*dims, dtype=f32):
        return jax.ShapeDtypeStruct(dims, dtype)

    vector = shape(cols, rows)
    tile = shape(cols, LANES)

    def over_sub(blocks):
        return lax.all_to_all(blocks, "sub", 0, 0, axis_index_groups=[order_of(subs)])

    def over_crs(blocks):
        return lax.all_to_all(blocks, "crs", 0, 0)

    held = [r, basis, picked]
    vmem = pl.BlockSpec(memory_space=pltpu.VMEM)
    sent, near, r, basis, picked = pl.pallas_call(
        first_send_kernel,
        out_shape=[shape(subs, cols, rows + LANES, dtype=bf16), shape(1, LANES, dtype=jnp.int32)]
        + [shape(*x.shape, dtype=x.dtype) for x in held],
        in_specs=[pl.BlockSpec(memory_space=pltpu.SMEM)]
        + [pl.BlockSpec(memory_space=pl.ANY)] * 4,
        out_specs=[vmem] * 5,
        scratch_shapes=[pltpu.VMEM(near.shape, jnp.int32), pltpu.SemaphoreType.DMA((8,))],
        compiler_params=pltpu.CompilerParams(vmem_limit_bytes=VMEM_BYTES),
        cost_estimate=pl.CostEstimate(
            flops=1 << 34, bytes_accessed=1 << 30, transcendentals=0
        ),
        name="first_send",
    )(live, *[pltpu.with_memory_space_constraint(x, pltpu.HBM) for x in (near, *held)])
    got = over_sub(sent)
    extended, asked, shares = call(
        first_gather_kernel,
        (
            shape(cols, inverse.shape[1], dtype=bf16),
            shape(subs // 2, 2 * cols, LANES, dtype=jnp.int32),
            shape(owners, cols, LANES),
        ),
        near, r, picked, got, coarse, name="first_gather",
    )
    shares = over_crs(shares)
    p1, sent = call(
        first_direction_kernel, (vector, shape(subs, cols, LANES, dtype=bf16)),
        shares, extended, inverse, basis, asked, name="first_direction",
    )
    got = over_sub(sent)
    q1, sent = call(
        first_operate_kernel, (vector, shape(subs, cols, 2 * LANES, dtype=bf16)),
        near, p1, got, own, couple, r, basis, asked, name="first_operate",
    )
    got = over_sub(sent)
    extended, shares = call(
        second_gather_kernel,
        (shape(cols, inverse.shape[1], dtype=bf16), shape(owners, cols, LANES)),
        near, q1, got, coarse, name="second_gather",
    )
    shares = over_crs(shares)

    def second_direction(*refs):
        second_direction_kernel(float(all_rows), *refs)

    v1, v2, z1, z2, scalars, sent = call(
        second_direction,
        (vector, vector, vector, vector, tile, shape(subs, cols, LANES, dtype=bf16)),
        shares, extended, inverse, basis, asked, r, q1, p1, name="second_direction",
    )
    got = over_sub(sent)
    w, sent = call(
        second_operate_kernel, (vector, shape(owners, 1, LANES)),
        near, z2, got, own, couple, v1, v2, name="second_operate",
    )
    got = over_crs(sent)
    sent = call(between_kernel, shape(subs, 1, LANES), got, name="between")
    got = over_sub(sent).reshape(subs, LANES)

    def last(*refs):
        last_kernel(float(all_rows), *refs)

    answer, following = call(
        last, (shape(cols, 1, rows), shape(cols, 1, rows)),
        got, w, v1, v2, z1, z2, scalars, name="last",
    )
    out = (cols, 1, 1, rows)
    return answer.reshape(out), following.reshape(out)


def solution(mesh):
    in_specs = (
        P(None, "sub", "crs", None),
        P("sub", "crs", None, None),
        P("sub", "crs", None, None),
        P("sub", "crs", None, None),
        P("sub", "crs", None, None),
        P("sub", None, "crs", None),
        P("sub", "crs", None),
        P("sub", "crs", None, None),
        P("sub", "crs"),
    )
    out_specs = (P(None, "sub", "crs", None), P(None, "sub", "crs", None))
    return jax.shard_map(body, mesh=mesh, in_specs=in_specs, out_specs=out_specs, check_vma=False)
```

```python
import jax
import jax.numpy as jnp
from jax import lax
from jax.experimental import pallas as pl
from jax.experimental.pallas import tpu as pltpu
from jax.sharding import PartitionSpec as P

EPS = 1e-06
HIGH = lax.Precision.HIGH
LAST = (((1,), (1,)), ((), ()))
FIRST = (((1,), (0,)), ((), ()))
LANES = 128
VMEM_BYTES = 16 << 20
PLANES = 16
NEAR = 4
STRIDE = 7
BACK = pow(STRIDE, -1, PLANES)


def order_of(subs):
    return [STRIDE * (i // NEAR) % PLANES * NEAR + i % NEAR for i in range(subs)]


def place_of(sub):
    return (((sub >> 2) * BACK) & (PLANES - 1)) * NEAR + (sub & (NEAR - 1))


def least_squares(start_norm, columns):
    cosines = []
    sine_terms = []
    triangle = []
    target = [start_norm] + [jnp.zeros_like(start_norm) for j in range(len(columns))]
    for j, column in enumerate(columns):
        column = list(column)
        for i in range(j):
            upper_value = cosines[i] * column[i] + sine_terms[i] * column[i + 1]
            column[i + 1] = -sine_terms[i] * column[i] + cosines[i] * column[i + 1]
            column[i] = upper_value
        radius = jnp.sqrt(column[j] * column[j] + column[j + 1] * column[j + 1])
        cosine = column[j] / radius
        sine_part = column[j + 1] / radius
        column[j] = radius
        target[j + 1] = -sine_part * target[j]
        target[j] = cosine * target[j]
        cosines.append(cosine)
        sine_terms.append(sine_part)
        triangle.append(column[: j + 1])
    weights = [None] * len(columns)
    for j in reversed(range(len(columns))):
        running = target[j]
        for k in range(j + 1, len(columns)):
            running = running - triangle[k][j] * weights[k]
        weights[j] = running / triangle[j][j]
    return weights


def split3(x):
    hi = x.astype(jnp.bfloat16).astype(jnp.float32)
    rest = x - hi
    mid = rest.astype(jnp.bfloat16).astype(jnp.float32)
    return hi, mid, rest - mid


def halves(x):
    hi = x.astype(jnp.bfloat16)
    return jnp.concatenate([hi, (x - hi.astype(jnp.float32)).astype(jnp.bfloat16)], axis=0)


def joined(x):
    rows = x.shape[0] // 2
    return x[:rows] + x[rows:]


def place(column, lane, at):
    return jnp.where(lane == at, column, 0.0)


def pick_lanes(tiles, index):
    low = index & (LANES - 1)
    high = index >> 7
    out = jnp.take_along_axis(tiles[0], low, axis=1, mode="promise_in_bounds")
    for t in range(1, len(tiles)):
        other = jnp.take_along_axis(tiles[t], low, axis=1, mode="promise_in_bounds")
        out = jnp.where(high == t, other, out)
    return out


def lanes_of(shape):
    return lax.broadcasted_iota(jnp.int32, shape, 1)


def twice(x):
    return jnp.concatenate([x, x], axis=0)


def send_rows(vector, asked_ref, out_ref):
    tiles = [twice(vector[:, t * LANES : (t + 1) * LANES]) for t in range(vector.shape[1] // LANES)]
    cols = vector.shape[0]
    for i in range(asked_ref.shape[0]):
        chosen = pick_lanes(tiles, asked_ref[i])
        out_ref[2 * i, :, 0:LANES] = chosen[:cols].astype(jnp.bfloat16)
        out_ref[2 * i + 1, :, 0:LANES] = chosen[cols:].astype(jnp.bfloat16)


def margin_from(got_ref, near_ref, slots):
    near = near_ref[...]
    parts = []
    for j in range(slots):
        source = near[0, j]
        part = got_ref[jnp.maximum(source, 0), :, 0:LANES]
        parts.append(jnp.where(source >= 0, part, jnp.zeros_like(part)))
    return jnp.concatenate(parts, axis=1)


def first_send_kernel(
    live, near_hbm, r_hbm, basis_hbm, picked_hbm,
    out_ref, table_ref, r_ref, basis_ref, picked, near_ref, sems,
):
    pairs = [
        (r_hbm, r_ref),
        (basis_hbm, basis_ref),
        (picked_hbm, picked),
        (near_hbm, near_ref),
    ]
    moves = [
        pltpu.make_async_copy(source, target, sems.at[i])
        for i, (source, target) in enumerate(pairs)
    ]
    for move in moves:
        move.start()
    for move in moves[:4]:
        move.wait()
    subs, cols, _ = out_ref.shape
    rows = r_ref.shape[2]
    kc = basis_ref.shape[0]
    r = r_ref[:, 0, :]
    low = r.astype(jnp.bfloat16)
    residual = lax.dot_general(
        r, basis_ref[...], LAST, precision=HIGH, preferred_element_type=jnp.float32
    )
    tail = jnp.concatenate([residual, jnp.zeros((cols, LANES - kc), jnp.float32)], axis=1)
    whole = jnp.concatenate([low, tail.astype(jnp.bfloat16)], axis=1)
    out_ref[...] = jnp.broadcast_to(whole[None], out_ref.shape)
    lane = lanes_of((cols, LANES))
    sub = lax.broadcasted_iota(jnp.int32, (cols, LANES), 0)
    wide = LANES // cols
    slots = picked.shape[0]
    near = place_of(near_ref[...])
    table = jnp.concatenate([near, jnp.zeros((1, LANES - slots), jnp.int32)], axis=1)
    table_ref[...] = jnp.where(lanes_of((1, LANES)) < live[0, 0], table, -1)
    for j in reversed(range(slots)):
        wanted = (picked[j] - rows // 2).astype(jnp.float32)
        wanted = jnp.broadcast_to(wanted, (cols, LANES))
        packed = jnp.zeros((cols, LANES), jnp.float32)
        for i in range(cols):
            moved = pltpu.roll(wanted, (kc - i * wide) % LANES, 1)
            packed = jnp.where(sub == i, moved, packed)
        packed = jnp.where((lane >= kc) & (lane < kc + wide), packed, tail)
        out_ref[near[0, j], :, rows : rows + LANES] = packed.astype(jnp.bfloat16)
    for move in moves[4:]:
        move.wait()


def write_share(at, with_terms, got_ref, coarse_ref, out_ref):
    subs, cols, _ = got_ref.shape
    owners = out_ref.shape[0]
    kc = coarse_ref.shape[0] // owners
    lane = lanes_of((cols, LANES))
    tiles = [jnp.zeros((cols, LANES), jnp.float32) for _ in range(subs * kc // LANES)]
    terms = jnp.zeros((cols, LANES), jnp.float32)
    for block, s in enumerate(order_of(subs)):
        got = got_ref[block, :, at : at + LANES].astype(jnp.float32)
        if with_terms:
            terms = terms + got
        t, off = divmod(s * kc, LANES)
        moved = pltpu.roll(got, off, 1) if off else got
        if off + kc <= LANES:
            tiles[t] = jnp.where((lane >= off) & (lane < off + kc), moved, tiles[t])
        else:
            tiles[t] = jnp.where(lane >= off, moved, tiles[t])
            tiles[t + 1] = jnp.where(lane < off + kc - LANES, moved, tiles[t + 1])
    residuals = jnp.concatenate(tiles, axis=1).astype(jnp.bfloat16)
    share = lax.dot_general(
        residuals, coarse_ref[...], LAST, preferred_element_type=jnp.float32
    )
    extra = jnp.zeros((cols, LANES), jnp.float32)
    if with_terms:
        summed = terms + pltpu.roll(terms, LANES - 3, 1) + pltpu.roll(terms, LANES - 6, 1)
        extra = jnp.where((lane >= kc) & (lane < kc + 3), summed, 0.0)
    wide = jnp.concatenate(
        [share, jnp.zeros((cols, -share.shape[1] % LANES), jnp.float32)], axis=1
    )
    for c in range(owners):
        t, off = divmod(c * kc, LANES)
        part = wide[:, t * LANES : (t + 1) * LANES]
        if off:
            part = pltpu.roll(part, LANES - off, 1)
        if off + kc > LANES:
            after = pltpu.roll(wide[:, (t + 1) * LANES : (t + 2) * LANES], LANES - off, 1)
            part = jnp.where(lane < LANES - off, part, after)
        out_ref[c] = jnp.where(lane < kc, part, extra)


def first_gather_kernel(
    near_ref, r_ref, picked_ref, got_ref, coarse_ref, extended_ref, asked_ref, out_ref
):
    subs, cols, _ = got_ref.shape
    rows = r_ref.shape[2]
    slots = picked_ref.shape[0]
    write_share(rows, False, got_ref, coarse_ref, out_ref)
    near = near_ref[...]
    parts = []
    for j in range(slots):
        source = near[0, j]
        other = got_ref[jnp.maximum(source, 0), :, 0:rows].astype(jnp.float32)
        tiles = [twice(other[:, t * LANES : (t + 1) * LANES]) for t in range(rows // LANES)]
        index = jnp.broadcast_to(picked_ref[j], (2 * cols, LANES))
        part = pick_lanes(tiles, index)[:cols]
        parts.append(jnp.where(source >= 0, part, 0.0).astype(jnp.bfloat16))
    margin = jnp.concatenate(parts, axis=1)
    extended_ref[...] = extend(r_ref[:, 0, :], margin)
    lane = lanes_of((cols, LANES))
    kc = coarse_ref.shape[0] // out_ref.shape[0]
    wide = LANES // cols
    for i in range(subs // 2):
        pair = []
        for s in (2 * i, 2 * i + 1):
            got = got_ref[s, :, rows : rows + LANES].astype(jnp.float32)
            index = jnp.zeros((cols, LANES), jnp.float32)
            for k in range(cols):
                moved = pltpu.roll(
                    jnp.broadcast_to(got[k : k + 1], (cols, LANES)), (k * wide - kc) % LANES, 1
                )
                index = jnp.where((lane >= k * wide) & (lane < (k + 1) * wide), moved, index)
            pair.append(index)
        index = jnp.concatenate(pair, axis=0).astype(jnp.int32) + rows // 2
        asked_ref[i] = jnp.clip(index, 0, rows - 1)


def second_gather_kernel(
    near_ref, vector_ref, got_ref, coarse_ref, extended_ref, out_ref
):
    rows = vector_ref.shape[1]
    slots = (extended_ref.shape[1] - rows) // LANES
    write_share(LANES, True, got_ref, coarse_ref, out_ref)
    margin = margin_from(got_ref, near_ref, slots)
    extended_ref[...] = extend(vector_ref[...], margin)


def prolong(summed, extended_ref, inverse_ref, basis_ref):
    kc = basis_ref.shape[0]
    fine = lax.dot_general(
        extended_ref[...], inverse_ref[...], LAST, preferred_element_type=jnp.float32
    )
    return joined(fine) + lax.dot_general(
        summed[:, :kc], basis_ref[...], FIRST, precision=HIGH, preferred_element_type=jnp.float32
    )


def first_direction_kernel(shares_ref, extended_ref, inverse_ref, basis_ref, asked_ref, p_ref, out_ref):
    p = prolong(jnp.sum(shares_ref[...], axis=0), extended_ref, inverse_ref, basis_ref)
    p_ref[...] = p
    send_rows(p, asked_ref, out_ref)


def operate(near_ref, vector_ref, got_ref, own_ref, coupling_ref):
    margin = margin_from(got_ref, near_ref, coupling_ref.shape[1] // LANES)
    own = lax.dot_general(
        halves(vector_ref[...]), own_ref[...], LAST, preferred_element_type=jnp.float32
    )
    return joined(own) + lax.dot_general(margin, coupling_ref[...], LAST, preferred_element_type=jnp.float32)


def extend(vector, margin):
    return jnp.concatenate([halves(vector), jnp.concatenate([margin, jnp.zeros_like(margin)])], axis=1)


def row_sum(x):
    return jnp.sum(x, axis=1, keepdims=True)


def first_operate_kernel(
    near_ref, p_ref, got_ref, own_ref, coupling_ref, r_ref, basis_ref, asked_ref, q_ref, out_ref
):
    cols = r_ref.shape[0]
    kc = basis_ref.shape[0]
    q = operate(near_ref, p_ref, got_ref, own_ref, coupling_ref)
    q_ref[...] = q
    r = r_ref[:, 0, :]
    residual = lax.dot_general(
        q, basis_ref[...], LAST, precision=HIGH, preferred_element_type=jnp.float32
    )
    tail = jnp.concatenate([residual, jnp.zeros((cols, LANES - kc), jnp.float32)], axis=1)
    lane = lanes_of((cols, LANES))
    for i, inner in enumerate([row_sum(r * r), row_sum(q * r), row_sum(q * q)]):
        for k, term in enumerate(split3(inner)):
            tail = jnp.where(lane == kc + 3 * k + i, term, tail)
    send_rows(q, asked_ref, out_ref)
    out_ref[:, :, LANES : 2 * LANES] = jnp.broadcast_to(
        tail.astype(jnp.bfloat16)[None], (out_ref.shape[0], cols, LANES)
    )


def second_direction_kernel(
    all_rows, shares_ref, extended_ref, inverse_ref, basis_ref, asked_ref, r_ref, q_ref, p_ref,
    v1_ref, v2_ref, z1_ref, z2_ref, scalars_ref, out_ref,
):
    kc = basis_ref.shape[0]
    summed = jnp.sum(shares_ref[...], axis=0)
    p2 = prolong(summed, extended_ref, inverse_ref, basis_ref)
    rr, qr, qq = [summed[:, kc + i : kc + i + 1] / all_rows for i in range(3)]
    start = jnp.sqrt(rr + EPS)
    h11 = qr / start / start
    part = h11 / start
    left = qq / start / start - 2.0 * part * (qr / start) + part * part * rr
    h21 = jnp.sqrt(jnp.maximum(left, 0.0) + EPS)
    v1 = r_ref[:, 0, :] / start
    z1 = p_ref[...] / start
    v2 = (q_ref[...] / start - h11 * v1) / h21
    z2 = (p2 / start - h11 * z1) / h21
    v1_ref[...] = v1
    v2_ref[...] = v2
    z1_ref[...] = z1
    z2_ref[...] = z2
    lane = lanes_of(scalars_ref.shape)
    scalars_ref[...] = place(start, lane, 0) + place(h11, lane, 1) + place(h21, lane, 2)
    send_rows(z2, asked_ref, out_ref)


def second_operate_kernel(
    near_ref, z_ref, got_ref, own_ref, coupling_ref, v1_ref, v2_ref, w_ref, out_ref
):
    w = operate(near_ref, z_ref, got_ref, own_ref, coupling_ref)
    w_ref[...] = w
    v1 = v1_ref[...]
    v2 = v2_ref[...]
    cols = w.shape[0]
    lane = lanes_of((cols, LANES))
    col = lax.broadcasted_iota(jnp.int32, (cols, LANES), 0)
    pairs = [(w, v1), (w, v2), (w, w), (v1, v1), (v1, v2), (v2, v2)]
    inner = jnp.zeros((cols, LANES), jnp.float32)
    for i, (a, b) in enumerate(pairs):
        inner = jnp.where(lane == i * cols + col, row_sum(a * b), inner)
    out_ref[...] = jnp.broadcast_to(jnp.sum(inner, axis=0, keepdims=True)[None], out_ref.shape)


def between_kernel(got_ref, out_ref):
    out_ref[...] = jnp.broadcast_to(jnp.sum(got_ref[...], axis=0)[None], out_ref.shape)


def last_kernel(
    all_rows, got_ref, w_ref, v1_ref, v2_ref, z1_ref, z2_ref, scalars_ref, answer_ref, next_ref
):
    cols = w_ref.shape[0]
    lane = lanes_of((cols, LANES))
    col = lax.broadcasted_iota(jnp.int32, (cols, LANES), 0)
    inner = jnp.sum(got_ref[...], axis=0, keepdims=True) / all_rows
    inner = jnp.broadcast_to(inner, (cols, LANES))
    h12, h22, ww, g11, g12, g22 = [
        row_sum(jnp.where(lane == i * cols + col, inner, 0.0)) for i in range(6)
    ]
    start, h11, h21 = [scalars_ref[:, i : i + 1] for i in range(3)]
    left = (
        ww
        - 2.0 * (h12 * h12 + h22 * h22)
        + h12 * h12 * g11
        + 2.0 * h12 * h22 * g12
        + h22 * h22 * g22
    )
    h32 = jnp.sqrt(jnp.maximum(left, 0.0) + EPS)
    next_ref[:, 0, :] = (w_ref[...] - h12 * v1_ref[...] - h22 * v2_ref[...]) / h32
    weights = least_squares(start, [[h11, h21], [h12, h22, h32]])
    answer_ref[:, 0, :] = weights[0] * z1_ref[...] + weights[1] * z2_ref[...]


def call(kernel, outs, *args, name):
    vmem = pl.BlockSpec(memory_space=pltpu.VMEM)
    return pl.pallas_call(
        kernel,
        out_shape=outs,
        in_specs=[vmem] * len(args),
        out_specs=jax.tree.map(lambda _: vmem, outs),
        compiler_params=pltpu.CompilerParams(vmem_limit_bytes=VMEM_BYTES),
        name=name,
    )(*args)


def body(
    right_side,
    own_block,
    coupling,
    local_inverse,
    coarse_basis,
    coarse_inverse,
    neighbours,
    margin_rows,
    block_counts,
):
    cols, rows = right_side.shape[0], right_side.shape[3]
    r = right_side.reshape(cols, 1, rows)
    own = own_block[0, 0]
    couple = coupling[0, 0]
    inverse = local_inverse[0, 0]
    basis = coarse_basis[0, 0]
    coarse = coarse_inverse[0, :, 0, :]
    near = neighbours[0]
    picked = margin_rows.reshape(margin_rows.shape[2], 1, margin_rows.shape[3])
    live = block_counts
    subs, owners = lax.axis_size("sub"), lax.axis_size("crs")
    all_rows = rows * subs * owners
    f32, bf16 = jnp.float32, jnp.bfloat16

    def shape(*dims, dtype=f32):
        return jax.ShapeDtypeStruct(dims, dtype)

    vector = shape(cols, rows)
    tile = shape(cols, LANES)

    def over_sub(blocks):
        return lax.all_to_all(blocks, "sub", 0, 0, axis_index_groups=[order_of(subs)])

    def over_crs(blocks):
        return lax.all_to_all(blocks, "crs", 0, 0)

    held = [r, basis, picked]
    vmem = pl.BlockSpec(memory_space=pltpu.VMEM)
    sent, near, r, basis, picked = pl.pallas_call(
        first_send_kernel,
        out_shape=[shape(subs, cols, rows + LANES, dtype=bf16), shape(1, LANES, dtype=jnp.int32)]
        + [shape(*x.shape, dtype=x.dtype) for x in held],
        in_specs=[pl.BlockSpec(memory_space=pltpu.SMEM)]
        + [pl.BlockSpec(memory_space=pl.ANY)] * 4,
        out_specs=[vmem] * 5,
        scratch_shapes=[pltpu.VMEM(near.shape, jnp.int32), pltpu.SemaphoreType.DMA((8,))],
        compiler_params=pltpu.CompilerParams(vmem_limit_bytes=VMEM_BYTES),
        cost_estimate=pl.CostEstimate(
            flops=1 << 34, bytes_accessed=1 << 30, transcendentals=0
        ),
        name="first_send",
    )(live, *[pltpu.with_memory_space_constraint(x, pltpu.HBM) for x in (near, *held)])
    got = over_sub(sent)
    extended, asked, shares = call(
        first_gather_kernel,
        (
            shape(2 * cols, inverse.shape[1], dtype=bf16),
            shape(subs // 2, 2 * cols, LANES, dtype=jnp.int32),
            shape(owners, cols, LANES),
        ),
        near, r, picked, got, coarse, name="first_gather",
    )
    shares = over_crs(shares)
    p1, sent = call(
        first_direction_kernel, (vector, shape(subs, cols, LANES, dtype=bf16)),
        shares, extended, inverse, basis, asked, name="first_direction",
    )
    got = over_sub(sent)
    q1, sent = call(
        first_operate_kernel, (vector, shape(subs, cols, 2 * LANES, dtype=bf16)),
        near, p1, got, own, couple, r, basis, asked, name="first_operate",
    )
    got = over_sub(sent)
    extended, shares = call(
        second_gather_kernel,
        (shape(2 * cols, inverse.shape[1], dtype=bf16), shape(owners, cols, LANES)),
        near, q1, got, coarse, name="second_gather",
    )
    shares = over_crs(shares)

    def second_direction(*refs):
        second_direction_kernel(float(all_rows), *refs)

    v1, v2, z1, z2, scalars, sent = call(
        second_direction,
        (vector, vector, vector, vector, tile, shape(subs, cols, LANES, dtype=bf16)),
        shares, extended, inverse, basis, asked, r, q1, p1, name="second_direction",
    )
    got = over_sub(sent)
    w, sent = call(
        second_operate_kernel, (vector, shape(owners, 1, LANES)),
        near, z2, got, own, couple, v1, v2, name="second_operate",
    )
    got = over_crs(sent)
    sent = call(between_kernel, shape(subs, 1, LANES), got, name="between")
    got = over_sub(sent).reshape(subs, LANES)

    def last(*refs):
        last_kernel(float(all_rows), *refs)

    answer, following = call(
        last, (shape(cols, 1, rows), shape(cols, 1, rows)),
        got, w, v1, v2, z1, z2, scalars, name="last",
    )
    out = (cols, 1, 1, rows)
    return answer.reshape(out), following.reshape(out)


def solution(mesh):
    in_specs = (
        P(None, "sub", "crs", None),
        P("sub", "crs", None, None),
        P("sub", "crs", None, None),
        P("sub", "crs", None, None),
        P("sub", "crs", None, None),
        P("sub", None, "crs", None),
        P("sub", "crs", None),
        P("sub", "crs", None, None),
        P("sub", "crs"),
    )
    out_specs = (P(None, "sub", "crs", None), P(None, "sub", "crs", None))
    return jax.shard_map(body, mesh=mesh, in_specs=in_specs, out_specs=out_specs, check_vma=False)
```

```python
import jax
import jax.numpy as jnp
from jax import lax
from jax.experimental import pallas as pl
from jax.experimental.pallas import tpu as pltpu
from jax.sharding import PartitionSpec as P

EPS = 1e-06
HIGH = lax.Precision.HIGH
LAST = (((1,), (1,)), ((), ()))
FIRST = (((1,), (0,)), ((), ()))
LANES = 128
VMEM_BYTES = 16 << 20
PLANES = 16
NEAR = 4
STRIDE = 7
BACK = pow(STRIDE, -1, PLANES)


def order_of(subs):
    return [STRIDE * (i // NEAR) % PLANES * NEAR + i % NEAR for i in range(subs)]


def place_of(sub):
    return (((sub >> 2) * BACK) & (PLANES - 1)) * NEAR + (sub & (NEAR - 1))


def least_squares(start_norm, columns):
    cosines = []
    sine_terms = []
    triangle = []
    target = [start_norm] + [jnp.zeros_like(start_norm) for j in range(len(columns))]
    for j, column in enumerate(columns):
        column = list(column)
        for i in range(j):
            upper_value = cosines[i] * column[i] + sine_terms[i] * column[i + 1]
            column[i + 1] = -sine_terms[i] * column[i] + cosines[i] * column[i + 1]
            column[i] = upper_value
        radius = jnp.sqrt(column[j] * column[j] + column[j + 1] * column[j + 1])
        cosine = column[j] / radius
        sine_part = column[j + 1] / radius
        column[j] = radius
        target[j + 1] = -sine_part * target[j]
        target[j] = cosine * target[j]
        cosines.append(cosine)
        sine_terms.append(sine_part)
        triangle.append(column[: j + 1])
    weights = [None] * len(columns)
    for j in reversed(range(len(columns))):
        running = target[j]
        for k in range(j + 1, len(columns)):
            running = running - triangle[k][j] * weights[k]
        weights[j] = running / triangle[j][j]
    return weights


def split3(x):
    hi = x.astype(jnp.bfloat16).astype(jnp.float32)
    rest = x - hi
    mid = rest.astype(jnp.bfloat16).astype(jnp.float32)
    return hi, mid, rest - mid


def halves(x):
    hi = x.astype(jnp.bfloat16)
    return jnp.concatenate([hi, (x - hi.astype(jnp.float32)).astype(jnp.bfloat16)], axis=0)


def joined(x):
    rows = x.shape[0] // 2
    return x[:rows] + x[rows:]


def place(column, lane, at):
    return jnp.where(lane == at, column, 0.0)


def pick_lanes(tiles, index):
    low = index & (LANES - 1)
    high = index >> 7
    out = jnp.take_along_axis(tiles[0], low, axis=1, mode="promise_in_bounds")
    for t in range(1, len(tiles)):
        other = jnp.take_along_axis(tiles[t], low, axis=1, mode="promise_in_bounds")
        out = jnp.where(high == t, other, out)
    return out


def lanes_of(shape):
    return lax.broadcasted_iota(jnp.int32, shape, 1)


def twice(x):
    return jnp.concatenate([x, x], axis=0)


def send_rows(vector, asked_ref, out_ref):
    tiles = [twice(vector[:, t * LANES : (t + 1) * LANES]) for t in range(vector.shape[1] // LANES)]
    cols = vector.shape[0]
    height = out_ref.shape[1]
    for i in range(asked_ref.shape[0]):
        chosen = pick_lanes(tiles, asked_ref[i])
        for at in range(0, 2 * cols, height):
            part, t = divmod(at, cols)
            lanes = pl.ds(t // height * LANES, LANES)
            out_ref[2 * i + part, :, lanes] = chosen[at : at + height].astype(jnp.bfloat16)


def margin_from(got_ref, near_ref, slots, cols):
    near = near_ref[...]
    parts = []
    for j in range(slots):
        source = near[0, j]
        part = got_ref[jnp.maximum(source, 0)]
        parts.append(jnp.where(source >= 0, part, jnp.zeros_like(part)).astype(jnp.float32))
    width = cols // got_ref.shape[1]
    columns = [
        jnp.concatenate([part[:, t * LANES : (t + 1) * LANES] for part in parts], axis=1)
        for t in range(width)
    ]
    return jnp.concatenate(columns, axis=0).astype(jnp.bfloat16)


def first_send_kernel(
    live, near_hbm, r_hbm, basis_hbm, picked_hbm,
    out_ref, table_ref, r_ref, basis_ref, picked, near_ref, sems,
):
    pairs = [
        (r_hbm, r_ref),
        (basis_hbm, basis_ref),
        (picked_hbm, picked),
        (near_hbm, near_ref),
    ]
    moves = [
        pltpu.make_async_copy(source, target, sems.at[i])
        for i, (source, target) in enumerate(pairs)
    ]
    for move in moves:
        move.start()
    for move in moves[:4]:
        move.wait()
    subs, cols, _ = out_ref.shape
    rows = r_ref.shape[2]
    kc = basis_ref.shape[0]
    r = r_ref[:, 0, :]
    low = r.astype(jnp.bfloat16)
    residual = lax.dot_general(
        r, basis_ref[...], LAST, precision=HIGH, preferred_element_type=jnp.float32
    )
    tail = jnp.concatenate([residual, jnp.zeros((cols, LANES - kc), jnp.float32)], axis=1)
    whole = jnp.concatenate([low, tail.astype(jnp.bfloat16)], axis=1)
    out_ref[...] = jnp.broadcast_to(whole[None], out_ref.shape)
    lane = lanes_of((cols, LANES))
    sub = lax.broadcasted_iota(jnp.int32, (cols, LANES), 0)
    wide = LANES // cols
    slots = picked.shape[0]
    near = place_of(near_ref[...])
    table = jnp.concatenate([near, jnp.zeros((1, LANES - slots), jnp.int32)], axis=1)
    table_ref[...] = jnp.where(lanes_of((1, LANES)) < live[0, 0], table, -1)
    for j in reversed(range(slots)):
        wanted = (picked[j] - rows // 2).astype(jnp.float32)
        wanted = jnp.broadcast_to(wanted, (cols, LANES))
        packed = jnp.zeros((cols, LANES), jnp.float32)
        for i in range(cols):
            moved = pltpu.roll(wanted, (kc - i * wide) % LANES, 1)
            packed = jnp.where(sub == i, moved, packed)
        packed = jnp.where((lane >= kc) & (lane < kc + wide), packed, tail)
        out_ref[near[0, j], :, rows : rows + LANES] = packed.astype(jnp.bfloat16)
    for move in moves[4:]:
        move.wait()


def write_share(at, with_terms, got_ref, coarse_ref, out_ref):
    subs, height, _ = got_ref.shape
    owners, cols, _ = out_ref.shape
    kc = coarse_ref.shape[0] // owners
    lane = lanes_of((height, LANES))
    width = cols // height
    zero = jnp.zeros((height, LANES), jnp.float32)
    tiles = [[zero] * (subs * kc // LANES) for _ in range(width)]
    terms = zero
    for block, s in enumerate(order_of(subs)):
        got = got_ref[block, :, at : at + LANES].astype(jnp.float32)
        if with_terms:
            terms = terms + got
        t, off = divmod(s * kc, LANES)
        for part in range(width):
            mine = tiles[part]
            turn = (off - part * (LANES // width)) % LANES
            moved = pltpu.roll(got, turn, 1) if turn else got
            if off + kc <= LANES:
                mine[t] = jnp.where((lane >= off) & (lane < off + kc), moved, mine[t])
            else:
                mine[t] = jnp.where(lane >= off, moved, mine[t])
                mine[t + 1] = jnp.where(lane < off + kc - LANES, moved, mine[t + 1])
    residuals = [jnp.concatenate(mine, axis=1) for mine in tiles]
    residuals = jnp.concatenate(residuals, axis=0).astype(jnp.bfloat16)
    if width > 1:
        terms = jnp.concatenate([terms, pltpu.roll(terms, LANES // width, 1)], axis=0)
    lane = lanes_of((cols, LANES))
    share = lax.dot_general(
        residuals, coarse_ref[...], LAST, preferred_element_type=jnp.float32
    )
    extra = jnp.zeros((cols, LANES), jnp.float32)
    if with_terms:
        summed = terms + pltpu.roll(terms, LANES - 3, 1) + pltpu.roll(terms, LANES - 6, 1)
        extra = jnp.where((lane >= kc) & (lane < kc + 3), summed, 0.0)
    wide = jnp.concatenate(
        [share, jnp.zeros((cols, -share.shape[1] % LANES), jnp.float32)], axis=1
    )
    for c in range(owners):
        t, off = divmod(c * kc, LANES)
        part = wide[:, t * LANES : (t + 1) * LANES]
        if off:
            part = pltpu.roll(part, LANES - off, 1)
        if off + kc > LANES:
            after = pltpu.roll(wide[:, (t + 1) * LANES : (t + 2) * LANES], LANES - off, 1)
            part = jnp.where(lane < LANES - off, part, after)
        out_ref[c] = jnp.where(lane < kc, part, extra)


def first_gather_kernel(
    near_ref, r_ref, picked_ref, got_ref, coarse_ref, extended_ref, asked_ref, out_ref
):
    subs, cols, _ = got_ref.shape
    rows = r_ref.shape[2]
    slots = picked_ref.shape[0]
    write_share(rows, False, got_ref, coarse_ref, out_ref)
    near = near_ref[...]
    parts = []
    for j in range(slots):
        source = near[0, j]
        other = got_ref[jnp.maximum(source, 0), :, 0:rows].astype(jnp.float32)
        tiles = [twice(other[:, t * LANES : (t + 1) * LANES]) for t in range(rows // LANES)]
        index = jnp.broadcast_to(picked_ref[j], (2 * cols, LANES))
        part = pick_lanes(tiles, index)[:cols]
        parts.append(jnp.where(source >= 0, part, 0.0).astype(jnp.bfloat16))
    margin = jnp.concatenate(parts, axis=1)
    extended_ref[...] = extend(r_ref[:, 0, :], margin)
    lane = lanes_of((cols, LANES))
    kc = coarse_ref.shape[0] // out_ref.shape[0]
    wide = LANES // cols
    for i in range(subs // 2):
        pair = []
        for s in (2 * i, 2 * i + 1):
            got = got_ref[s, :, rows : rows + LANES].astype(jnp.float32)
            index = jnp.zeros((cols, LANES), jnp.float32)
            for k in range(cols):
                moved = pltpu.roll(
                    jnp.broadcast_to(got[k : k + 1], (cols, LANES)), (k * wide - kc) % LANES, 1
                )
                index = jnp.where((lane >= k * wide) & (lane < (k + 1) * wide), moved, index)
            pair.append(index)
        index = jnp.concatenate(pair, axis=0).astype(jnp.int32) + rows // 2
        asked_ref[i] = jnp.clip(index, 0, rows - 1)


def second_gather_kernel(
    near_ref, vector_ref, got_ref, coarse_ref, extended_ref, out_ref
):
    rows = vector_ref.shape[1]
    slots = (extended_ref.shape[1] - rows) // LANES
    write_share(2 * LANES, True, got_ref, coarse_ref, out_ref)
    margin = margin_from(got_ref, near_ref, slots, vector_ref.shape[0])
    extended_ref[...] = extend(vector_ref[...], margin)


def prolong(summed, extended_ref, inverse_ref, basis_ref):
    kc = basis_ref.shape[0]
    fine = lax.dot_general(
        extended_ref[...], inverse_ref[...], LAST, preferred_element_type=jnp.float32
    )
    return joined(fine) + lax.dot_general(
        summed[:, :kc], basis_ref[...], FIRST, precision=HIGH, preferred_element_type=jnp.float32
    )


def first_direction_kernel(shares_ref, extended_ref, inverse_ref, basis_ref, asked_ref, p_ref, out_ref):
    p = prolong(jnp.sum(shares_ref[...], axis=0), extended_ref, inverse_ref, basis_ref)
    p_ref[...] = p
    send_rows(p, asked_ref, out_ref)


def operate(near_ref, vector_ref, got_ref, own_ref, coupling_ref):
    slots = coupling_ref.shape[1] // LANES
    margin = margin_from(got_ref, near_ref, slots, vector_ref.shape[0])
    own = lax.dot_general(
        halves(vector_ref[...]), own_ref[...], LAST, preferred_element_type=jnp.float32
    )
    return joined(own) + lax.dot_general(margin, coupling_ref[...], LAST, preferred_element_type=jnp.float32)


def extend(vector, margin):
    return jnp.concatenate([halves(vector), jnp.concatenate([margin, jnp.zeros_like(margin)])], axis=1)


def row_sum(x):
    return jnp.sum(x, axis=1, keepdims=True)


def first_operate_kernel(
    near_ref, p_ref, got_ref, own_ref, coupling_ref, r_ref, basis_ref, asked_ref, q_ref, out_ref
):
    cols = r_ref.shape[0]
    kc = basis_ref.shape[0]
    q = operate(near_ref, p_ref, got_ref, own_ref, coupling_ref)
    q_ref[...] = q
    r = r_ref[:, 0, :]
    residual = lax.dot_general(
        q, basis_ref[...], LAST, precision=HIGH, preferred_element_type=jnp.float32
    )
    tail = jnp.concatenate([residual, jnp.zeros((cols, LANES - kc), jnp.float32)], axis=1)
    lane = lanes_of((cols, LANES))
    for i, inner in enumerate([row_sum(r * r), row_sum(q * r), row_sum(q * q)]):
        for k, term in enumerate(split3(inner)):
            tail = jnp.where(lane == kc + 3 * k + i, term, tail)
    send_rows(q, asked_ref, out_ref)
    half = cols // 2
    tail = tail[:half] + pltpu.roll(tail[half:], LANES // 2, 1)
    out_ref[:, :, 2 * LANES : 3 * LANES] = jnp.broadcast_to(
        tail.astype(jnp.bfloat16)[None], (out_ref.shape[0], half, LANES)
    )


def second_direction_kernel(
    all_rows, shares_ref, extended_ref, inverse_ref, basis_ref, asked_ref, r_ref, q_ref, p_ref,
    v1_ref, v2_ref, z1_ref, z2_ref, scalars_ref, out_ref,
):
    kc = basis_ref.shape[0]
    summed = jnp.sum(shares_ref[...], axis=0)
    p2 = prolong(summed, extended_ref, inverse_ref, basis_ref)
    rr, qr, qq = [summed[:, kc + i : kc + i + 1] / all_rows for i in range(3)]
    start = jnp.sqrt(rr + EPS)
    h11 = qr / start / start
    part = h11 / start
    left = qq / start / start - 2.0 * part * (qr / start) + part * part * rr
    h21 = jnp.sqrt(jnp.maximum(left, 0.0) + EPS)
    v1 = r_ref[:, 0, :] / start
    z1 = p_ref[...] / start
    v2 = (q_ref[...] / start - h11 * v1) / h21
    z2 = (p2 / start - h11 * z1) / h21
    v1_ref[...] = v1
    v2_ref[...] = v2
    z1_ref[...] = z1
    z2_ref[...] = z2
    lane = lanes_of(scalars_ref.shape)
    scalars_ref[...] = place(start, lane, 0) + place(h11, lane, 1) + place(h21, lane, 2)
    send_rows(z2, asked_ref, out_ref)


def second_operate_kernel(
    near_ref, z_ref, got_ref, own_ref, coupling_ref, v1_ref, v2_ref, w_ref, out_ref
):
    w = operate(near_ref, z_ref, got_ref, own_ref, coupling_ref)
    w_ref[...] = w
    v1 = v1_ref[...]
    v2 = v2_ref[...]
    cols = w.shape[0]
    lane = lanes_of((cols, LANES))
    col = lax.broadcasted_iota(jnp.int32, (cols, LANES), 0)
    pairs = [(w, v1), (w, v2), (w, w), (v1, v1), (v1, v2), (v2, v2)]
    inner = jnp.zeros((cols, LANES), jnp.float32)
    for i, (a, b) in enumerate(pairs):
        inner = jnp.where(lane == i * cols + col, row_sum(a * b), inner)
    out_ref[...] = jnp.broadcast_to(jnp.sum(inner, axis=0, keepdims=True)[None], out_ref.shape)


def between_kernel(got_ref, out_ref):
    out_ref[...] = jnp.broadcast_to(jnp.sum(got_ref[...], axis=0)[None], out_ref.shape)


def last_kernel(
    all_rows, got_ref, w_ref, v1_ref, v2_ref, z1_ref, z2_ref, scalars_ref, answer_ref, next_ref
):
    cols = w_ref.shape[0]
    lane = lanes_of((cols, LANES))
    col = lax.broadcasted_iota(jnp.int32, (cols, LANES), 0)
    inner = jnp.sum(got_ref[...], axis=0, keepdims=True) / all_rows
    inner = jnp.broadcast_to(inner, (cols, LANES))
    h12, h22, ww, g11, g12, g22 = [
        row_sum(jnp.where(lane == i * cols + col, inner, 0.0)) for i in range(6)
    ]
    start, h11, h21 = [scalars_ref[:, i : i + 1] for i in range(3)]
    left = (
        ww
        - 2.0 * (h12 * h12 + h22 * h22)
        + h12 * h12 * g11
        + 2.0 * h12 * h22 * g12
        + h22 * h22 * g22
    )
    h32 = jnp.sqrt(jnp.maximum(left, 0.0) + EPS)
    next_ref[:, 0, :] = (w_ref[...] - h12 * v1_ref[...] - h22 * v2_ref[...]) / h32
    weights = least_squares(start, [[h11, h21], [h12, h22, h32]])
    answer_ref[:, 0, :] = weights[0] * z1_ref[...] + weights[1] * z2_ref[...]


def call(kernel, outs, *args, name):
    vmem = pl.BlockSpec(memory_space=pltpu.VMEM)
    return pl.pallas_call(
        kernel,
        out_shape=outs,
        in_specs=[vmem] * len(args),
        out_specs=jax.tree.map(lambda _: vmem, outs),
        compiler_params=pltpu.CompilerParams(vmem_limit_bytes=VMEM_BYTES),
        name=name,
    )(*args)


def body(
    right_side,
    own_block,
    coupling,
    local_inverse,
    coarse_basis,
    coarse_inverse,
    neighbours,
    margin_rows,
    block_counts,
):
    cols, rows = right_side.shape[0], right_side.shape[3]
    r = right_side.reshape(cols, 1, rows)
    own = own_block[0, 0]
    couple = coupling[0, 0]
    inverse = local_inverse[0, 0]
    basis = coarse_basis[0, 0]
    coarse = coarse_inverse[0, :, 0, :]
    near = neighbours[0]
    picked = margin_rows.reshape(margin_rows.shape[2], 1, margin_rows.shape[3])
    live = block_counts
    subs, owners = lax.axis_size("sub"), lax.axis_size("crs")
    all_rows = rows * subs * owners
    f32, bf16 = jnp.float32, jnp.bfloat16

    def shape(*dims, dtype=f32):
        return jax.ShapeDtypeStruct(dims, dtype)

    vector = shape(cols, rows)
    tile = shape(cols, LANES)

    def over_sub(blocks):
        return lax.all_to_all(blocks, "sub", 0, 0, axis_index_groups=[order_of(subs)])

    def over_crs(blocks):
        return lax.all_to_all(blocks, "crs", 0, 0)

    held = [r, basis, picked]
    vmem = pl.BlockSpec(memory_space=pltpu.VMEM)
    sent, near, r, basis, picked = pl.pallas_call(
        first_send_kernel,
        out_shape=[shape(subs, cols, rows + LANES, dtype=bf16), shape(1, LANES, dtype=jnp.int32)]
        + [shape(*x.shape, dtype=x.dtype) for x in held],
        in_specs=[pl.BlockSpec(memory_space=pltpu.SMEM)]
        + [pl.BlockSpec(memory_space=pl.ANY)] * 4,
        out_specs=[vmem] * 5,
        scratch_shapes=[pltpu.VMEM(near.shape, jnp.int32), pltpu.SemaphoreType.DMA((8,))],
        compiler_params=pltpu.CompilerParams(vmem_limit_bytes=VMEM_BYTES),
        cost_estimate=pl.CostEstimate(
            flops=1 << 34, bytes_accessed=1 << 30, transcendentals=0
        ),
        name="first_send",
    )(live, *[pltpu.with_memory_space_constraint(x, pltpu.HBM) for x in (near, *held)])
    got = over_sub(sent)
    extended, asked, shares = call(
        first_gather_kernel,
        (
            shape(2 * cols, inverse.shape[1], dtype=bf16),
            shape(subs // 2, 2 * cols, LANES, dtype=jnp.int32),
            shape(owners, cols, LANES),
        ),
        near, r, picked, got, coarse, name="first_gather",
    )
    shares = over_crs(shares)
    p1, sent = call(
        first_direction_kernel, (vector, shape(subs, cols, LANES, dtype=bf16)),
        shares, extended, inverse, basis, asked, name="first_direction",
    )
    got = over_sub(sent)
    q1, sent = call(
        first_operate_kernel, (vector, shape(subs, cols // 2, 3 * LANES, dtype=bf16)),
        near, p1, got, own, couple, r, basis, asked, name="first_operate",
    )
    got = over_sub(sent)
    extended, shares = call(
        second_gather_kernel,
        (shape(2 * cols, inverse.shape[1], dtype=bf16), shape(owners, cols, LANES)),
        near, q1, got, coarse, name="second_gather",
    )
    shares = over_crs(shares)

    def second_direction(*refs):
        second_direction_kernel(float(all_rows), *refs)

    v1, v2, z1, z2, scalars, sent = call(
        second_direction,
        (vector, vector, vector, vector, tile, shape(subs, cols, LANES, dtype=bf16)),
        shares, extended, inverse, basis, asked, r, q1, p1, name="second_direction",
    )
    got = over_sub(sent)
    w, sent = call(
        second_operate_kernel, (vector, shape(owners, 1, LANES)),
        near, z2, got, own, couple, v1, v2, name="second_operate",
    )
    got = over_crs(sent)
    sent = call(between_kernel, shape(subs, 1, LANES), got, name="between")
    got = over_sub(sent).reshape(subs, LANES)

    def last(*refs):
        last_kernel(float(all_rows), *refs)

    answer, following = call(
        last, (shape(cols, 1, rows), shape(cols, 1, rows)),
        got, w, v1, v2, z1, z2, scalars, name="last",
    )
    out = (cols, 1, 1, rows)
    return answer.reshape(out), following.reshape(out)


def solution(mesh):
    in_specs = (
        P(None, "sub", "crs", None),
        P("sub", "crs", None, None),
        P("sub", "crs", None, None),
        P("sub", "crs", None, None),
        P("sub", "crs", None, None),
        P("sub", None, "crs", None),
        P("sub", "crs", None),
        P("sub", "crs", None, None),
        P("sub", "crs"),
    )
    out_specs = (P(None, "sub", "crs", None), P(None, "sub", "crs", None))
    return jax.shard_map(body, mesh=mesh, in_specs=in_specs, out_specs=out_specs, check_vma=False)
```

```python
import jax
import jax.numpy as jnp
from jax import lax
from jax.experimental import pallas as pl
from jax.experimental.pallas import tpu as pltpu
from jax.sharding import PartitionSpec as P

EPS = 1e-06
HIGH = lax.Precision.HIGH
LAST = (((1,), (1,)), ((), ()))
FIRST = (((1,), (0,)), ((), ()))
LANES = 128
VMEM_BYTES = 16 << 20
PLANES = 16
NEAR = 4
def order_of(subs):
    planes = [i // (2 * NEAR) + i // NEAR % 2 * (PLANES // 2) for i in range(subs)]
    return [plane * NEAR + i % NEAR for i, plane in enumerate(planes)]


def place_of(sub):
    plane = sub >> 2
    return (((plane & 7) << 1) | (plane >> 3)) * NEAR + (sub & (NEAR - 1))


def least_squares(start_norm, columns):
    cosines = []
    sine_terms = []
    triangle = []
    target = [start_norm] + [jnp.zeros_like(start_norm) for j in range(len(columns))]
    for j, column in enumerate(columns):
        column = list(column)
        for i in range(j):
            upper_value = cosines[i] * column[i] + sine_terms[i] * column[i + 1]
            column[i + 1] = -sine_terms[i] * column[i] + cosines[i] * column[i + 1]
            column[i] = upper_value
        radius = jnp.sqrt(column[j] * column[j] + column[j + 1] * column[j + 1])
        cosine = column[j] / radius
        sine_part = column[j + 1] / radius
        column[j] = radius
        target[j + 1] = -sine_part * target[j]
        target[j] = cosine * target[j]
        cosines.append(cosine)
        sine_terms.append(sine_part)
        triangle.append(column[: j + 1])
    weights = [None] * len(columns)
    for j in reversed(range(len(columns))):
        running = target[j]
        for k in range(j + 1, len(columns)):
            running = running - triangle[k][j] * weights[k]
        weights[j] = running / triangle[j][j]
    return weights


def split3(x):
    hi = x.astype(jnp.bfloat16).astype(jnp.float32)
    rest = x - hi
    mid = rest.astype(jnp.bfloat16).astype(jnp.float32)
    return hi, mid, rest - mid


def halves(x):
    hi = x.astype(jnp.bfloat16)
    return jnp.concatenate([hi, (x - hi.astype(jnp.float32)).astype(jnp.bfloat16)], axis=0)


def joined(x):
    rows = x.shape[0] // 2
    return x[:rows] + x[rows:]


def place(column, lane, at):
    return jnp.where(lane == at, column, 0.0)


def pick_lanes(tiles, index):
    low = index & (LANES - 1)
    high = index >> 7
    out = jnp.take_along_axis(tiles[0], low, axis=1, mode="promise_in_bounds")
    for t in range(1, len(tiles)):
        other = jnp.take_along_axis(tiles[t], low, axis=1, mode="promise_in_bounds")
        out = jnp.where(high == t, other, out)
    return out


def lanes_of(shape):
    return lax.broadcasted_iota(jnp.int32, shape, 1)


def twice(x):
    return jnp.concatenate([x, x], axis=0)


def send_rows(vector, asked_ref, out_ref):
    tiles = [twice(vector[:, t * LANES : (t + 1) * LANES]) for t in range(vector.shape[1] // LANES)]
    cols = vector.shape[0]
    height = out_ref.shape[1]
    for i in range(asked_ref.shape[0]):
        chosen = pick_lanes(tiles, asked_ref[i])
        for at in range(0, 2 * cols, height):
            part, t = divmod(at, cols)
            lanes = pl.ds(t // height * LANES, LANES)
            out_ref[2 * i + part, :, lanes] = chosen[at : at + height].astype(jnp.bfloat16)


def margin_from(got_ref, near_ref, slots, cols):
    near = near_ref[...]
    parts = []
    for j in range(slots):
        source = near[0, j]
        part = got_ref[jnp.maximum(source, 0)]
        parts.append(jnp.where(source >= 0, part, jnp.zeros_like(part)).astype(jnp.float32))
    width = cols // got_ref.shape[1]
    columns = [
        jnp.concatenate([part[:, t * LANES : (t + 1) * LANES] for part in parts], axis=1)
        for t in range(width)
    ]
    return jnp.concatenate(columns, axis=0).astype(jnp.bfloat16)


def first_send_kernel(
    live, near_hbm, r_hbm, basis_hbm, picked_hbm,
    out_ref, table_ref, r_ref, basis_ref, picked, near_ref, sems,
):
    pairs = [
        (r_hbm, r_ref),
        (basis_hbm, basis_ref),
        (picked_hbm, picked),
        (near_hbm, near_ref),
    ]
    moves = [
        pltpu.make_async_copy(source, target, sems.at[i])
        for i, (source, target) in enumerate(pairs)
    ]
    for move in moves:
        move.start()
    for move in moves[:4]:
        move.wait()
    subs, cols, _ = out_ref.shape
    rows = r_ref.shape[2]
    kc = basis_ref.shape[0]
    r = r_ref[:, 0, :]
    low = r.astype(jnp.bfloat16)
    residual = lax.dot_general(
        r, basis_ref[...], LAST, precision=HIGH, preferred_element_type=jnp.float32
    )
    tail = jnp.concatenate([residual, jnp.zeros((cols, LANES - kc), jnp.float32)], axis=1)
    whole = jnp.concatenate([low, tail.astype(jnp.bfloat16)], axis=1)
    out_ref[...] = jnp.broadcast_to(whole[None], out_ref.shape)
    lane = lanes_of((cols, LANES))
    sub = lax.broadcasted_iota(jnp.int32, (cols, LANES), 0)
    wide = LANES // cols
    slots = picked.shape[0]
    near = place_of(near_ref[...])
    table = jnp.concatenate([near, jnp.zeros((1, LANES - slots), jnp.int32)], axis=1)
    table_ref[...] = jnp.where(lanes_of((1, LANES)) < live[0, 0], table, -1)
    for j in reversed(range(slots)):
        wanted = (picked[j] - rows // 2).astype(jnp.float32)
        wanted = jnp.broadcast_to(wanted, (cols, LANES))
        packed = jnp.zeros((cols, LANES), jnp.float32)
        for i in range(cols):
            moved = pltpu.roll(wanted, (kc - i * wide) % LANES, 1)
            packed = jnp.where(sub == i, moved, packed)
        packed = jnp.where((lane >= kc) & (lane < kc + wide), packed, tail)
        out_ref[near[0, j], :, rows : rows + LANES] = packed.astype(jnp.bfloat16)
    for move in moves[4:]:
        move.wait()


def write_share(at, with_terms, got_ref, coarse_ref, out_ref):
    subs, height, _ = got_ref.shape
    owners, cols, _ = out_ref.shape
    kc = coarse_ref.shape[0] // owners
    lane = lanes_of((height, LANES))
    width = cols // height
    zero = jnp.zeros((height, LANES), jnp.float32)
    tiles = [[zero] * (subs * kc // LANES) for _ in range(width)]
    terms = zero
    for block, s in enumerate(order_of(subs)):
        got = got_ref[block, :, at : at + LANES].astype(jnp.float32)
        if with_terms:
            terms = terms + got
        t, off = divmod(s * kc, LANES)
        for part in range(width):
            mine = tiles[part]
            turn = (off - part * (LANES // width)) % LANES
            moved = pltpu.roll(got, turn, 1) if turn else got
            if off + kc <= LANES:
                mine[t] = jnp.where((lane >= off) & (lane < off + kc), moved, mine[t])
            else:
                mine[t] = jnp.where(lane >= off, moved, mine[t])
                mine[t + 1] = jnp.where(lane < off + kc - LANES, moved, mine[t + 1])
    residuals = [jnp.concatenate(mine, axis=1) for mine in tiles]
    residuals = jnp.concatenate(residuals, axis=0).astype(jnp.bfloat16)
    if width > 1:
        terms = jnp.concatenate([terms, pltpu.roll(terms, LANES // width, 1)], axis=0)
    lane = lanes_of((cols, LANES))
    share = lax.dot_general(
        residuals, coarse_ref[...], LAST, preferred_element_type=jnp.float32
    )
    extra = jnp.zeros((cols, LANES), jnp.float32)
    if with_terms:
        summed = terms + pltpu.roll(terms, LANES - 3, 1) + pltpu.roll(terms, LANES - 6, 1)
        extra = jnp.where((lane >= kc) & (lane < kc + 3), summed, 0.0)
    wide = jnp.concatenate(
        [share, jnp.zeros((cols, -share.shape[1] % LANES), jnp.float32)], axis=1
    )
    for c in range(owners):
        t, off = divmod(c * kc, LANES)
        part = wide[:, t * LANES : (t + 1) * LANES]
        if off:
            part = pltpu.roll(part, LANES - off, 1)
        if off + kc > LANES:
            after = pltpu.roll(wide[:, (t + 1) * LANES : (t + 2) * LANES], LANES - off, 1)
            part = jnp.where(lane < LANES - off, part, after)
        out_ref[c] = jnp.where(lane < kc, part, extra)


def first_gather_kernel(
    near_ref, r_ref, picked_ref, got_ref, coarse_ref, extended_ref, asked_ref, out_ref
):
    subs, cols, _ = got_ref.shape
    rows = r_ref.shape[2]
    slots = picked_ref.shape[0]
    write_share(rows, False, got_ref, coarse_ref, out_ref)
    near = near_ref[...]
    parts = []
    for j in range(slots):
        source = near[0, j]
        other = got_ref[jnp.maximum(source, 0), :, 0:rows].astype(jnp.float32)
        tiles = [twice(other[:, t * LANES : (t + 1) * LANES]) for t in range(rows // LANES)]
        index = jnp.broadcast_to(picked_ref[j], (2 * cols, LANES))
        part = pick_lanes(tiles, index)[:cols]
        parts.append(jnp.where(source >= 0, part, 0.0).astype(jnp.bfloat16))
    margin = jnp.concatenate(parts, axis=1)
    extended_ref[...] = extend(r_ref[:, 0, :], margin)
    lane = lanes_of((cols, LANES))
    kc = coarse_ref.shape[0] // out_ref.shape[0]
    wide = LANES // cols
    for i in range(subs // 2):
        pair = []
        for s in (2 * i, 2 * i + 1):
            got = got_ref[s, :, rows : rows + LANES].astype(jnp.float32)
            index = jnp.zeros((cols, LANES), jnp.float32)
            for k in range(cols):
                moved = pltpu.roll(
                    jnp.broadcast_to(got[k : k + 1], (cols, LANES)), (k * wide - kc) % LANES, 1
                )
                index = jnp.where((lane >= k * wide) & (lane < (k + 1) * wide), moved, index)
            pair.append(index)
        index = jnp.concatenate(pair, axis=0).astype(jnp.int32) + rows // 2
        asked_ref[i] = jnp.clip(index, 0, rows - 1)


def second_gather_kernel(
    near_ref, vector_ref, got_ref, coarse_ref, extended_ref, out_ref
):
    rows = vector_ref.shape[1]
    slots = (extended_ref.shape[1] - rows) // LANES
    write_share(2 * LANES, True, got_ref, coarse_ref, out_ref)
    margin = margin_from(got_ref, near_ref, slots, vector_ref.shape[0])
    extended_ref[...] = extend(vector_ref[...], margin)


def prolong(summed, extended_ref, inverse_ref, basis_ref):
    kc = basis_ref.shape[0]
    fine = lax.dot_general(
        extended_ref[...], inverse_ref[...], LAST, preferred_element_type=jnp.float32
    )
    return joined(fine) + lax.dot_general(
        summed[:, :kc], basis_ref[...], FIRST, precision=HIGH, preferred_element_type=jnp.float32
    )


def first_direction_kernel(shares_ref, extended_ref, inverse_ref, basis_ref, asked_ref, p_ref, out_ref):
    p = prolong(jnp.sum(shares_ref[...], axis=0), extended_ref, inverse_ref, basis_ref)
    p_ref[...] = p
    send_rows(p, asked_ref, out_ref)


def operate(near_ref, vector_ref, got_ref, own_ref, coupling_ref):
    slots = coupling_ref.shape[1] // LANES
    margin = margin_from(got_ref, near_ref, slots, vector_ref.shape[0])
    own = lax.dot_general(
        halves(vector_ref[...]), own_ref[...], LAST, preferred_element_type=jnp.float32
    )
    return joined(own) + lax.dot_general(margin, coupling_ref[...], LAST, preferred_element_type=jnp.float32)


def extend(vector, margin):
    return jnp.concatenate([halves(vector), jnp.concatenate([margin, jnp.zeros_like(margin)])], axis=1)


def row_sum(x):
    return jnp.sum(x, axis=1, keepdims=True)


def first_operate_kernel(
    near_ref, p_ref, got_ref, own_ref, coupling_ref, r_ref, basis_ref, asked_ref, q_ref, out_ref
):
    cols = r_ref.shape[0]
    kc = basis_ref.shape[0]
    q = operate(near_ref, p_ref, got_ref, own_ref, coupling_ref)
    q_ref[...] = q
    r = r_ref[:, 0, :]
    residual = lax.dot_general(
        q, basis_ref[...], LAST, precision=HIGH, preferred_element_type=jnp.float32
    )
    tail = jnp.concatenate([residual, jnp.zeros((cols, LANES - kc), jnp.float32)], axis=1)
    lane = lanes_of((cols, LANES))
    for i, inner in enumerate([row_sum(r * r), row_sum(q * r), row_sum(q * q)]):
        for k, term in enumerate(split3(inner)):
            tail = jnp.where(lane == kc + 3 * k + i, term, tail)
    send_rows(q, asked_ref, out_ref)
    half = cols // 2
    tail = tail[:half] + pltpu.roll(tail[half:], LANES // 2, 1)
    out_ref[:, :, 2 * LANES : 3 * LANES] = jnp.broadcast_to(
        tail.astype(jnp.bfloat16)[None], (out_ref.shape[0], half, LANES)
    )


def second_direction_kernel(
    all_rows, shares_ref, extended_ref, inverse_ref, basis_ref, asked_ref, r_ref, q_ref, p_ref,
    v1_ref, v2_ref, z1_ref, z2_ref, scalars_ref, out_ref,
):
    kc = basis_ref.shape[0]
    summed = jnp.sum(shares_ref[...], axis=0)
    p2 = prolong(summed, extended_ref, inverse_ref, basis_ref)
    rr, qr, qq = [summed[:, kc + i : kc + i + 1] / all_rows for i in range(3)]
    start = jnp.sqrt(rr + EPS)
    h11 = qr / start / start
    part = h11 / start
    left = qq / start / start - 2.0 * part * (qr / start) + part * part * rr
    h21 = jnp.sqrt(jnp.maximum(left, 0.0) + EPS)
    v1 = r_ref[:, 0, :] / start
    z1 = p_ref[...] / start
    v2 = (q_ref[...] / start - h11 * v1) / h21
    z2 = (p2 / start - h11 * z1) / h21
    v1_ref[...] = v1
    v2_ref[...] = v2
    z1_ref[...] = z1
    z2_ref[...] = z2
    lane = lanes_of(scalars_ref.shape)
    scalars_ref[...] = place(start, lane, 0) + place(h11, lane, 1) + place(h21, lane, 2)
    send_rows(z2, asked_ref, out_ref)


def second_operate_kernel(
    near_ref, z_ref, got_ref, own_ref, coupling_ref, v1_ref, v2_ref, w_ref, out_ref
):
    w = operate(near_ref, z_ref, got_ref, own_ref, coupling_ref)
    w_ref[...] = w
    v1 = v1_ref[...]
    v2 = v2_ref[...]
    cols = w.shape[0]
    lane = lanes_of((cols, LANES))
    col = lax.broadcasted_iota(jnp.int32, (cols, LANES), 0)
    pairs = [(w, v1), (w, v2), (w, w), (v1, v1), (v1, v2), (v2, v2)]
    inner = jnp.zeros((cols, LANES), jnp.float32)
    for i, (a, b) in enumerate(pairs):
        inner = jnp.where(lane == i * cols + col, row_sum(a * b), inner)
    out_ref[...] = jnp.broadcast_to(jnp.sum(inner, axis=0, keepdims=True)[None], out_ref.shape)


def between_kernel(got_ref, out_ref):
    out_ref[...] = jnp.broadcast_to(jnp.sum(got_ref[...], axis=0)[None], out_ref.shape)


def last_kernel(
    all_rows, got_ref, w_ref, v1_ref, v2_ref, z1_ref, z2_ref, scalars_ref, answer_ref, next_ref
):
    cols = w_ref.shape[0]
    lane = lanes_of((cols, LANES))
    col = lax.broadcasted_iota(jnp.int32, (cols, LANES), 0)
    inner = jnp.sum(got_ref[...], axis=0, keepdims=True) / all_rows
    inner = jnp.broadcast_to(inner, (cols, LANES))
    h12, h22, ww, g11, g12, g22 = [
        row_sum(jnp.where(lane == i * cols + col, inner, 0.0)) for i in range(6)
    ]
    start, h11, h21 = [scalars_ref[:, i : i + 1] for i in range(3)]
    left = (
        ww
        - 2.0 * (h12 * h12 + h22 * h22)
        + h12 * h12 * g11
        + 2.0 * h12 * h22 * g12
        + h22 * h22 * g22
    )
    h32 = jnp.sqrt(jnp.maximum(left, 0.0) + EPS)
    next_ref[:, 0, :] = (w_ref[...] - h12 * v1_ref[...] - h22 * v2_ref[...]) / h32
    weights = least_squares(start, [[h11, h21], [h12, h22, h32]])
    answer_ref[:, 0, :] = weights[0] * z1_ref[...] + weights[1] * z2_ref[...]


def call(kernel, outs, *args, name):
    vmem = pl.BlockSpec(memory_space=pltpu.VMEM)
    return pl.pallas_call(
        kernel,
        out_shape=outs,
        in_specs=[vmem] * len(args),
        out_specs=jax.tree.map(lambda _: vmem, outs),
        compiler_params=pltpu.CompilerParams(vmem_limit_bytes=VMEM_BYTES),
        name=name,
    )(*args)


def body(
    right_side,
    own_block,
    coupling,
    local_inverse,
    coarse_basis,
    coarse_inverse,
    neighbours,
    margin_rows,
    block_counts,
):
    cols, rows = right_side.shape[0], right_side.shape[3]
    r = right_side.reshape(cols, 1, rows)
    own = own_block[0, 0]
    couple = coupling[0, 0]
    inverse = local_inverse[0, 0]
    basis = coarse_basis[0, 0]
    coarse = coarse_inverse[0, :, 0, :]
    near = neighbours[0]
    picked = margin_rows.reshape(margin_rows.shape[2], 1, margin_rows.shape[3])
    live = block_counts
    subs, owners = lax.axis_size("sub"), lax.axis_size("crs")
    all_rows = rows * subs * owners
    f32, bf16 = jnp.float32, jnp.bfloat16

    def shape(*dims, dtype=f32):
        return jax.ShapeDtypeStruct(dims, dtype)

    vector = shape(cols, rows)
    tile = shape(cols, LANES)

    def over_sub(blocks):
        return lax.all_to_all(blocks, "sub", 0, 0, axis_index_groups=[order_of(subs)])

    def over_crs(blocks):
        return lax.all_to_all(blocks, "crs", 0, 0)

    held = [r, basis, picked]
    vmem = pl.BlockSpec(memory_space=pltpu.VMEM)
    sent, near, r, basis, picked = pl.pallas_call(
        first_send_kernel,
        out_shape=[shape(subs, cols, rows + LANES, dtype=bf16), shape(1, LANES, dtype=jnp.int32)]
        + [shape(*x.shape, dtype=x.dtype) for x in held],
        in_specs=[pl.BlockSpec(memory_space=pltpu.SMEM)]
        + [pl.BlockSpec(memory_space=pl.ANY)] * 4,
        out_specs=[vmem] * 5,
        scratch_shapes=[pltpu.VMEM(near.shape, jnp.int32), pltpu.SemaphoreType.DMA((8,))],
        compiler_params=pltpu.CompilerParams(vmem_limit_bytes=VMEM_BYTES),
        cost_estimate=pl.CostEstimate(
            flops=1 << 34, bytes_accessed=1 << 30, transcendentals=0
        ),
        name="first_send",
    )(live, *[pltpu.with_memory_space_constraint(x, pltpu.HBM) for x in (near, *held)])
    got = over_sub(sent)
    extended, asked, shares = call(
        first_gather_kernel,
        (
            shape(2 * cols, inverse.shape[1], dtype=bf16),
            shape(subs // 2, 2 * cols, LANES, dtype=jnp.int32),
            shape(owners, cols, LANES),
        ),
        near, r, picked, got, coarse, name="first_gather",
    )
    shares = over_crs(shares)
    p1, sent = call(
        first_direction_kernel, (vector, shape(subs, cols, LANES, dtype=bf16)),
        shares, extended, inverse, basis, asked, name="first_direction",
    )
    got = over_sub(sent)
    q1, sent = call(
        first_operate_kernel, (vector, shape(subs, cols // 2, 3 * LANES, dtype=bf16)),
        near, p1, got, own, couple, r, basis, asked, name="first_operate",
    )
    got = over_sub(sent)
    extended, shares = call(
        second_gather_kernel,
        (shape(2 * cols, inverse.shape[1], dtype=bf16), shape(owners, cols, LANES)),
        near, q1, got, coarse, name="second_gather",
    )
    shares = over_crs(shares)

    def second_direction(*refs):
        second_direction_kernel(float(all_rows), *refs)

    v1, v2, z1, z2, scalars, sent = call(
        second_direction,
        (vector, vector, vector, vector, tile, shape(subs, cols, LANES, dtype=bf16)),
        shares, extended, inverse, basis, asked, r, q1, p1, name="second_direction",
    )
    got = over_sub(sent)
    w, sent = call(
        second_operate_kernel, (vector, shape(owners, 1, LANES)),
        near, z2, got, own, couple, v1, v2, name="second_operate",
    )
    got = over_crs(sent)
    sent = call(between_kernel, shape(subs, 1, LANES), got, name="between")
    got = over_sub(sent).reshape(subs, LANES)

    def last(*refs):
        last_kernel(float(all_rows), *refs)

    answer, following = call(
        last, (shape(cols, 1, rows), shape(cols, 1, rows)),
        got, w, v1, v2, z1, z2, scalars, name="last",
    )
    out = (cols, 1, 1, rows)
    return answer.reshape(out), following.reshape(out)


def solution(mesh):
    in_specs = (
        P(None, "sub", "crs", None),
        P("sub", "crs", None, None),
        P("sub", "crs", None, None),
        P("sub", "crs", None, None),
        P("sub", "crs", None, None),
        P("sub", None, "crs", None),
        P("sub", "crs", None),
        P("sub", "crs", None, None),
        P("sub", "crs"),
    )
    out_specs = (P(None, "sub", "crs", None), P(None, "sub", "crs", None))
    return jax.shard_map(body, mesh=mesh, in_specs=in_specs, out_specs=out_specs, check_vma=False)
```

```python
import jax
import jax.numpy as jnp
from jax import lax
from jax.experimental import pallas as pl
from jax.experimental.pallas import tpu as pltpu
from jax.sharding import PartitionSpec as P

EPS = 1e-06
HIGH = lax.Precision.HIGH
LAST = (((1,), (1,)), ((), ()))
FIRST = (((1,), (0,)), ((), ()))
LANES = 128
VMEM_BYTES = 16 << 20
PLANES = 16
NEAR = 4
def order_of(subs):
    planes = [i // (2 * NEAR) + i % 2 * (PLANES // 2) for i in range(subs)]
    return [plane * NEAR + i // 2 % NEAR for i, plane in enumerate(planes)]


def place_of(sub):
    plane = sub >> 2
    return (plane & 7) * (2 * NEAR) + (sub & (NEAR - 1)) * 2 + (plane >> 3)


def least_squares(start_norm, columns):
    cosines = []
    sine_terms = []
    triangle = []
    target = [start_norm] + [jnp.zeros_like(start_norm) for j in range(len(columns))]
    for j, column in enumerate(columns):
        column = list(column)
        for i in range(j):
            upper_value = cosines[i] * column[i] + sine_terms[i] * column[i + 1]
            column[i + 1] = -sine_terms[i] * column[i] + cosines[i] * column[i + 1]
            column[i] = upper_value
        radius = jnp.sqrt(column[j] * column[j] + column[j + 1] * column[j + 1])
        cosine = column[j] / radius
        sine_part = column[j + 1] / radius
        column[j] = radius
        target[j + 1] = -sine_part * target[j]
        target[j] = cosine * target[j]
        cosines.append(cosine)
        sine_terms.append(sine_part)
        triangle.append(column[: j + 1])
    weights = [None] * len(columns)
    for j in reversed(range(len(columns))):
        running = target[j]
        for k in range(j + 1, len(columns)):
            running = running - triangle[k][j] * weights[k]
        weights[j] = running / triangle[j][j]
    return weights


def split3(x):
    hi = x.astype(jnp.bfloat16).astype(jnp.float32)
    rest = x - hi
    mid = rest.astype(jnp.bfloat16).astype(jnp.float32)
    return hi, mid, rest - mid


def halves(x):
    hi = x.astype(jnp.bfloat16)
    return jnp.concatenate([hi, (x - hi.astype(jnp.float32)).astype(jnp.bfloat16)], axis=0)


def joined(x):
    rows = x.shape[0] // 2
    return x[:rows] + x[rows:]


def place(column, lane, at):
    return jnp.where(lane == at, column, 0.0)


def pick_lanes(tiles, index):
    low = index & (LANES - 1)
    high = index >> 7
    out = jnp.take_along_axis(tiles[0], low, axis=1, mode="promise_in_bounds")
    for t in range(1, len(tiles)):
        other = jnp.take_along_axis(tiles[t], low, axis=1, mode="promise_in_bounds")
        out = jnp.where(high == t, other, out)
    return out


def lanes_of(shape):
    return lax.broadcasted_iota(jnp.int32, shape, 1)


def twice(x):
    return jnp.concatenate([x, x], axis=0)


def send_rows(vector, asked_ref, out_ref):
    tiles = [twice(vector[:, t * LANES : (t + 1) * LANES]) for t in range(vector.shape[1] // LANES)]
    cols = vector.shape[0]
    height = out_ref.shape[1]
    for i in range(asked_ref.shape[0]):
        chosen = pick_lanes(tiles, asked_ref[i])
        for at in range(0, 2 * cols, height):
            part, t = divmod(at, cols)
            lanes = pl.ds(t // height * LANES, LANES)
            out_ref[2 * i + part, :, lanes] = chosen[at : at + height].astype(jnp.bfloat16)


def margin_from(got_ref, near_ref, slots, cols):
    near = near_ref[...]
    parts = []
    for j in range(slots):
        source = near[0, j]
        part = got_ref[jnp.maximum(source, 0)]
        parts.append(jnp.where(source >= 0, part, jnp.zeros_like(part)).astype(jnp.float32))
    width = cols // got_ref.shape[1]
    columns = [
        jnp.concatenate([part[:, t * LANES : (t + 1) * LANES] for part in parts], axis=1)
        for t in range(width)
    ]
    return jnp.concatenate(columns, axis=0).astype(jnp.bfloat16)


def first_send_kernel(
    live, near_hbm, r_hbm, basis_hbm, picked_hbm,
    out_ref, table_ref, r_ref, basis_ref, picked, near_ref, sems,
):
    pairs = [
        (r_hbm, r_ref),
        (basis_hbm, basis_ref),
        (picked_hbm, picked),
        (near_hbm, near_ref),
    ]
    moves = [
        pltpu.make_async_copy(source, target, sems.at[i])
        for i, (source, target) in enumerate(pairs)
    ]
    for move in moves:
        move.start()
    for move in moves[:4]:
        move.wait()
    subs, cols, _ = out_ref.shape
    rows = r_ref.shape[2]
    kc = basis_ref.shape[0]
    r = r_ref[:, 0, :]
    low = r.astype(jnp.bfloat16)
    residual = lax.dot_general(
        r, basis_ref[...], LAST, precision=HIGH, preferred_element_type=jnp.float32
    )
    tail = jnp.concatenate([residual, jnp.zeros((cols, LANES - kc), jnp.float32)], axis=1)
    whole = jnp.concatenate([low, tail.astype(jnp.bfloat16)], axis=1)
    out_ref[...] = jnp.broadcast_to(whole[None], out_ref.shape)
    lane = lanes_of((cols, LANES))
    sub = lax.broadcasted_iota(jnp.int32, (cols, LANES), 0)
    wide = LANES // cols
    slots = picked.shape[0]
    near = place_of(near_ref[...])
    table = jnp.concatenate([near, jnp.zeros((1, LANES - slots), jnp.int32)], axis=1)
    table_ref[...] = jnp.where(lanes_of((1, LANES)) < live[0, 0], table, -1)
    for j in reversed(range(slots)):
        wanted = (picked[j] - rows // 2).astype(jnp.float32)
        wanted = jnp.broadcast_to(wanted, (cols, LANES))
        packed = jnp.zeros((cols, LANES), jnp.float32)
        for i in range(cols):
            moved = pltpu.roll(wanted, (kc - i * wide) % LANES, 1)
            packed = jnp.where(sub == i, moved, packed)
        packed = jnp.where((lane >= kc) & (lane < kc + wide), packed, tail)
        out_ref[near[0, j], :, rows : rows + LANES] = packed.astype(jnp.bfloat16)
    for move in moves[4:]:
        move.wait()


def write_share(at, with_terms, got_ref, coarse_ref, out_ref):
    subs, height, _ = got_ref.shape
    owners, cols, _ = out_ref.shape
    kc = coarse_ref.shape[0] // owners
    lane = lanes_of((height, LANES))
    width = cols // height
    zero = jnp.zeros((height, LANES), jnp.float32)
    tiles = [[zero] * (subs * kc // LANES) for _ in range(width)]
    terms = zero
    for block, s in enumerate(order_of(subs)):
        got = got_ref[block, :, at : at + LANES].astype(jnp.float32)
        if with_terms:
            terms = terms + got
        t, off = divmod(s * kc, LANES)
        for part in range(width):
            mine = tiles[part]
            turn = (off - part * (LANES // width)) % LANES
            moved = pltpu.roll(got, turn, 1) if turn else got
            if off + kc <= LANES:
                mine[t] = jnp.where((lane >= off) & (lane < off + kc), moved, mine[t])
            else:
                mine[t] = jnp.where(lane >= off, moved, mine[t])
                mine[t + 1] = jnp.where(lane < off + kc - LANES, moved, mine[t + 1])
    residuals = [jnp.concatenate(mine, axis=1) for mine in tiles]
    residuals = jnp.concatenate(residuals, axis=0).astype(jnp.bfloat16)
    if width > 1:
        terms = jnp.concatenate([terms, pltpu.roll(terms, LANES // width, 1)], axis=0)
    lane = lanes_of((cols, LANES))
    share = lax.dot_general(
        residuals, coarse_ref[...], LAST, preferred_element_type=jnp.float32
    )
    extra = jnp.zeros((cols, LANES), jnp.float32)
    if with_terms:
        summed = terms + pltpu.roll(terms, LANES - 3, 1) + pltpu.roll(terms, LANES - 6, 1)
        extra = jnp.where((lane >= kc) & (lane < kc + 3), summed, 0.0)
    wide = jnp.concatenate(
        [share, jnp.zeros((cols, -share.shape[1] % LANES), jnp.float32)], axis=1
    )
    for c in range(owners):
        t, off = divmod(c * kc, LANES)
        part = wide[:, t * LANES : (t + 1) * LANES]
        if off:
            part = pltpu.roll(part, LANES - off, 1)
        if off + kc > LANES:
            after = pltpu.roll(wide[:, (t + 1) * LANES : (t + 2) * LANES], LANES - off, 1)
            part = jnp.where(lane < LANES - off, part, after)
        out_ref[c] = jnp.where(lane < kc, part, extra)


def first_gather_kernel(
    near_ref, r_ref, picked_ref, got_ref, coarse_ref, extended_ref, asked_ref, out_ref
):
    subs, cols, _ = got_ref.shape
    rows = r_ref.shape[2]
    slots = picked_ref.shape[0]
    write_share(rows, False, got_ref, coarse_ref, out_ref)
    near = near_ref[...]
    parts = []
    for j in range(slots):
        source = near[0, j]
        other = got_ref[jnp.maximum(source, 0), :, 0:rows].astype(jnp.float32)
        tiles = [twice(other[:, t * LANES : (t + 1) * LANES]) for t in range(rows // LANES)]
        index = jnp.broadcast_to(picked_ref[j], (2 * cols, LANES))
        part = pick_lanes(tiles, index)[:cols]
        parts.append(jnp.where(source >= 0, part, 0.0).astype(jnp.bfloat16))
    margin = jnp.concatenate(parts, axis=1)
    extended_ref[...] = extend(r_ref[:, 0, :], margin)
    lane = lanes_of((cols, LANES))
    kc = coarse_ref.shape[0] // out_ref.shape[0]
    wide = LANES // cols
    for i in range(subs // 2):
        pair = []
        for s in (2 * i, 2 * i + 1):
            got = got_ref[s, :, rows : rows + LANES].astype(jnp.float32)
            index = jnp.zeros((cols, LANES), jnp.float32)
            for k in range(cols):
                moved = pltpu.roll(
                    jnp.broadcast_to(got[k : k + 1], (cols, LANES)), (k * wide - kc) % LANES, 1
                )
                index = jnp.where((lane >= k * wide) & (lane < (k + 1) * wide), moved, index)
            pair.append(index)
        index = jnp.concatenate(pair, axis=0).astype(jnp.int32) + rows // 2
        asked_ref[i] = jnp.clip(index, 0, rows - 1)


def second_gather_kernel(
    near_ref, vector_ref, got_ref, coarse_ref, extended_ref, out_ref
):
    rows = vector_ref.shape[1]
    slots = (extended_ref.shape[1] - rows) // LANES
    write_share(2 * LANES, True, got_ref, coarse_ref, out_ref)
    margin = margin_from(got_ref, near_ref, slots, vector_ref.shape[0])
    extended_ref[...] = extend(vector_ref[...], margin)


def prolong(summed, extended_ref, inverse_ref, basis_ref):
    kc = basis_ref.shape[0]
    fine = lax.dot_general(
        extended_ref[...], inverse_ref[...], LAST, preferred_element_type=jnp.float32
    )
    return joined(fine) + lax.dot_general(
        summed[:, :kc], basis_ref[...], FIRST, precision=HIGH, preferred_element_type=jnp.float32
    )


def first_direction_kernel(shares_ref, extended_ref, inverse_ref, basis_ref, asked_ref, p_ref, out_ref):
    p = prolong(jnp.sum(shares_ref[...], axis=0), extended_ref, inverse_ref, basis_ref)
    p_ref[...] = p
    send_rows(p, asked_ref, out_ref)


def operate(near_ref, vector_ref, got_ref, own_ref, coupling_ref):
    slots = coupling_ref.shape[1] // LANES
    margin = margin_from(got_ref, near_ref, slots, vector_ref.shape[0])
    own = lax.dot_general(
        halves(vector_ref[...]), own_ref[...], LAST, preferred_element_type=jnp.float32
    )
    return joined(own) + lax.dot_general(margin, coupling_ref[...], LAST, preferred_element_type=jnp.float32)


def extend(vector, margin):
    return jnp.concatenate([halves(vector), jnp.concatenate([margin, jnp.zeros_like(margin)])], axis=1)


def row_sum(x):
    return jnp.sum(x, axis=1, keepdims=True)


def first_operate_kernel(
    near_ref, p_ref, got_ref, own_ref, coupling_ref, r_ref, basis_ref, asked_ref, q_ref, out_ref
):
    cols = r_ref.shape[0]
    kc = basis_ref.shape[0]
    q = operate(near_ref, p_ref, got_ref, own_ref, coupling_ref)
    q_ref[...] = q
    r = r_ref[:, 0, :]
    residual = lax.dot_general(
        q, basis_ref[...], LAST, precision=HIGH, preferred_element_type=jnp.float32
    )
    tail = jnp.concatenate([residual, jnp.zeros((cols, LANES - kc), jnp.float32)], axis=1)
    lane = lanes_of((cols, LANES))
    for i, inner in enumerate([row_sum(r * r), row_sum(q * r), row_sum(q * q)]):
        for k, term in enumerate(split3(inner)):
            tail = jnp.where(lane == kc + 3 * k + i, term, tail)
    send_rows(q, asked_ref, out_ref)
    half = cols // 2
    tail = tail[:half] + pltpu.roll(tail[half:], LANES // 2, 1)
    out_ref[:, :, 2 * LANES : 3 * LANES] = jnp.broadcast_to(
        tail.astype(jnp.bfloat16)[None], (out_ref.shape[0], half, LANES)
    )


def second_direction_kernel(
    all_rows, shares_ref, extended_ref, inverse_ref, basis_ref, asked_ref, r_ref, q_ref, p_ref,
    v1_ref, v2_ref, z1_ref, z2_ref, scalars_ref, out_ref,
):
    kc = basis_ref.shape[0]
    summed = jnp.sum(shares_ref[...], axis=0)
    p2 = prolong(summed, extended_ref, inverse_ref, basis_ref)
    rr, qr, qq = [summed[:, kc + i : kc + i + 1] / all_rows for i in range(3)]
    start = jnp.sqrt(rr + EPS)
    h11 = qr / start / start
    part = h11 / start
    left = qq / start / start - 2.0 * part * (qr / start) + part * part * rr
    h21 = jnp.sqrt(jnp.maximum(left, 0.0) + EPS)
    v1 = r_ref[:, 0, :] / start
    z1 = p_ref[...] / start
    v2 = (q_ref[...] / start - h11 * v1) / h21
    z2 = (p2 / start - h11 * z1) / h21
    v1_ref[...] = v1
    v2_ref[...] = v2
    z1_ref[...] = z1
    z2_ref[...] = z2
    lane = lanes_of(scalars_ref.shape)
    scalars_ref[...] = place(start, lane, 0) + place(h11, lane, 1) + place(h21, lane, 2)
    send_rows(z2, asked_ref, out_ref)


def second_operate_kernel(
    near_ref, z_ref, got_ref, own_ref, coupling_ref, v1_ref, v2_ref, w_ref, out_ref
):
    w = operate(near_ref, z_ref, got_ref, own_ref, coupling_ref)
    w_ref[...] = w
    v1 = v1_ref[...]
    v2 = v2_ref[...]
    cols = w.shape[0]
    lane = lanes_of((cols, LANES))
    col = lax.broadcasted_iota(jnp.int32, (cols, LANES), 0)
    pairs = [(w, v1), (w, v2), (w, w), (v1, v1), (v1, v2), (v2, v2)]
    inner = jnp.zeros((cols, LANES), jnp.float32)
    for i, (a, b) in enumerate(pairs):
        inner = jnp.where(lane == i * cols + col, row_sum(a * b), inner)
    out_ref[...] = jnp.broadcast_to(jnp.sum(inner, axis=0, keepdims=True)[None], out_ref.shape)


def between_kernel(got_ref, out_ref):
    out_ref[...] = jnp.broadcast_to(jnp.sum(got_ref[...], axis=0)[None], out_ref.shape)


def last_kernel(
    all_rows, got_ref, w_ref, v1_ref, v2_ref, z1_ref, z2_ref, scalars_ref, answer_ref, next_ref
):
    cols = w_ref.shape[0]
    lane = lanes_of((cols, LANES))
    col = lax.broadcasted_iota(jnp.int32, (cols, LANES), 0)
    inner = jnp.sum(got_ref[...], axis=0, keepdims=True) / all_rows
    inner = jnp.broadcast_to(inner, (cols, LANES))
    h12, h22, ww, g11, g12, g22 = [
        row_sum(jnp.where(lane == i * cols + col, inner, 0.0)) for i in range(6)
    ]
    start, h11, h21 = [scalars_ref[:, i : i + 1] for i in range(3)]
    left = (
        ww
        - 2.0 * (h12 * h12 + h22 * h22)
        + h12 * h12 * g11
        + 2.0 * h12 * h22 * g12
        + h22 * h22 * g22
    )
    h32 = jnp.sqrt(jnp.maximum(left, 0.0) + EPS)
    next_ref[:, 0, :] = (w_ref[...] - h12 * v1_ref[...] - h22 * v2_ref[...]) / h32
    weights = least_squares(start, [[h11, h21], [h12, h22, h32]])
    answer_ref[:, 0, :] = weights[0] * z1_ref[...] + weights[1] * z2_ref[...]


def call(kernel, outs, *args, name):
    vmem = pl.BlockSpec(memory_space=pltpu.VMEM)
    return pl.pallas_call(
        kernel,
        out_shape=outs,
        in_specs=[vmem] * len(args),
        out_specs=jax.tree.map(lambda _: vmem, outs),
        compiler_params=pltpu.CompilerParams(vmem_limit_bytes=VMEM_BYTES),
        name=name,
    )(*args)


def body(
    right_side,
    own_block,
    coupling,
    local_inverse,
    coarse_basis,
    coarse_inverse,
    neighbours,
    margin_rows,
    block_counts,
):
    cols, rows = right_side.shape[0], right_side.shape[3]
    r = right_side.reshape(cols, 1, rows)
    own = own_block[0, 0]
    couple = coupling[0, 0]
    inverse = local_inverse[0, 0]
    basis = coarse_basis[0, 0]
    coarse = coarse_inverse[0, :, 0, :]
    near = neighbours[0]
    picked = margin_rows.reshape(margin_rows.shape[2], 1, margin_rows.shape[3])
    live = block_counts
    subs, owners = lax.axis_size("sub"), lax.axis_size("crs")
    all_rows = rows * subs * owners
    f32, bf16 = jnp.float32, jnp.bfloat16

    def shape(*dims, dtype=f32):
        return jax.ShapeDtypeStruct(dims, dtype)

    vector = shape(cols, rows)
    tile = shape(cols, LANES)

    def over_sub(blocks):
        return lax.all_to_all(blocks, "sub", 0, 0, axis_index_groups=[order_of(subs)])

    def over_crs(blocks):
        return lax.all_to_all(blocks, "crs", 0, 0)

    held = [r, basis, picked]
    vmem = pl.BlockSpec(memory_space=pltpu.VMEM)
    sent, near, r, basis, picked = pl.pallas_call(
        first_send_kernel,
        out_shape=[shape(subs, cols, rows + LANES, dtype=bf16), shape(1, LANES, dtype=jnp.int32)]
        + [shape(*x.shape, dtype=x.dtype) for x in held],
        in_specs=[pl.BlockSpec(memory_space=pltpu.SMEM)]
        + [pl.BlockSpec(memory_space=pl.ANY)] * 4,
        out_specs=[vmem] * 5,
        scratch_shapes=[pltpu.VMEM(near.shape, jnp.int32), pltpu.SemaphoreType.DMA((8,))],
        compiler_params=pltpu.CompilerParams(vmem_limit_bytes=VMEM_BYTES),
        cost_estimate=pl.CostEstimate(
            flops=1 << 34, bytes_accessed=1 << 30, transcendentals=0
        ),
        name="first_send",
    )(live, *[pltpu.with_memory_space_constraint(x, pltpu.HBM) for x in (near, *held)])
    got = over_sub(sent)
    extended, asked, shares = call(
        first_gather_kernel,
        (
            shape(2 * cols, inverse.shape[1], dtype=bf16),
            shape(subs // 2, 2 * cols, LANES, dtype=jnp.int32),
            shape(owners, cols, LANES),
        ),
        near, r, picked, got, coarse, name="first_gather",
    )
    shares = over_crs(shares)
    p1, sent = call(
        first_direction_kernel, (vector, shape(subs, cols, LANES, dtype=bf16)),
        shares, extended, inverse, basis, asked, name="first_direction",
    )
    got = over_sub(sent)
    q1, sent = call(
        first_operate_kernel, (vector, shape(subs, cols // 2, 3 * LANES, dtype=bf16)),
        near, p1, got, own, couple, r, basis, asked, name="first_operate",
    )
    got = over_sub(sent)
    extended, shares = call(
        second_gather_kernel,
        (shape(2 * cols, inverse.shape[1], dtype=bf16), shape(owners, cols, LANES)),
        near, q1, got, coarse, name="second_gather",
    )
    shares = over_crs(shares)

    def second_direction(*refs):
        second_direction_kernel(float(all_rows), *refs)

    v1, v2, z1, z2, scalars, sent = call(
        second_direction,
        (vector, vector, vector, vector, tile, shape(subs, cols, LANES, dtype=bf16)),
        shares, extended, inverse, basis, asked, r, q1, p1, name="second_direction",
    )
    got = over_sub(sent)
    w, sent = call(
        second_operate_kernel, (vector, shape(owners, 1, LANES)),
        near, z2, got, own, couple, v1, v2, name="second_operate",
    )
    got = over_crs(sent)
    sent = call(between_kernel, shape(subs, 1, LANES), got, name="between")
    got = over_sub(sent).reshape(subs, LANES)

    def last(*refs):
        last_kernel(float(all_rows), *refs)

    answer, following = call(
        last, (shape(cols, 1, rows), shape(cols, 1, rows)),
        got, w, v1, v2, z1, z2, scalars, name="last",
    )
    out = (cols, 1, 1, rows)
    return answer.reshape(out), following.reshape(out)


def solution(mesh):
    in_specs = (
        P(None, "sub", "crs", None),
        P("sub", "crs", None, None),
        P("sub", "crs", None, None),
        P("sub", "crs", None, None),
        P("sub", "crs", None, None),
        P("sub", None, "crs", None),
        P("sub", "crs", None),
        P("sub", "crs", None, None),
        P("sub", "crs"),
    )
    out_specs = (P(None, "sub", "crs", None), P(None, "sub", "crs", None))
    return jax.shard_map(body, mesh=mesh, in_specs=in_specs, out_specs=out_specs, check_vma=False)
```

```python
import jax
import jax.numpy as jnp
from jax import lax
from jax.experimental import pallas as pl
from jax.experimental.pallas import tpu as pltpu
from jax.sharding import PartitionSpec as P

EPS = 1e-06
HIGH = lax.Precision.HIGH
LAST = (((1,), (1,)), ((), ()))
FIRST = (((1,), (0,)), ((), ()))
LANES = 128
VMEM_BYTES = 16 << 20
PLANES = 16
NEAR = 4
def turned(plane):
    return ((plane & 1) << 2) | (plane & 2) | ((plane >> 2) & 1)


def order_of(subs):
    planes = [turned(i // (2 * NEAR)) + i % 2 * (PLANES // 2) for i in range(subs)]
    return [plane * NEAR + i // 2 % NEAR for i, plane in enumerate(planes)]


def place_of(sub):
    plane = sub >> 2
    return turned(plane & 7) * (2 * NEAR) + (sub & (NEAR - 1)) * 2 + (plane >> 3)


def least_squares(start_norm, columns):
    cosines = []
    sine_terms = []
    triangle = []
    target = [start_norm] + [jnp.zeros_like(start_norm) for j in range(len(columns))]
    for j, column in enumerate(columns):
        column = list(column)
        for i in range(j):
            upper_value = cosines[i] * column[i] + sine_terms[i] * column[i + 1]
            column[i + 1] = -sine_terms[i] * column[i] + cosines[i] * column[i + 1]
            column[i] = upper_value
        radius = jnp.sqrt(column[j] * column[j] + column[j + 1] * column[j + 1])
        cosine = column[j] / radius
        sine_part = column[j + 1] / radius
        column[j] = radius
        target[j + 1] = -sine_part * target[j]
        target[j] = cosine * target[j]
        cosines.append(cosine)
        sine_terms.append(sine_part)
        triangle.append(column[: j + 1])
    weights = [None] * len(columns)
    for j in reversed(range(len(columns))):
        running = target[j]
        for k in range(j + 1, len(columns)):
            running = running - triangle[k][j] * weights[k]
        weights[j] = running / triangle[j][j]
    return weights


def split3(x):
    hi = x.astype(jnp.bfloat16).astype(jnp.float32)
    rest = x - hi
    mid = rest.astype(jnp.bfloat16).astype(jnp.float32)
    return hi, mid, rest - mid


def halves(x):
    hi = x.astype(jnp.bfloat16)
    return jnp.concatenate([hi, (x - hi.astype(jnp.float32)).astype(jnp.bfloat16)], axis=0)


def joined(x):
    rows = x.shape[0] // 2
    return x[:rows] + x[rows:]


def place(column, lane, at):
    return jnp.where(lane == at, column, 0.0)


def pick_lanes(tiles, index):
    low = index & (LANES - 1)
    high = index >> 7
    out = jnp.take_along_axis(tiles[0], low, axis=1, mode="promise_in_bounds")
    for t in range(1, len(tiles)):
        other = jnp.take_along_axis(tiles[t], low, axis=1, mode="promise_in_bounds")
        out = jnp.where(high == t, other, out)
    return out


def lanes_of(shape):
    return lax.broadcasted_iota(jnp.int32, shape, 1)


def twice(x):
    return jnp.concatenate([x, x], axis=0)


def send_rows(vector, asked_ref, out_ref):
    tiles = [twice(vector[:, t * LANES : (t + 1) * LANES]) for t in range(vector.shape[1] // LANES)]
    cols = vector.shape[0]
    height = out_ref.shape[1]
    for i in range(asked_ref.shape[0]):
        chosen = pick_lanes(tiles, asked_ref[i])
        for at in range(0, 2 * cols, height):
            part, t = divmod(at, cols)
            lanes = pl.ds(t // height * LANES, LANES)
            out_ref[2 * i + part, :, lanes] = chosen[at : at + height].astype(jnp.bfloat16)


def margin_from(got_ref, near_ref, slots, cols):
    near = near_ref[...]
    parts = []
    for j in range(slots):
        source = near[0, j]
        part = got_ref[jnp.maximum(source, 0)]
        parts.append(jnp.where(source >= 0, part, jnp.zeros_like(part)).astype(jnp.float32))
    width = cols // got_ref.shape[1]
    columns = [
        jnp.concatenate([part[:, t * LANES : (t + 1) * LANES] for part in parts], axis=1)
        for t in range(width)
    ]
    return jnp.concatenate(columns, axis=0).astype(jnp.bfloat16)


def first_send_kernel(
    live, near_hbm, r_hbm, basis_hbm, picked_hbm,
    out_ref, table_ref, r_ref, basis_ref, picked, near_ref, sems,
):
    pairs = [
        (r_hbm, r_ref),
        (basis_hbm, basis_ref),
        (picked_hbm, picked),
        (near_hbm, near_ref),
    ]
    moves = [
        pltpu.make_async_copy(source, target, sems.at[i])
        for i, (source, target) in enumerate(pairs)
    ]
    for move in moves:
        move.start()
    for move in moves[:4]:
        move.wait()
    subs, cols, _ = out_ref.shape
    rows = r_ref.shape[2]
    kc = basis_ref.shape[0]
    r = r_ref[:, 0, :]
    low = r.astype(jnp.bfloat16)
    residual = lax.dot_general(
        r, basis_ref[...], LAST, precision=HIGH, preferred_element_type=jnp.float32
    )
    tail = jnp.concatenate([residual, jnp.zeros((cols, LANES - kc), jnp.float32)], axis=1)
    whole = jnp.concatenate([low, tail.astype(jnp.bfloat16)], axis=1)
    out_ref[...] = jnp.broadcast_to(whole[None], out_ref.shape)
    lane = lanes_of((cols, LANES))
    sub = lax.broadcasted_iota(jnp.int32, (cols, LANES), 0)
    wide = LANES // cols
    slots = picked.shape[0]
    near = place_of(near_ref[...])
    table = jnp.concatenate([near, jnp.zeros((1, LANES - slots), jnp.int32)], axis=1)
    table_ref[...] = jnp.where(lanes_of((1, LANES)) < live[0, 0], table, -1)
    for j in reversed(range(slots)):
        wanted = (picked[j] - rows // 2).astype(jnp.float32)
        wanted = jnp.broadcast_to(wanted, (cols, LANES))
        packed = jnp.zeros((cols, LANES), jnp.float32)
        for i in range(cols):
            moved = pltpu.roll(wanted, (kc - i * wide) % LANES, 1)
            packed = jnp.where(sub == i, moved, packed)
        packed = jnp.where((lane >= kc) & (lane < kc + wide), packed, tail)
        out_ref[near[0, j], :, rows : rows + LANES] = packed.astype(jnp.bfloat16)
    for move in moves[4:]:
        move.wait()


def write_share(at, with_terms, got_ref, coarse_ref, out_ref):
    subs, height, _ = got_ref.shape
    owners, cols, _ = out_ref.shape
    kc = coarse_ref.shape[0] // owners
    lane = lanes_of((height, LANES))
    width = cols // height
    zero = jnp.zeros((height, LANES), jnp.float32)
    tiles = [[zero] * (subs * kc // LANES) for _ in range(width)]
    terms = zero
    for block, s in enumerate(order_of(subs)):
        got = got_ref[block, :, at : at + LANES].astype(jnp.float32)
        if with_terms:
            terms = terms + got
        t, off = divmod(s * kc, LANES)
        for part in range(width):
            mine = tiles[part]
            turn = (off - part * (LANES // width)) % LANES
            moved = pltpu.roll(got, turn, 1) if turn else got
            if off + kc <= LANES:
                mine[t] = jnp.where((lane >= off) & (lane < off + kc), moved, mine[t])
            else:
                mine[t] = jnp.where(lane >= off, moved, mine[t])
                mine[t + 1] = jnp.where(lane < off + kc - LANES, moved, mine[t + 1])
    residuals = [jnp.concatenate(mine, axis=1) for mine in tiles]
    residuals = jnp.concatenate(residuals, axis=0).astype(jnp.bfloat16)
    if width > 1:
        terms = jnp.concatenate([terms, pltpu.roll(terms, LANES // width, 1)], axis=0)
    lane = lanes_of((cols, LANES))
    share = lax.dot_general(
        residuals, coarse_ref[...], LAST, preferred_element_type=jnp.float32
    )
    extra = jnp.zeros((cols, LANES), jnp.float32)
    if with_terms:
        summed = terms + pltpu.roll(terms, LANES - 3, 1) + pltpu.roll(terms, LANES - 6, 1)
        extra = jnp.where((lane >= kc) & (lane < kc + 3), summed, 0.0)
    wide = jnp.concatenate(
        [share, jnp.zeros((cols, -share.shape[1] % LANES), jnp.float32)], axis=1
    )
    for c in range(owners):
        t, off = divmod(c * kc, LANES)
        part = wide[:, t * LANES : (t + 1) * LANES]
        if off:
            part = pltpu.roll(part, LANES - off, 1)
        if off + kc > LANES:
            after = pltpu.roll(wide[:, (t + 1) * LANES : (t + 2) * LANES], LANES - off, 1)
            part = jnp.where(lane < LANES - off, part, after)
        out_ref[c] = jnp.where(lane < kc, part, extra)


def first_gather_kernel(
    near_ref, r_ref, picked_ref, got_ref, coarse_ref, extended_ref, asked_ref, out_ref
):
    subs, cols, _ = got_ref.shape
    rows = r_ref.shape[2]
    slots = picked_ref.shape[0]
    write_share(rows, False, got_ref, coarse_ref, out_ref)
    near = near_ref[...]
    parts = []
    for j in range(slots):
        source = near[0, j]
        other = got_ref[jnp.maximum(source, 0), :, 0:rows].astype(jnp.float32)
        tiles = [twice(other[:, t * LANES : (t + 1) * LANES]) for t in range(rows // LANES)]
        index = jnp.broadcast_to(picked_ref[j], (2 * cols, LANES))
        part = pick_lanes(tiles, index)[:cols]
        parts.append(jnp.where(source >= 0, part, 0.0).astype(jnp.bfloat16))
    margin = jnp.concatenate(parts, axis=1)
    extended_ref[...] = extend(r_ref[:, 0, :], margin)
    lane = lanes_of((cols, LANES))
    kc = coarse_ref.shape[0] // out_ref.shape[0]
    wide = LANES // cols
    for i in range(subs // 2):
        pair = []
        for s in (2 * i, 2 * i + 1):
            got = got_ref[s, :, rows : rows + LANES].astype(jnp.float32)
            index = jnp.zeros((cols, LANES), jnp.float32)
            for k in range(cols):
                moved = pltpu.roll(
                    jnp.broadcast_to(got[k : k + 1], (cols, LANES)), (k * wide - kc) % LANES, 1
                )
                index = jnp.where((lane >= k * wide) & (lane < (k + 1) * wide), moved, index)
            pair.append(index)
        index = jnp.concatenate(pair, axis=0).astype(jnp.int32) + rows // 2
        asked_ref[i] = jnp.clip(index, 0, rows - 1)


def second_gather_kernel(
    near_ref, vector_ref, got_ref, coarse_ref, extended_ref, out_ref
):
    rows = vector_ref.shape[1]
    slots = (extended_ref.shape[1] - rows) // LANES
    write_share(2 * LANES, True, got_ref, coarse_ref, out_ref)
    margin = margin_from(got_ref, near_ref, slots, vector_ref.shape[0])
    extended_ref[...] = extend(vector_ref[...], margin)


def prolong(summed, extended_ref, inverse_ref, basis_ref):
    kc = basis_ref.shape[0]
    fine = lax.dot_general(
        extended_ref[...], inverse_ref[...], LAST, preferred_element_type=jnp.float32
    )
    return joined(fine) + lax.dot_general(
        summed[:, :kc], basis_ref[...], FIRST, precision=HIGH, preferred_element_type=jnp.float32
    )


def first_direction_kernel(shares_ref, extended_ref, inverse_ref, basis_ref, asked_ref, p_ref, out_ref):
    p = prolong(jnp.sum(shares_ref[...], axis=0), extended_ref, inverse_ref, basis_ref)
    p_ref[...] = p
    send_rows(p, asked_ref, out_ref)


def operate(near_ref, vector_ref, got_ref, own_ref, coupling_ref):
    slots = coupling_ref.shape[1] // LANES
    margin = margin_from(got_ref, near_ref, slots, vector_ref.shape[0])
    own = lax.dot_general(
        halves(vector_ref[...]), own_ref[...], LAST, preferred_element_type=jnp.float32
    )
    return joined(own) + lax.dot_general(margin, coupling_ref[...], LAST, preferred_element_type=jnp.float32)


def extend(vector, margin):
    return jnp.concatenate([halves(vector), jnp.concatenate([margin, jnp.zeros_like(margin)])], axis=1)


def row_sum(x):
    return jnp.sum(x, axis=1, keepdims=True)


def first_operate_kernel(
    near_ref, p_ref, got_ref, own_ref, coupling_ref, r_ref, basis_ref, asked_ref, q_ref, out_ref
):
    cols = r_ref.shape[0]
    kc = basis_ref.shape[0]
    q = operate(near_ref, p_ref, got_ref, own_ref, coupling_ref)
    q_ref[...] = q
    r = r_ref[:, 0, :]
    residual = lax.dot_general(
        q, basis_ref[...], LAST, precision=HIGH, preferred_element_type=jnp.float32
    )
    tail = jnp.concatenate([residual, jnp.zeros((cols, LANES - kc), jnp.float32)], axis=1)
    lane = lanes_of((cols, LANES))
    for i, inner in enumerate([row_sum(r * r), row_sum(q * r), row_sum(q * q)]):
        for k, term in enumerate(split3(inner)):
            tail = jnp.where(lane == kc + 3 * k + i, term, tail)
    send_rows(q, asked_ref, out_ref)
    half = cols // 2
    tail = tail[:half] + pltpu.roll(tail[half:], LANES // 2, 1)
    out_ref[:, :, 2 * LANES : 3 * LANES] = jnp.broadcast_to(
        tail.astype(jnp.bfloat16)[None], (out_ref.shape[0], half, LANES)
    )


def second_direction_kernel(
    all_rows, shares_ref, extended_ref, inverse_ref, basis_ref, asked_ref, r_ref, q_ref, p_ref,
    v1_ref, v2_ref, z1_ref, z2_ref, scalars_ref, out_ref,
):
    kc = basis_ref.shape[0]
    summed = jnp.sum(shares_ref[...], axis=0)
    p2 = prolong(summed, extended_ref, inverse_ref, basis_ref)
    rr, qr, qq = [summed[:, kc + i : kc + i + 1] / all_rows for i in range(3)]
    start = jnp.sqrt(rr + EPS)
    h11 = qr / start / start
    part = h11 / start
    left = qq / start / start - 2.0 * part * (qr / start) + part * part * rr
    h21 = jnp.sqrt(jnp.maximum(left, 0.0) + EPS)
    v1 = r_ref[:, 0, :] / start
    z1 = p_ref[...] / start
    v2 = (q_ref[...] / start - h11 * v1) / h21
    z2 = (p2 / start - h11 * z1) / h21
    v1_ref[...] = v1
    v2_ref[...] = v2
    z1_ref[...] = z1
    z2_ref[...] = z2
    lane = lanes_of(scalars_ref.shape)
    scalars_ref[...] = place(start, lane, 0) + place(h11, lane, 1) + place(h21, lane, 2)
    send_rows(z2, asked_ref, out_ref)


def second_operate_kernel(
    near_ref, z_ref, got_ref, own_ref, coupling_ref, v1_ref, v2_ref, w_ref, out_ref
):
    w = operate(near_ref, z_ref, got_ref, own_ref, coupling_ref)
    w_ref[...] = w
    v1 = v1_ref[...]
    v2 = v2_ref[...]
    cols = w.shape[0]
    lane = lanes_of((cols, LANES))
    col = lax.broadcasted_iota(jnp.int32, (cols, LANES), 0)
    pairs = [(w, v1), (w, v2), (w, w), (v1, v1), (v1, v2), (v2, v2)]
    inner = jnp.zeros((cols, LANES), jnp.float32)
    for i, (a, b) in enumerate(pairs):
        inner = jnp.where(lane == i * cols + col, row_sum(a * b), inner)
    out_ref[...] = jnp.broadcast_to(jnp.sum(inner, axis=0, keepdims=True)[None], out_ref.shape)


def between_kernel(got_ref, out_ref):
    out_ref[...] = jnp.broadcast_to(jnp.sum(got_ref[...], axis=0)[None], out_ref.shape)


def last_kernel(
    all_rows, got_ref, w_ref, v1_ref, v2_ref, z1_ref, z2_ref, scalars_ref, answer_ref, next_ref
):
    cols = w_ref.shape[0]
    lane = lanes_of((cols, LANES))
    col = lax.broadcasted_iota(jnp.int32, (cols, LANES), 0)
    inner = jnp.sum(got_ref[...], axis=0, keepdims=True) / all_rows
    inner = jnp.broadcast_to(inner, (cols, LANES))
    h12, h22, ww, g11, g12, g22 = [
        row_sum(jnp.where(lane == i * cols + col, inner, 0.0)) for i in range(6)
    ]
    start, h11, h21 = [scalars_ref[:, i : i + 1] for i in range(3)]
    left = (
        ww
        - 2.0 * (h12 * h12 + h22 * h22)
        + h12 * h12 * g11
        + 2.0 * h12 * h22 * g12
        + h22 * h22 * g22
    )
    h32 = jnp.sqrt(jnp.maximum(left, 0.0) + EPS)
    next_ref[:, 0, :] = (w_ref[...] - h12 * v1_ref[...] - h22 * v2_ref[...]) / h32
    weights = least_squares(start, [[h11, h21], [h12, h22, h32]])
    answer_ref[:, 0, :] = weights[0] * z1_ref[...] + weights[1] * z2_ref[...]


def call(kernel, outs, *args, name):
    vmem = pl.BlockSpec(memory_space=pltpu.VMEM)
    return pl.pallas_call(
        kernel,
        out_shape=outs,
        in_specs=[vmem] * len(args),
        out_specs=jax.tree.map(lambda _: vmem, outs),
        compiler_params=pltpu.CompilerParams(vmem_limit_bytes=VMEM_BYTES),
        name=name,
    )(*args)


def body(
    right_side,
    own_block,
    coupling,
    local_inverse,
    coarse_basis,
    coarse_inverse,
    neighbours,
    margin_rows,
    block_counts,
):
    cols, rows = right_side.shape[0], right_side.shape[3]
    r = right_side.reshape(cols, 1, rows)
    own = own_block[0, 0]
    couple = coupling[0, 0]
    inverse = local_inverse[0, 0]
    basis = coarse_basis[0, 0]
    coarse = coarse_inverse[0, :, 0, :]
    near = neighbours[0]
    picked = margin_rows.reshape(margin_rows.shape[2], 1, margin_rows.shape[3])
    live = block_counts
    subs, owners = lax.axis_size("sub"), lax.axis_size("crs")
    all_rows = rows * subs * owners
    f32, bf16 = jnp.float32, jnp.bfloat16

    def shape(*dims, dtype=f32):
        return jax.ShapeDtypeStruct(dims, dtype)

    vector = shape(cols, rows)
    tile = shape(cols, LANES)

    def over_sub(blocks):
        return lax.all_to_all(blocks, "sub", 0, 0, axis_index_groups=[order_of(subs)])

    def over_crs(blocks):
        return lax.all_to_all(blocks, "crs", 0, 0)

    held = [r, basis, picked]
    vmem = pl.BlockSpec(memory_space=pltpu.VMEM)
    sent, near, r, basis, picked = pl.pallas_call(
        first_send_kernel,
        out_shape=[shape(subs, cols, rows + LANES, dtype=bf16), shape(1, LANES, dtype=jnp.int32)]
        + [shape(*x.shape, dtype=x.dtype) for x in held],
        in_specs=[pl.BlockSpec(memory_space=pltpu.SMEM)]
        + [pl.BlockSpec(memory_space=pl.ANY)] * 4,
        out_specs=[vmem] * 5,
        scratch_shapes=[pltpu.VMEM(near.shape, jnp.int32), pltpu.SemaphoreType.DMA((8,))],
        compiler_params=pltpu.CompilerParams(vmem_limit_bytes=VMEM_BYTES),
        cost_estimate=pl.CostEstimate(
            flops=1 << 34, bytes_accessed=1 << 30, transcendentals=0
        ),
        name="first_send",
    )(live, *[pltpu.with_memory_space_constraint(x, pltpu.HBM) for x in (near, *held)])
    got = over_sub(sent)
    extended, asked, shares = call(
        first_gather_kernel,
        (
            shape(2 * cols, inverse.shape[1], dtype=bf16),
            shape(subs // 2, 2 * cols, LANES, dtype=jnp.int32),
            shape(owners, cols, LANES),
        ),
        near, r, picked, got, coarse, name="first_gather",
    )
    shares = over_crs(shares)
    p1, sent = call(
        first_direction_kernel, (vector, shape(subs, cols, LANES, dtype=bf16)),
        shares, extended, inverse, basis, asked, name="first_direction",
    )
    got = over_sub(sent)
    q1, sent = call(
        first_operate_kernel, (vector, shape(subs, cols // 2, 3 * LANES, dtype=bf16)),
        near, p1, got, own, couple, r, basis, asked, name="first_operate",
    )
    got = over_sub(sent)
    extended, shares = call(
        second_gather_kernel,
        (shape(2 * cols, inverse.shape[1], dtype=bf16), shape(owners, cols, LANES)),
        near, q1, got, coarse, name="second_gather",
    )
    shares = over_crs(shares)

    def second_direction(*refs):
        second_direction_kernel(float(all_rows), *refs)

    v1, v2, z1, z2, scalars, sent = call(
        second_direction,
        (vector, vector, vector, vector, tile, shape(subs, cols, LANES, dtype=bf16)),
        shares, extended, inverse, basis, asked, r, q1, p1, name="second_direction",
    )
    got = over_sub(sent)
    w, sent = call(
        second_operate_kernel, (vector, shape(owners, 1, LANES)),
        near, z2, got, own, couple, v1, v2, name="second_operate",
    )
    got = over_crs(sent)
    sent = call(between_kernel, shape(subs, 1, LANES), got, name="between")
    got = over_sub(sent).reshape(subs, LANES)

    def last(*refs):
        last_kernel(float(all_rows), *refs)

    answer, following = call(
        last, (shape(cols, 1, rows), shape(cols, 1, rows)),
        got, w, v1, v2, z1, z2, scalars, name="last",
    )
    out = (cols, 1, 1, rows)
    return answer.reshape(out), following.reshape(out)


def solution(mesh):
    in_specs = (
        P(None, "sub", "crs", None),
        P("sub", "crs", None, None),
        P("sub", "crs", None, None),
        P("sub", "crs", None, None),
        P("sub", "crs", None, None),
        P("sub", None, "crs", None),
        P("sub", "crs", None),
        P("sub", "crs", None, None),
        P("sub", "crs"),
    )
    out_specs = (P(None, "sub", "crs", None), P(None, "sub", "crs", None))
    return jax.shard_map(body, mesh=mesh, in_specs=in_specs, out_specs=out_specs, check_vma=False)
```
